32 devices in a mesh: ctxa: 4 (over y, x), ctxb: 8 (over z, core).
Axes of the slice: x: 2, y: 2, z: 4, core: 2. Of those that a mesh axis runs over, the one named last changes fastest.
Arguments:
- queries: bfloat16 [8192, 384], P(('ctxa', 'ctxb')), may hold values from -6 to 6
- key_matrix: bfloat16 [8192, 384], P(('ctxa', 'ctxb')), may hold values from -6 to 6
- value_matrix: bfloat16 [8192, 384], P(('ctxa', 'ctxb')), may hold values from -6 to 6
- grad_out: bfloat16 [8192, 384], P(('ctxa', 'ctxb')), may hold values from -6 to 6
- offsets: int32 [6], replicated, may hold values from 0 to 127
Outputs:
- grad_queries: bfloat16 [8192, 384], P(('ctxa', 'ctxb'))
- grad_keys: bfloat16 [8192, 384], P(('ctxa', 'ctxb'))
- grad_values: bfloat16 [8192, 384], P(('ctxa', 'ctxb'))
The draws below stay inside these ranges and needn't reach their ends.
All inputs are finite; a program needn't handle non-finite values.
Results may differ from the reference program's by a relative error of at most 0.0086.
Values may be sent and summed in bfloat16 or wider, within the bound.
No kernel may reach another device: no remote copies, remote signals or barrier semaphores. Data moves between devices by JAX's collectives and lax.ppermute only.
A program may use at most 128 MiB of HBM per device.

```python
import jax
import jax.numpy as jnp
from jax import lax

HEAD_TOTAL = 6
HD = 64
TOKENS_PER_UNIT = 256
MIDDLE_DILATION = 8
UPPER_DILATION = 128
BOTTOM_GROUP = 4
TOKENS = 8192
N_CTXB = 8


def drawn_pair(key):
    base_key = jax.random.fold_in(key, 7)
    key_query, key_other = jax.random.split(base_key, 2)
    full_shape = (TOKENS, HEAD_TOTAL * HD)
    query_draw = jnp.clip(1.5 * jax.random.normal(key_query, full_shape, jnp.float32), -6.0, 6.0)
    sample_key = jnp.clip(1.5 * jax.random.normal(key_other, full_shape, jnp.float32), -6.0, 6.0)
    return (query_draw, sample_key)


def draw_queries(key, part):
    return drawn_pair(key)[0].astype(jnp.bfloat16)


def draw_key_matrix(key, part):
    return drawn_pair(key)[1].astype(jnp.bfloat16)


def draw_offsets(key, part):
    primary_key, key_slot = jax.random.split(jax.random.fold_in(key, 3))
    sampled_rows = jax.random.randint(primary_key, (HEAD_TOTAL,), 0, UPPER_DILATION)
    upper_level_slot = jax.random.randint(key_slot, (), 0, HEAD_TOTAL)
    return jnp.where(jnp.arange(HEAD_TOTAL) == upper_level_slot, UPPER_DILATION - 1, sampled_rows).astype(jnp.int32)


def block_scale(rng, shape, shards, low, top_value):
    level, own = 1.0, jax.random.fold_in(rng, 6)
    for dim, parts in shards:
        steps = jnp.exp(jax.random.uniform(jax.random.fold_in(own, dim), (parts,), jnp.float32, low / len(shards), top_value / len(shards)))
        level = level * jnp.repeat(steps, shape[dim] // parts).reshape([-1 if axis == dim else 1 for axis in range(len(shape))])
    return level


def gaussian(own_key, extent, width, limit, shards=(), kind=jnp.bfloat16):
    array = jax.random.normal(own_key, extent, jnp.float32) * width
    if len(shards) > 0:
        array = block_scale(own_key, extent, shards, -0.22, 0.18) * array
    return jnp.clip(array, min=-limit, max=limit).astype(kind)


def setup_inputs(seed: int = 0) -> dict:
    key_list = jax.random.split(jax.random.key(seed), 6)
    return {
        "queries": draw_queries(jax.random.fold_in(key_list[5], 71), 0),
        "key_matrix": draw_key_matrix(jax.random.fold_in(key_list[5], 71), 0),
        "value_matrix": gaussian(key_list[2], (TOKENS, HEAD_TOTAL * HD), 1.0, 6.0, ((0, 32),)),
        "grad_out": gaussian(key_list[3], (TOKENS, HEAD_TOTAL * HD), 1.0, 6.0, ((0, 32),)),
        "offsets": draw_offsets(jax.random.fold_in(key_list[5], 71), 0),
    }


FILL_LOW = -1e30


def selection_mask(offsets, spacing_factor):
    return jnp.arange(spacing_factor, dtype=jnp.int32)[None, :] == (offsets % spacing_factor).astype(jnp.int32)[:, None]


def select_rows(source, level_mask):
    head_count, spacing_factor = level_mask.shape
    pieces = source.reshape(source.shape[0] // spacing_factor, spacing_factor, head_count, source.shape[1] // head_count)
    kept = jnp.where(level_mask.T[None, :, :, None], pieces, jnp.zeros((), source.dtype))
    return jnp.transpose(jnp.sum(kept, axis=1), (1, 0, 2))


def place_rows(rows, level_mask):
    head_count, spacing_factor = level_mask.shape
    spread = jnp.where(level_mask.T[None, :, :, None], jnp.transpose(rows, (1, 0, 2))[:, None, :, :], 0.0)
    return spread.reshape(rows.shape[1] * spacing_factor, head_count * rows.shape[2])


def spread_scalar(values, level_mask, filler):
    return jnp.where(level_mask[:, None, :], values[:, :, None], filler).reshape(values.shape[0], -1)


def collect_scalar(values, level_mask):
    head_count, spacing_factor = level_mask.shape
    shaped = values.reshape(head_count, -1, spacing_factor)
    return jnp.sum(jnp.where(level_mask[:, None, :], shaped, 0.0), axis=2)


def level_forward(query_matrix, key_matrix, value_matrix):
    logit_scale = HD ** -0.5
    attention_logits = jnp.einsum("sle,sie->sli", query_matrix.astype(jnp.float32), key_matrix.astype(jnp.float32)) * logit_scale
    row_max = jnp.max(attention_logits, axis=-1)
    weight_tensors = jnp.exp(attention_logits - row_max[..., None])
    row_sum = jnp.sum(weight_tensors, axis=-1)
    rounded_values = lax.optimization_barrier(weight_tensors.astype(jnp.bfloat16)).astype(jnp.float32)
    row_accumulator = jnp.einsum("fco,fox->fcx", rounded_values, value_matrix.astype(jnp.float32))
    return row_max, row_sum, row_accumulator


def level_backward(query_matrix, key_matrix, value_matrix, gradient_rows, log_sum, row_dot):
    logit_scale = HD ** -0.5
    attention_logits = jnp.einsum("sle,sie->sli", query_matrix.astype(jnp.float32), key_matrix.astype(jnp.float32)) * logit_scale
    probs = jnp.exp(attention_logits - log_sum[..., None])
    probability_gradient = jnp.einsum("sle,sie->sli", gradient_rows.astype(jnp.float32), value_matrix.astype(jnp.float32))
    score_gradient = probs * (probability_gradient - row_dot[..., None]) * logit_scale
    score_gradient = lax.optimization_barrier(score_gradient.astype(jnp.bfloat16)).astype(jnp.float32)
    rounded_probabilities = lax.optimization_barrier(probs.astype(jnp.bfloat16)).astype(jnp.float32)
    query_gradient = jnp.einsum("fco,fox->fcx", score_gradient, key_matrix.astype(jnp.float32))
    key_gradient = jnp.einsum("axm,axh->amh", score_gradient, query_matrix.astype(jnp.float32))
    value_gradient = jnp.einsum("axm,axh->amh", rounded_probabilities, gradient_rows.astype(jnp.float32))
    return query_gradient, key_gradient, value_gradient


def in_segments(kernel, arrays, seg_keys):
    head_count = arrays[0].shape[0]
    seg_count = arrays[0].shape[1] // seg_keys
    stacked = tuple(jnp.moveaxis(member.reshape((head_count, seg_count, seg_keys) + member.shape[2:]), 1, 0) for member in arrays)
    results = lax.map(lambda grouped: kernel(*grouped), stacked)
    return tuple(jnp.moveaxis(member, 0, 1).reshape((head_count, seg_count * seg_keys) + member.shape[3:]) for member in results)


def reference(queries, key_matrix, value_matrix, grad_out, offsets):
    count_of_tokens = queries.shape[0]
    head_count = offsets.shape[0]
    level_layout = ((1, TOKENS_PER_UNIT * BOTTOM_GROUP), (MIDDLE_DILATION, TOKENS_PER_UNIT * N_CTXB // MIDDLE_DILATION), (UPPER_DILATION, count_of_tokens // UPPER_DILATION))
    mask_per_level = [selection_mask(offsets, spacing_factor) for spacing_factor, seg_keys in level_layout]
    query_sets = [select_rows(queries, level_mask) for level_mask in mask_per_level]
    key_sets = [select_rows(key_matrix, level_mask) for level_mask in mask_per_level]
    value_sets = [select_rows(value_matrix, level_mask) for level_mask in mask_per_level]
    grad_sets = [select_rows(grad_out, level_mask) for level_mask in mask_per_level]
    stats = [in_segments(level_forward, (query_sets[level_idx], key_sets[level_idx], value_sets[level_idx]), level_layout[level_idx][1]) for level_idx in range(3)]
    spread_levels = jnp.stack([spread_scalar(stats[level_idx][0] + jnp.log(stats[level_idx][1]), mask_per_level[level_idx], FILL_LOW) for level_idx in range(3)])
    lse_max = jnp.max(spread_levels, axis=0)
    log_sum = lse_max + jnp.log(jnp.sum(jnp.exp(spread_levels - lse_max), axis=0))
    level_sums = [collect_scalar(log_sum, level_mask) for level_mask in mask_per_level]
    attended = jnp.zeros((count_of_tokens, queries.shape[1]), jnp.float32)
    for level_idx in range(3):
        row_max, row_sum, row_accumulator = stats[level_idx]
        attended = attended + place_rows(row_accumulator * jnp.exp(row_max - level_sums[level_idx])[..., None], mask_per_level[level_idx])
    row_dots = jnp.sum(grad_out.astype(jnp.float32).reshape(count_of_tokens, head_count, -1) * attended.reshape(count_of_tokens, head_count, -1), axis=-1).T
    dot_sets = [collect_scalar(row_dots, level_mask) for level_mask in mask_per_level]
    grad_q = jnp.zeros((count_of_tokens, queries.shape[1]), jnp.float32)
    grad_k = jnp.zeros((count_of_tokens, queries.shape[1]), jnp.float32)
    grad_v = jnp.zeros((count_of_tokens, queries.shape[1]), jnp.float32)
    for level_idx in range(3):
        level_q, level_k, level_v = in_segments(level_backward, (query_sets[level_idx], key_sets[level_idx], value_sets[level_idx], grad_sets[level_idx], level_sums[level_idx], dot_sets[level_idx]), level_layout[level_idx][1])
        grad_q = grad_q + place_rows(level_q, mask_per_level[level_idx])
        grad_k = grad_k + place_rows(level_k, mask_per_level[level_idx])
        grad_v = grad_v + place_rows(level_v, mask_per_level[level_idx])
    return grad_q.astype(jnp.bfloat16), grad_k.astype(jnp.bfloat16), grad_v.astype(jnp.bfloat16)
```

```python
from functools import partial

import jax
import jax.numpy as jnp
from jax import lax
from jax.experimental import pallas as pl
from jax.experimental.pallas import tpu as pltpu
from jax.sharding import PartitionSpec as P

HD = 64
PAIR = 2 * HD
GROUP = 4
MIDDLE = 8
UPPER = 128
LOW = -1e30
HIGH = 1e30
SCALE = HD**-0.5
F32 = jnp.float32
BF16 = jnp.bfloat16
STAT_ROWS = 16


def iota(shape, dim):
    return lax.broadcasted_iota(jnp.int32, shape, dim)


def dot_nt(a, b):
    return lax.dot_general(a, b, (((1,), (1,)), ((), ())), preferred_element_type=F32)


def dot_nn(a, b):
    return jnp.dot(a, b, preferred_element_type=F32)


def pair_slice(head):
    low = head // 2 * PAIR
    return slice(low, low + PAIR)


def half_mask(head):
    return iota((1, PAIR), 1) // HD == head % 2


def one_head(block, head, scale=1.0):
    return jnp.where(half_mask(head), block.astype(F32) * scale, 0.0).astype(BF16)


def lane_offsets(off_ref, heads, width):
    lane_head = iota((1, width), 1) // HD
    out = jnp.zeros((1, width), jnp.int32)
    for head in range(heads):
        out = jnp.where(lane_head == head, off_ref[head], out)
    return out


def row_offsets(off_ref, heads):
    rows = iota((STAT_ROWS, 1), 0)
    out = jnp.zeros((STAT_ROWS, 1), jnp.int32)
    for head in range(heads):
        out = jnp.where((rows == head) | (rows == head + heads), off_ref[head], out)
    return out


def pair_weights(rows, middle_offset):
    both = (iota((rows, rows), 0) % MIDDLE == middle_offset) & (
        iota((rows, rows), 1) % MIDDLE == middle_offset
    )
    return jnp.where(both, 2.0, 1.0)


def pack_kernel(off_ref, q_ref, k_ref, v_ref, g_ref, near_ref, spec_ref):
    rows, width = q_ref.shape
    heads = width // HD
    near_rows, spec_rows = rows // MIDDLE, rows // UPPER
    offsets = lane_offsets(off_ref, heads, width)
    token = iota((rows, width), 0)
    middle = token % MIDDLE == offsets % MIDDLE
    upper = token % UPPER == offsets
    for near_slot, spec_slot, ref in ((0, 1, k_ref), (1, 2, v_ref), (2, 0, q_ref), (3, 3, g_ref)):
        whole = ref[...].astype(F32)
        kept = jnp.where(middle, whole, 0.0).reshape(near_rows, MIDDLE, width).sum(axis=1)
        near_ref[near_slot * near_rows : (near_slot + 1) * near_rows, :] = kept.astype(BF16)
        top = jnp.where(upper, whole, 0.0).reshape(spec_rows, UPPER, width).sum(axis=1)
        spec_ref[spec_slot * spec_rows : (spec_slot + 1) * spec_rows, :] = top


def near_part(near_refs, slot, lanes):
    rows = near_refs[0].shape[0] // 4
    return jnp.concatenate([r[slot * rows : (slot + 1) * rows, lanes] for r in near_refs], axis=0)


def forward_kernel(near_count, off_ref, q_ref, g_ref, spec_ref, *refs):
    k_refs, v_refs = refs[:GROUP], refs[GROUP : 2 * GROUP]
    near_refs = refs[2 * GROUP : 2 * GROUP + near_count]
    out_ref = refs[-1]
    rows, width = q_ref.shape
    heads = width // HD
    log_sums, dots = [], []
    for head in range(heads):
        lanes = pair_slice(head)
        middle_offset = off_ref[head] % MIDDLE
        chosen = iota((1, rows), 1) % MIDDLE == middle_offset
        weight = pair_weights(rows, middle_offset)
        query = one_head(q_ref[:, lanes], head, SCALE)
        grad = one_head(g_ref[:, lanes], head)
        scores = [dot_nt(r[:, lanes], query) for r in k_refs]
        top = jnp.max(scores[0], axis=0, keepdims=True)
        for part in scores[1:]:
            top = jnp.maximum(top, jnp.max(part, axis=0, keepdims=True))
        if near_count:
            far_scores = dot_nt(near_part(near_refs, 0, lanes), query)
            far_scores = jnp.where(chosen, far_scores, LOW)
            top = jnp.maximum(top, jnp.max(far_scores, axis=0, keepdims=True))
        total = jnp.zeros((1, rows), F32)
        product = jnp.zeros((1, rows), F32)
        for part, v_ref in zip(scores, v_refs):
            weights = jnp.exp(part - top) * weight
            total = total + jnp.sum(weights, axis=0, keepdims=True)
            inner = dot_nt(v_ref[:, lanes], grad)
            product = product + jnp.sum(weights * inner, axis=0, keepdims=True)
        if near_count:
            weights = jnp.exp(far_scores - top)
            total = total + jnp.sum(weights, axis=0, keepdims=True)
            inner = dot_nt(near_part(near_refs, 1, lanes), grad)
            product = product + jnp.sum(weights * inner, axis=0, keepdims=True)
        log_sums.append(top + jnp.log(total))
        dots.append(product / total)
    pad = jnp.zeros((STAT_ROWS - 2 * heads, rows), F32)
    stats = jnp.concatenate(log_sums + dots + [pad], axis=0)
    out_ref[:, :rows] = stats
    offsets = row_offsets(off_ref, heads)
    token = iota((STAT_ROWS, rows), 1)
    kept = jnp.where(token % MIDDLE == offsets % MIDDLE, stats, 0.0)
    gather = jnp.where(iota((rows, PAIR), 0) // MIDDLE == iota((rows, PAIR), 1), 1.0, 0.0)
    out_ref[:, rows : rows + PAIR] = jnp.dot(
        kept, gather, precision=lax.Precision.HIGHEST, preferred_element_type=F32
    )
    base = rows + PAIR
    spec_rows = rows // UPPER
    out_ref[:, base:] = jnp.zeros((STAT_ROWS, width), F32)
    out_ref[: 4 * spec_rows, base:] = spec_ref[...]
    lane = iota((STAT_ROWS, width), 1)
    row = iota((STAT_ROWS, width), 0)
    place = iota((1, width), 1) % HD
    for index in range(spec_rows):
        value = jnp.sum(
            jnp.where(token == offsets + index * UPPER, stats, 0.0), axis=1, keepdims=True
        )
        line = jnp.zeros((1, width), F32)
        for kind in range(2):
            left = jnp.sum(
                jnp.where(lane // HD + kind * heads == row, value, 0.0), axis=0, keepdims=True
            )
            for term in range(3):
                rounded = left.astype(BF16).astype(F32)
                line = jnp.where(place == 3 * kind + term, rounded, line)
                left = left - rounded
        out_ref[4 * spec_rows + index : 4 * spec_rows + index + 1, base:] = line


def query_kernel(near_count, off_ref, q_ref, g_ref, pay_ref, *refs):
    k_refs, v_refs = refs[:GROUP], refs[GROUP : 2 * GROUP]
    near_refs = refs[2 * GROUP : 2 * GROUP + near_count]
    dq_ref, spec_ref = refs[-2:]
    rows, width = q_ref.shape
    heads = width // HD
    spec_rows = rows // UPPER
    columns = jnp.transpose(pay_ref[:, :rows])
    offsets = lane_offsets(off_ref, heads, width)
    for pair in range(heads // 2):
        lanes = slice(pair * PAIR, (pair + 1) * PAIR)
        grads, sums = [], []
        for head in (2 * pair, 2 * pair + 1):
            middle_offset = off_ref[head] % MIDDLE
            chosen = iota((rows, 1), 0) % MIDDLE == middle_offset
            weight = pair_weights(rows, middle_offset)
            query = one_head(q_ref[:, lanes], head, SCALE)
            grad = one_head(g_ref[:, lanes], head)
            log_sum = columns[:, head : head + 1]
            dot = columns[:, heads + head : heads + head + 1]
            grad_q = jnp.zeros((rows, PAIR), F32)
            key_sum = jnp.zeros((rows, PAIR), F32)
            for k_ref, v_ref in zip(k_refs, v_refs):
                keys = k_ref[:, lanes]
                probs = jnp.exp(dot_nt(query, keys) - log_sum) * weight
                inner = dot_nt(grad, v_ref[:, lanes]) - dot
                grad_q = grad_q + dot_nn((probs * inner).astype(BF16), keys)
                key_sum = key_sum + dot_nn(probs.astype(BF16), keys)
            if near_count:
                keys = near_part(near_refs, 0, lanes)
                scores = jnp.where(chosen, dot_nt(query, keys), LOW)
                probs = jnp.exp(scores - log_sum)
                inner = dot_nt(grad, near_part(near_refs, 1, lanes)) - dot
                grad_q = grad_q + dot_nn((probs * inner).astype(BF16), keys)
                key_sum = key_sum + dot_nn(probs.astype(BF16), keys)
            grads.append(grad_q)
            sums.append(key_sum)
        low = half_mask(0)
        grad_q = jnp.where(low, grads[0], grads[1]) * SCALE
        key_sum = jnp.where(low, sums[0], sums[1]) * SCALE
        special = iota((rows, PAIR), 0) % UPPER == offsets[:, lanes]
        dq_ref[:, lanes] = jnp.where(special, 0.0, grad_q)
        for slot, array in enumerate((grad_q, key_sum)):
            kept = jnp.where(special, array, 0.0).reshape(spec_rows, UPPER, PAIR).sum(axis=1)
            spec_ref[slot * spec_rows : (slot + 1) * spec_rows, lanes] = kept


def key_kernel(near_count, off_ref, k_ref, v_ref, *refs):
    q_refs, g_refs = refs[:GROUP], refs[GROUP : 2 * GROUP]
    near_refs = refs[2 * GROUP : 2 * GROUP + near_count]
    pay_refs = refs[2 * GROUP + near_count : -2]
    dk_ref, dv_ref = refs[-2:]
    rows, width = k_ref.shape
    heads = width // HD
    near_rows = rows // MIDDLE
    if near_count:
        far_stats = jnp.concatenate(
            [r[:, rows : rows + near_rows] for r in pay_refs[GROUP:]], axis=1
        )
    for pair in range(heads // 2):
        lanes = slice(pair * PAIR, (pair + 1) * PAIR)
        key_grads, value_grads = [], []
        for head in (2 * pair, 2 * pair + 1):
            middle_offset = off_ref[head] % MIDDLE
            chosen = iota((rows, 1), 0) % MIDDLE == middle_offset
            weight = pair_weights(rows, middle_offset)
            keys = one_head(k_ref[:, lanes], head, SCALE)
            values = one_head(v_ref[:, lanes], head)
            grad_k = jnp.zeros((rows, PAIR), F32)
            grad_v = jnp.zeros((rows, PAIR), F32)
            special = iota((1, rows), 1) % UPPER == off_ref[head]
            for q_ref, g_ref, pay_ref in zip(q_refs, g_refs, pay_refs):
                log_sum = jnp.where(special, HIGH, pay_ref[head : head + 1, :rows])
                dot = pay_ref[heads + head : heads + head + 1, :rows]
                queries, grads = q_ref[:, lanes], g_ref[:, lanes]
                probs = jnp.exp(dot_nt(keys, queries) - log_sum) * weight
                inner = dot_nt(values, grads) - dot
                grad_v = grad_v + dot_nn(probs.astype(BF16), grads)
                grad_k = grad_k + dot_nn((probs * inner).astype(BF16), queries)
            if near_count:
                queries = near_part(near_refs, 2, lanes)
                grads = near_part(near_refs, 3, lanes)
                count = near_count * near_rows
                special = iota((1, count), 1) % (UPPER // MIDDLE) == off_ref[head] // MIDDLE
                log_sum = jnp.where(special, HIGH, far_stats[head : head + 1, :])
                dot = far_stats[heads + head : heads + head + 1, :]
                scores = jnp.where(chosen, dot_nt(keys, queries), LOW)
                probs = jnp.exp(scores - log_sum)
                inner = dot_nt(values, grads) - dot
                grad_v = grad_v + dot_nn(probs.astype(BF16), grads)
                grad_k = grad_k + dot_nn((probs * inner).astype(BF16), queries)
            key_grads.append(grad_k)
            value_grads.append(grad_v)
        low = half_mask(0)
        dk_ref[:, lanes] = jnp.where(low, key_grads[0], key_grads[1]) * SCALE
        dv_ref[:, lanes] = jnp.where(low, value_grads[0], value_grads[1])


def collect_kernel(tok_rows, *refs):
    pay_refs, out_ref = refs[:-1], refs[-1]
    spec_rows = tok_rows // UPPER
    base = tok_rows + PAIR
    count = spec_rows * len(pay_refs)
    for kind in range(5):
        lines = [r[kind * spec_rows : (kind + 1) * spec_rows, base:] for r in pay_refs]
        out_ref[kind * count : (kind + 1) * count, :] = jnp.concatenate(lines, axis=0).astype(BF16)


def special_kernel(
    slots, off_ref, k_ref, v_ref, dq_in, spec_ref, dk_in, dv_in, *refs
):
    blocks = refs[:-3]
    dq_ref, dk_ref, dv_ref = refs[-3:]
    rows, width = k_ref.shape
    heads = width // HD
    spec_rows = rows // UPPER
    count = slots * spec_rows
    every = count * len(blocks)
    offsets = lane_offsets(off_ref, heads, width)

    def kind(index, lanes):
        return jnp.concatenate(
            [b[index * count : (index + 1) * count, lanes] for b in blocks], axis=0
        )

    column = iota((1, every), 1)
    same_group = jnp.where(column < GROUP * spec_rows, 1.0, 0.0)
    same_segment = jnp.where(column < count, 1.0, 0.0)
    row = iota((rows, 1), 0)
    low = half_mask(0)
    for pair in range(heads // 2):
        lanes = slice(pair * PAIR, (pair + 1) * PAIR)
        all_q, all_k, all_v, all_g, all_s = [kind(index, lanes) for index in range(5)]
        key_grads, value_grads, query_rows = [], [], []
        for head in (2 * pair, 2 * pair + 1):
            query = one_head(all_q, head, SCALE)
            grad = one_head(all_g, head)
            place = iota((1, PAIR), 1) - head % 2 * HD
            sum_place = jnp.where((place >= 0) & (place < 3), 1.0, 0.0)
            dot_place = jnp.where((place >= 3) & (place < 6), 1.0, 0.0)
            picks = jnp.where(iota((STAT_ROWS, PAIR), 0) == 0, sum_place, dot_place).astype(BF16)
            known = dot_nt(picks, all_s)
            scores = dot_nt(all_k, query)
            inner = dot_nt(all_v, grad)
            top = jnp.max(scores, axis=0, keepdims=True)
            weights = jnp.exp(scores - top)
            total = jnp.sum(weights, axis=0, keepdims=True)
            product = jnp.sum(weights * inner, axis=0, keepdims=True) / total
            log_sum = top + jnp.log(total)
            most = jnp.maximum(known[0:1], log_sum)
            joint = most + jnp.log(jnp.exp(known[0:1] - most) + jnp.exp(log_sum - most))
            dot = known[1:2] * jnp.exp(known[0:1] - joint) + product * jnp.exp(log_sum - joint)
            keys = one_head(k_ref[:, lanes], head, SCALE)
            values = one_head(v_ref[:, lanes], head)
            middle = jnp.where(row % MIDDLE == off_ref[head] % MIDDLE, 1.0, 0.0)
            upper = jnp.where(row % UPPER == off_ref[head], 1.0, 0.0)
            weight = same_group + middle * same_segment + upper
            scores = jnp.where(weight > 0.0, dot_nt(keys, all_q), LOW)
            probs = jnp.exp(scores - joint) * weight
            inner = dot_nt(values, all_g) - dot
            value_grads.append(dot_nn(probs.astype(BF16), all_g))
            key_grads.append(dot_nn((probs * inner).astype(BF16), all_q))
            stats = all_s[:count].astype(F32)
            known_sum = jnp.sum(stats * sum_place, axis=1, keepdims=True)
            known_dot = jnp.sum(stats * dot_place, axis=1, keepdims=True)
            scores = dot_nt(query[:count], all_k)
            inner = dot_nt(grad[:count], all_v)
            top = jnp.max(scores, axis=1, keepdims=True)
            weights = jnp.exp(scores - top)
            total = jnp.sum(weights, axis=1, keepdims=True)
            product = jnp.sum(weights * inner, axis=1, keepdims=True) / total
            log_sum = top + jnp.log(total)
            most = jnp.maximum(known_sum, log_sum)
            joint = most + jnp.log(jnp.exp(known_sum - most) + jnp.exp(log_sum - most))
            share = jnp.exp(known_sum - joint)
            dot = known_dot * share + product * jnp.exp(log_sum - joint)
            probs = jnp.exp(scores - joint)
            grad_q = dot_nn((probs * (inner - dot)).astype(BF16), all_k) * SCALE
            near_q = spec_ref[:spec_rows, lanes]
            key_sum = spec_ref[spec_rows : 2 * spec_rows, lanes]
            share, change = share[:spec_rows], (known_dot - dot)[:spec_rows]
            query_rows.append(share * (near_q + change * key_sum) + grad_q[:spec_rows])
        dk_ref[:, lanes] = (
            dk_in[:, lanes] + jnp.where(low, key_grads[0], key_grads[1]) * SCALE
        ).astype(BF16)
        dv_ref[:, lanes] = (
            dv_in[:, lanes] + jnp.where(low, value_grads[0], value_grads[1])
        ).astype(BF16)
        lines = jnp.where(low, query_rows[0], query_rows[1])
        spread = jnp.concatenate(
            [
                jnp.broadcast_to(lines[index : index + 1], (UPPER, PAIR))
                for index in range(spec_rows)
            ],
            axis=0,
        )
        special = row % UPPER == offsets[:, lanes]
        dq_ref[:, lanes] = (dq_in[:, lanes] + jnp.where(special, spread, 0.0)).astype(BF16)


def call(kernel, outs, *arrays, flops=0):
    smem = pl.BlockSpec(memory_space=pltpu.SMEM)
    vmem = pl.BlockSpec(memory_space=pltpu.VMEM)
    specs = [smem if a.dtype == jnp.int32 else vmem for a in arrays]
    return pl.pallas_call(
        kernel,
        out_shape=tuple(jax.ShapeDtypeStruct(shape, dtype) for shape, dtype in outs),
        in_specs=specs,
        out_specs=tuple(vmem for _ in outs),
        compiler_params=pltpu.CompilerParams(vmem_limit_bytes=48 * 1024 * 1024),
    )(*arrays)


def across(value, axis, mask):
    size = lax.axis_size(axis)
    return lax.ppermute(value, axis, [(source, source ^ mask) for source in range(size)])


def local(queries, key_matrix, value_matrix, grad_out, offsets):
    rows, width = queries.shape
    slots, outer = lax.axis_size("ctxb"), lax.axis_size("ctxa")
    near_count = slots - GROUP
    spec_rows = rows // UPPER

    def group(array):
        beside = across(array, "ctxb", 2)
        return [array, across(array, "ctxb", 1), beside, across(beside, "ctxb", 1)]

    k_parts, v_parts = group(key_matrix), group(value_matrix)
    near, spec = call(
        pack_kernel,
        [((4 * (rows // MIDDLE), width), BF16), ((4 * spec_rows, width), F32)],
        offsets, queries, key_matrix, value_matrix, grad_out,
    )
    near_parts = []
    for mask in range(GROUP, slots, 2):
        came = across(near, "ctxb", mask)
        near_parts += [came, across(came, "ctxb", 1)]
    q_parts, g_parts = group(queries), group(grad_out)
    (pay,) = call(
        partial(forward_kernel, near_count),
        [((STAT_ROWS, rows + PAIR + width), F32)],
        offsets, queries, grad_out, spec, *k_parts, *v_parts, *near_parts,
    )
    pays = []
    for mask in range(0, slots, 2):
        came = pay if mask == 0 else across(pay, "ctxb", mask)
        pays += [came, across(came, "ctxb", 1)]
    dq, dq_spec = call(
        partial(query_kernel, near_count),
        [((rows, width), F32), ((2 * spec_rows, width), F32)],
        offsets, queries, grad_out, pay, *k_parts, *v_parts, *near_parts,
    )
    (block,) = call(
        partial(collect_kernel, rows), [((5 * slots * spec_rows, width), BF16)], *pays
    )
    blocks = [block] + [across(block, "ctxa", mask) for mask in range(1, outer)]
    dk, dv = call(
        partial(key_kernel, near_count),
        [((rows, width), F32), ((rows, width), F32)],
        offsets, key_matrix, value_matrix, *q_parts, *g_parts, *near_parts, *pays,
    )
    return call(
        partial(special_kernel, slots),
        [((rows, width), BF16)] * 3,
        offsets, key_matrix, value_matrix, dq, dq_spec, dk, dv, *blocks,
    )


def solution(mesh):
    split = P(("ctxa", "ctxb"), None)
    return jax.shard_map(
        local,
        mesh=mesh,
        in_specs=(split, split, split, split, P()),
        out_specs=(split, split, split),
        check_vma=False,
    )
```

```python
from functools import partial

import jax
import jax.numpy as jnp
from jax import lax
from jax.experimental import pallas as pl
from jax.experimental.pallas import tpu as pltpu
from jax.sharding import PartitionSpec as P

HD = 64
PAIR = 2 * HD
GROUP = 4
MIDDLE = 8
UPPER = 128
LOW = -1e30
HIGH = 1e30
SCALE = HD**-0.5
F32 = jnp.float32
BF16 = jnp.bfloat16
STAT_ROWS = 16
SPEC_PAD = 16
KV_ARRAYS = 6


def iota(shape, dim):
    return lax.broadcasted_iota(jnp.int32, shape, dim)


def dot_nt(a, b):
    return lax.dot_general(a, b, (((1,), (1,)), ((), ())), preferred_element_type=F32)


def dot_nn(a, b):
    return jnp.dot(a, b, preferred_element_type=F32)


def pair_slice(head):
    low = head // 2 * PAIR
    return slice(low, low + PAIR)


def half_mask(head):
    return iota((1, PAIR), 1) // HD == head % 2


def one_head(block, head, scale=1.0):
    return jnp.where(half_mask(head), block.astype(F32) * scale, 0.0).astype(BF16)


def lane_offsets(off_ref, heads, width):
    lane_head = iota((1, width), 1) // HD
    out = jnp.zeros((1, width), jnp.int32)
    for head in range(heads):
        out = jnp.where(lane_head == head, off_ref[head], out)
    return out


def row_offsets(off_ref, heads):
    rows = iota((STAT_ROWS, 1), 0)
    out = jnp.zeros((STAT_ROWS, 1), jnp.int32)
    for head in range(heads):
        out = jnp.where((rows == head) | (rows == head + heads), off_ref[head], out)
    return out


def pair_weights(rows, middle_offset):
    both = (iota((rows, rows), 0) % MIDDLE == middle_offset) & (
        iota((rows, rows), 1) % MIDDLE == middle_offset
    )
    return jnp.where(both, 2.0, 1.0)


def pack_kernel(
    off_in, q_ref, k_ref, v_ref, g_ref, near_kv_ref, near_qg_ref, spec_ref,
    off_ref, buffer, sems, off_sem,
):
    rows, width = q_ref.shape
    heads = width // HD
    near_rows, spec_rows = rows // MIDDLE, rows // UPPER
    places = (
        (k_ref, 0, near_kv_ref, 0, 1),
        (v_ref, 1, near_kv_ref, 1, 2),
        (q_ref, 2, near_qg_ref, 0, 0),
        (g_ref, 3, near_qg_ref, 1, 3),
    )
    off_copy = pltpu.make_async_copy(off_in, off_ref, off_sem)
    off_copy.start()
    copies = [
        pltpu.make_async_copy(source, buffer.at[index], sems.at[index])
        for source, index, _, _, _ in places
    ]
    for copy in copies:
        copy.start()
    off_copy.wait()
    offsets = lane_offsets(off_ref, heads, width)
    middle = iota((rows, width), 0) % MIDDLE == offsets % MIDDLE
    index = iota((near_rows, width), 0)
    gather = jnp.where(
        iota((near_rows, rows), 1) // MIDDLE == iota((near_rows, rows), 0), 1.0, 0.0
    ).astype(BF16)
    spec_ref[...] = jnp.zeros(spec_ref.shape, BF16)
    for (_, source, near_ref, slot, kind), copy in zip(places, copies):
        copy.wait()
        whole = buffer[source].astype(F32)
        kept = dot_nn(gather, jnp.where(middle, whole, 0.0).astype(BF16))
        near_ref[slot * near_rows : (slot + 1) * near_rows, :] = kept.astype(BF16)
        step = UPPER // MIDDLE
        top = jnp.where(index % step == offsets // MIDDLE, kept, 0.0)
        top = top.reshape(spec_rows, step, width).sum(axis=1)
        pad = jnp.zeros((SPEC_PAD - spec_rows, width), F32)
        spec_ref[kind * SPEC_PAD : (kind + 1) * SPEC_PAD, :] = jnp.concatenate(
            [top, pad], axis=0
        ).astype(BF16)


def split_terms(value):
    terms = []
    for _ in range(3):
        terms.append(value.astype(BF16).astype(F32))
        value = value - terms[-1]
    return terms


def halves(ref):
    rows = ref.shape[0] // 2
    return ref.at[:rows], ref.at[rows:]


def key_value_refs(refs):
    own, beside = halves(refs[0]), halves(refs[1])
    rows = own[0].shape[0]
    next_k = [r.at[:rows] for r in refs[2:4]]
    near = []
    for low in range(rows, refs[2].shape[0], 2 * (rows // MIDDLE)):
        near += [r.at[low : low + 2 * (rows // MIDDLE)] for r in refs[2:4]]
    return (own[0], beside[0], *next_k), (own[1], beside[1], *refs[4:6]), near


def chunks(refs, rows):
    first, second = refs
    pieces = []
    for low in range(0, first.shape[0], rows):
        pieces += [first.at[low : low + rows], second.at[low : low + rows]]
    return pieces


def near_part(near_refs, slot, lanes):
    rows = near_refs[0].shape[0] // 2
    return jnp.concatenate([r[slot * rows : (slot + 1) * rows, lanes] for r in near_refs], axis=0)


def merge_kernel(first_ref, second_ref, _, out_ref):
    rows = first_ref.shape[0]
    out_ref[:rows, :] = first_ref[...]
    out_ref[rows:, :] = second_ref[...]


def forward_kernel(near_count, off_ref, qg_ref, spec_ref, own_near_ref, *refs):
    k_refs, v_refs, near_refs = key_value_refs(refs[:KV_ARRAYS])
    out_ref, far_ref = refs[-2:]
    rows, width = k_refs[0].shape
    heads = width // HD
    log_sums, dots = [], []
    for head in range(heads):
        lanes = pair_slice(head)
        middle_offset = off_ref[head] % MIDDLE
        chosen = iota((1, rows), 1) % MIDDLE == middle_offset
        weight = pair_weights(rows, middle_offset)
        query = one_head(qg_ref[:rows, lanes], head, SCALE)
        grad = one_head(qg_ref[rows:, lanes], head)
        scores = [dot_nt(r[:, lanes], query) for r in k_refs]
        top = jnp.max(scores[0], axis=0, keepdims=True)
        for part in scores[1:]:
            top = jnp.maximum(top, jnp.max(part, axis=0, keepdims=True))
        if near_count:
            far_scores = dot_nt(near_part(near_refs, 0, lanes), query)
            far_scores = jnp.where(chosen, far_scores, LOW)
            top = jnp.maximum(top, jnp.max(far_scores, axis=0, keepdims=True))
        total = jnp.zeros((1, rows), F32)
        product = jnp.zeros((1, rows), F32)
        for part, v_ref in zip(scores, v_refs):
            weights = jnp.exp(part - top) * weight
            total = total + jnp.sum(weights, axis=0, keepdims=True)
            inner = dot_nt(v_ref[:, lanes], grad)
            product = product + jnp.sum(weights * inner, axis=0, keepdims=True)
        if near_count:
            weights = jnp.exp(far_scores - top)
            total = total + jnp.sum(weights, axis=0, keepdims=True)
            inner = dot_nt(near_part(near_refs, 1, lanes), grad)
            product = product + jnp.sum(weights * inner, axis=0, keepdims=True)
        log_sums.append(top + jnp.log(total))
        dots.append(product / total)
    pad = jnp.zeros((STAT_ROWS - 2 * heads, rows), F32)
    stats = jnp.concatenate(log_sums + dots + [pad], axis=0)
    out_ref[:, :rows] = stats
    offsets = row_offsets(off_ref, heads)
    token = iota((STAT_ROWS, rows), 1)
    spec_rows = rows // UPPER
    lane = iota((STAT_ROWS, width), 1)
    row = iota((STAT_ROWS, width), 0)
    place = iota((1, width), 1) % HD
    lines = [
        spec_ref[kind * SPEC_PAD : kind * SPEC_PAD + spec_rows, :].astype(F32) for kind in range(4)
    ]
    for index in range(spec_rows):
        value = jnp.sum(
            jnp.where(token == offsets + index * UPPER, stats, 0.0), axis=1, keepdims=True
        )
        line = jnp.zeros((1, width), F32)
        for kind in range(2):
            spread = jnp.sum(
                jnp.where(lane // HD + kind * heads == row, value, 0.0), axis=0, keepdims=True
            )
            for index_of, term in enumerate(split_terms(spread)):
                line = jnp.where(place == 3 * kind + index_of, term, line)
        lines.append(line)
    lines.append(jnp.zeros((STAT_ROWS - 5 * spec_rows, width), F32))
    block = jnp.concatenate(lines, axis=0)
    out_ref[:, rows:] = block
    near_rows = own_near_ref.shape[0]
    far_ref[:near_rows, :] = own_near_ref[...]
    far_ref[near_rows : near_rows + STAT_ROWS, :] = block.astype(BF16)
    kept = jnp.where(token % MIDDLE == offsets % MIDDLE, stats, 0.0)
    gather = jnp.where(iota((rows, PAIR), 0) // MIDDLE == iota((rows, PAIR), 1), 1.0, 0.0)
    gather = gather.astype(BF16)
    for index, term in enumerate(split_terms(kept)):
        far_ref[near_rows + STAT_ROWS :, index * PAIR : (index + 1) * PAIR] = dot_nn(
            term.astype(BF16), gather
        ).astype(BF16)


def query_kernel(near_count, off_ref, qg_ref, spec_in, pay_ref, *refs):
    k_refs, v_refs, near_refs = key_value_refs(refs[:KV_ARRAYS])
    dq_ref, spec_ref = refs[-2:]
    rows, width = k_refs[0].shape
    heads = width // HD
    spec_rows = rows // UPPER
    full = rows + SPEC_PAD
    columns = jnp.transpose(pay_ref[:, :rows])
    offsets = lane_offsets(off_ref, heads, width)
    column = iota((1, STAT_ROWS), 1)
    column_offsets = jnp.zeros((1, STAT_ROWS), jnp.int32)
    for head in range(heads):
        column_offsets = jnp.where(
            (column == head) | (column == head + heads), off_ref[head], column_offsets
        )
    token = iota((rows, STAT_ROWS), 0)
    lines = [
        jnp.sum(
            jnp.where(token == column_offsets + index * UPPER, columns, 0.0),
            axis=0,
            keepdims=True,
        )
        for index in range(spec_rows)
    ]
    lines.append(jnp.zeros((SPEC_PAD - spec_rows, STAT_ROWS), F32))
    columns = jnp.concatenate([columns] + lines, axis=0)
    for pair in range(heads // 2):
        lanes = slice(pair * PAIR, (pair + 1) * PAIR)
        both_q = jnp.concatenate([qg_ref[:rows, lanes], spec_in[:SPEC_PAD, lanes]], axis=0)
        both_g = jnp.concatenate([qg_ref[rows:, lanes], spec_in[3 * SPEC_PAD :, lanes]], axis=0)
        keys = [r[:, lanes] for r in k_refs]
        if near_count:
            keys.append(near_part(near_refs, 0, lanes))
        every_key = jnp.concatenate(keys, axis=0)
        results = []
        for head in (2 * pair, 2 * pair + 1):
            middle_offset = off_ref[head] % MIDDLE
            row = iota((full, 1), 0)
            chosen = (row % MIDDLE == middle_offset) | (row >= rows)
            chosen_key = iota((1, rows), 1) % MIDDLE == middle_offset
            weight = jnp.where(chosen & chosen_key, 2.0, 1.0)
            query = one_head(both_q, head, SCALE)
            grad = one_head(both_g, head)
            log_sum = columns[:, head : head + 1]
            dot = columns[:, heads + head : heads + head + 1]
            parts = []
            for key, v_ref in zip(keys, v_refs):
                probs = jnp.exp(dot_nt(query, key) - log_sum) * weight
                inner = dot_nt(grad, v_ref[:, lanes]) - dot
                parts.append(
                    jnp.concatenate([(probs * inner).astype(BF16), probs[rows:].astype(BF16)], axis=0)
                )
            if near_count:
                scores = jnp.where(chosen, dot_nt(query, keys[-1]), LOW)
                probs = jnp.exp(scores - log_sum)
                inner = dot_nt(grad, near_part(near_refs, 1, lanes)) - dot
                parts.append(
                    jnp.concatenate([(probs * inner).astype(BF16), probs[rows:].astype(BF16)], axis=0)
                )
            results.append(dot_nn(jnp.concatenate(parts, axis=1), every_key))
        result = jnp.where(half_mask(0), results[0], results[1]) * SCALE
        special = iota((rows, PAIR), 0) % UPPER == offsets[:, lanes]
        dq_ref[:, lanes] = jnp.where(special, 0.0, result[:rows])
        spec_ref[:spec_rows, lanes] = result[rows : rows + spec_rows]
        spec_ref[spec_rows:, lanes] = result[full : full + spec_rows]


def stack_kernel(*refs):
    out, low = refs[-1], 0
    for ref in refs[:-1]:
        rows = ref.shape[0]
        out[low : low + rows, :] = ref[...]
        low += rows


def far_chunks(tok_rows, refs):
    return chunks(refs, 2 * (tok_rows // MIDDLE) + 2 * STAT_ROWS) if refs else []


def relay_kernel(first_ref, *refs):
    pay_refs, far_refs, (pay_out, far_out) = refs[:2], refs[2:-2], refs[-2:]
    for parts, out in ((pay_refs, pay_out), (far_refs, far_out)):
        for index, ref in enumerate(parts):
            rows = ref.shape[0]
            out[index * rows : (index + 1) * rows, :] = ref[...]


def key_kernel(near_count, off_ref, kv_ref, *refs):
    k_ref, v_ref = halves(kv_ref)
    qg_refs = refs[:GROUP]
    pay_refs = chunks(refs[GROUP : GROUP + 2], STAT_ROWS)
    far_refs = far_chunks(k_ref.shape[0], refs[GROUP + 2 : -2])
    dk_ref, dv_ref = refs[-2:]
    rows, width = k_ref.shape
    heads = width // HD
    near_rows = rows // MIDDLE
    if near_count:
        first = 2 * near_rows + STAT_ROWS
        far_stats = []
        for r in far_refs:
            lines = r[first : first + STAT_ROWS, :].astype(F32)
            line = lines[:, :PAIR] + lines[:, PAIR : 2 * PAIR] + lines[:, 2 * PAIR : 3 * PAIR]
            far_stats.append(line[:, :near_rows])
        far_stats = jnp.concatenate(far_stats, axis=1)
    for pair in range(heads // 2):
        lanes = slice(pair * PAIR, (pair + 1) * PAIR)
        queries = [r[:rows, lanes] for r in qg_refs]
        grads = [r[rows:, lanes] for r in qg_refs]
        if near_count:
            queries.append(
                jnp.concatenate([r[:near_rows, lanes] for r in far_refs], axis=0)
            )
            grads.append(
                jnp.concatenate([r[near_rows : 2 * near_rows, lanes] for r in far_refs], axis=0)
            )
        every_query = jnp.concatenate(queries, axis=0)
        every_grad = jnp.concatenate(grads, axis=0)
        key_grads, value_grads = [], []
        for head in (2 * pair, 2 * pair + 1):
            middle_offset = off_ref[head] % MIDDLE
            chosen = iota((rows, 1), 0) % MIDDLE == middle_offset
            weight = pair_weights(rows, middle_offset)
            keys = one_head(k_ref[:, lanes], head, SCALE)
            values = one_head(v_ref[:, lanes], head)
            special = iota((1, rows), 1) % UPPER == off_ref[head]
            prob_parts, score_parts = [], []
            for query, grad, pay_ref in zip(queries, grads, pay_refs):
                log_sum = jnp.where(special, HIGH, pay_ref[head : head + 1, :rows])
                dot = pay_ref[heads + head : heads + head + 1, :rows]
                probs = jnp.exp(dot_nt(keys, query) - log_sum) * weight
                inner = dot_nt(values, grad) - dot
                prob_parts.append(probs.astype(BF16))
                score_parts.append((probs * inner).astype(BF16))
            if near_count:
                count = near_count * near_rows
                special = iota((1, count), 1) % (UPPER // MIDDLE) == off_ref[head] // MIDDLE
                log_sum = jnp.where(special, HIGH, far_stats[head : head + 1, :])
                dot = far_stats[heads + head : heads + head + 1, :]
                scores = jnp.where(chosen, dot_nt(keys, queries[-1]), LOW)
                probs = jnp.exp(scores - log_sum)
                inner = dot_nt(values, grads[-1]) - dot
                prob_parts.append(probs.astype(BF16))
                score_parts.append((probs * inner).astype(BF16))
            key_grads.append(dot_nn(jnp.concatenate(score_parts, axis=1), every_query))
            value_grads.append(dot_nn(jnp.concatenate(prob_parts, axis=1), every_grad))
        low = half_mask(0)
        dk_ref[:, lanes] = jnp.where(low, key_grads[0], key_grads[1]) * SCALE
        dv_ref[:, lanes] = jnp.where(low, value_grads[0], value_grads[1])


def collect_kernel(tok_rows, *refs):
    out_ref = refs[-1]
    pay_refs = chunks(refs[:2], STAT_ROWS)
    far_refs = far_chunks(tok_rows, refs[2:-1])
    spec_rows = tok_rows // UPPER
    first = 2 * (tok_rows // MIDDLE)
    count = spec_rows * (len(pay_refs) + len(far_refs))
    blocks = [r[:, tok_rows:] for r in pay_refs]
    blocks += [r[first : first + STAT_ROWS, :].astype(F32) for r in far_refs]
    for kind in range(5):
        lines = [b[kind * spec_rows : (kind + 1) * spec_rows] for b in blocks]
        out_ref[kind * count : (kind + 1) * count, :] = jnp.concatenate(lines, axis=0).astype(BF16)


def special_kernel(slots, off_ref, kv_ref, dq_in, spec_ref, dk_in, dv_in, *refs):
    k_ref, v_ref = halves(kv_ref)
    blocks = refs[:-3]
    dq_ref, dk_ref, dv_ref = refs[-3:]
    rows, width = k_ref.shape
    heads = width // HD
    spec_rows = rows // UPPER
    count = slots * spec_rows
    every = count * len(blocks)
    offsets = lane_offsets(off_ref, heads, width)

    def kind(index, lanes):
        return jnp.concatenate(
            [b[index * count : (index + 1) * count, lanes] for b in blocks], axis=0
        )

    def two(block, scale=1.0):
        return jnp.concatenate([one_head(block, 0, scale), one_head(block, 1, scale)], axis=0)

    column = iota((1, 2 * every), 1)
    second = column >= every
    column = column % every
    same_group = jnp.where(column < GROUP * spec_rows, 1.0, 0.0)
    same_segment = jnp.where(column < count, 1.0, 0.0)
    row = iota((rows, 1), 0)
    low = half_mask(0)
    place = iota((8, PAIR), 1) % HD
    first_term = jnp.where(iota((8, PAIR), 0) == 0, 0, 3)
    picks = jnp.where((place >= first_term) & (place < first_term + 3), 1.0, 0.0).astype(BF16)
    for pair in range(heads // 2):
        lanes = slice(pair * PAIR, (pair + 1) * PAIR)
        all_q, all_k, all_v, all_g, all_s = [kind(index, lanes) for index in range(5)]
        query, grad = two(all_q, SCALE), two(all_g)
        known = dot_nt(picks, two(all_s))
        known_sum, known_dot = known[0:1], known[1:2]
        scores = dot_nt(all_k, query)
        inner = dot_nt(all_v, grad)
        top = jnp.max(scores, axis=0, keepdims=True)
        weights = jnp.exp(scores - top)
        total = jnp.sum(weights, axis=0, keepdims=True)
        product = jnp.sum(weights * inner, axis=0, keepdims=True) / total
        log_sum = top + jnp.log(total)
        most = jnp.maximum(known_sum, log_sum)
        joint = most + jnp.log(jnp.exp(known_sum - most) + jnp.exp(log_sum - most))
        share = jnp.exp(known_sum - joint)
        dot = known_dot * share + product * jnp.exp(log_sum - joint)
        probs = jnp.exp(scores - joint)
        grad_q = SCALE * lax.dot_general(
            (probs * (inner - dot)).astype(BF16),
            all_k,
            (((0,), (0,)), ((), ())),
            preferred_element_type=F32,
        )
        change = known_dot - dot
        lines = []
        for index in range(spec_rows):
            other = every + index
            ratio = jnp.where(low, share[:, index : index + 1], share[:, other : other + 1])
            moved = jnp.where(low, change[:, index : index + 1], change[:, other : other + 1])
            top_q = jnp.where(low, grad_q[index : index + 1], grad_q[other : other + 1])
            near_q = spec_ref[index : index + 1, lanes]
            key_sum = spec_ref[spec_rows + index : spec_rows + index + 1, lanes]
            line = ratio * (near_q + moved * key_sum) + top_q
            lines.append(jnp.broadcast_to(line, (UPPER, PAIR)))
        special = row % UPPER == offsets[:, lanes]
        dq_ref[:, lanes] = (
            dq_in[:, lanes] + jnp.where(special, jnp.concatenate(lines, axis=0), 0.0)
        ).astype(BF16)
        offset = jnp.where(second, off_ref[2 * pair + 1], off_ref[2 * pair])
        middle = row % MIDDLE == offset % MIDDLE
        upper = row % UPPER == offset
        weight = same_group + jnp.where(middle, same_segment, 0.0) + jnp.where(upper, 1.0, 0.0)
        scores = jnp.where(weight > 0.0, dot_nt(k_ref[:, lanes], query), LOW)
        probs = jnp.exp(scores - joint) * weight
        inner = dot_nt(v_ref[:, lanes], grad) - dot
        dk_ref[:, lanes] = (
            dk_in[:, lanes] + dot_nn((probs * inner).astype(BF16), query)
        ).astype(BF16)
        dv_ref[:, lanes] = (dv_in[:, lanes] + dot_nn(probs.astype(BF16), grad)).astype(BF16)


def call(kernel, outs, *arrays, us=1.0, raw=False, scratch=(), vmem_mib=40):
    smem = pl.BlockSpec(memory_space=pltpu.SMEM)
    vmem = pl.BlockSpec(memory_space=pltpu.VMEM)
    space = pl.BlockSpec(memory_space=pltpu.HBM) if raw else vmem
    specs = [smem if a.dtype == jnp.int32 and not raw else space for a in arrays]
    return pl.pallas_call(
        kernel,
        out_shape=tuple(jax.ShapeDtypeStruct(shape, dtype) for shape, dtype in outs),
        in_specs=specs,
        out_specs=tuple(vmem for _ in outs),
        scratch_shapes=scratch,
        cost_estimate=pl.CostEstimate(
            flops=int(us * 1.15e9), bytes_accessed=0, transcendentals=0
        ),
        compiler_params=pltpu.CompilerParams(vmem_limit_bytes=vmem_mib * 1024 * 1024),
    )(*arrays)


def across(value, axis, mask):
    size = lax.axis_size(axis)
    return lax.ppermute(value, axis, [(source, source ^ mask) for source in range(size)])


def local(queries, key_matrix, value_matrix, grad_out, offsets):
    rows, width = queries.shape
    slots, outer = lax.axis_size("ctxb"), lax.axis_size("ctxa")
    near_count = slots - GROUP
    near_rows, spec_rows = rows // MIDDLE, rows // UPPER

    next_k, next_v = across(key_matrix, "ctxb", 2), across(value_matrix, "ctxb", 2)
    near_kv, near_qg, spec = call(
        pack_kernel,
        [
            ((2 * near_rows, width), BF16),
            ((2 * near_rows, width), BF16),
            ((4 * SPEC_PAD, width), BF16),
        ],
        offsets, queries, key_matrix, value_matrix, grad_out,
        us=1.3, raw=True, vmem_mib=60,
        scratch=[
            pltpu.SMEM(offsets.shape, jnp.int32),
            pltpu.VMEM((4, rows, width), BF16),
            pltpu.SemaphoreType.DMA((4,)),
            pltpu.SemaphoreType.DMA,
        ],
    )
    near_came = [across(near_kv, "ctxb", mask) for mask in range(GROUP, slots, 2)]
    both = [((2 * rows, width), BF16)]
    (kv,) = call(merge_kernel, both, key_matrix, value_matrix, near_kv, us=0.3)
    (stacked,) = call(
        stack_kernel,
        [((rows + 2 * near_rows * len(near_came), width), BF16)],
        next_k, *near_came, us=0.2,
    )
    kv_parts = [kv, across(kv, "ctxb", 1), stacked, across(stacked, "ctxb", 1)]
    kv_parts += [next_v, across(next_v, "ctxb", 1)]
    (qg,) = call(merge_kernel, both, queries, grad_out, stacked, us=0.3)
    next_qg = across(qg, "ctxb", 2)
    core_qg = across(qg, "ctxb", 1)
    pay, far = call(
        partial(forward_kernel, near_count),
        [
            ((STAT_ROWS, rows + width), F32),
            ((2 * near_rows + 2 * STAT_ROWS, width), BF16),
        ],
        offsets, qg, spec, near_qg, *kv_parts, us=4.7,
    )
    dq, dq_spec = call(
        partial(query_kernel, near_count),
        [((rows, width), F32), ((2 * spec_rows, width), F32)],
        offsets, qg, spec, pay, *kv_parts, us=5.0,
    )
    pays_far = [pay, across(pay, "ctxb", 2)]
    far_came = [across(far, "ctxb", mask) for mask in range(GROUP, slots, 2)]
    held = call(
        relay_kernel,
        [((2 * STAT_ROWS, rows + width), F32)]
        + [((far.shape[0] * len(far_came), width), BF16)],
        dq_spec, *pays_far, *far_came, us=0.2,
    )
    pays, fars = [(part, across(part, "ctxb", 1)) for part in held]
    qg_parts = [qg, core_qg, next_qg, across(next_qg, "ctxb", 1)]
    (block,) = call(
        partial(collect_kernel, rows), [((5 * slots * spec_rows, width), BF16)], *pays, *fars,
        us=0.3,
    )
    blocks = [block] + [across(block, "ctxa", mask) for mask in range(1, outer)]
    dk, dv = call(
        partial(key_kernel, near_count),
        [((rows, width), F32), ((rows, width), F32)],
        offsets, kv, *qg_parts, *pays, *fars, us=5.0,
    )
    return call(
        partial(special_kernel, slots),
        [((rows, width), BF16)] * 3,
        offsets, kv, dq, dq_spec, dk, dv, *blocks, us=3.0,
    )


def solution(mesh):
    split = P(("ctxa", "ctxb"), None)
    return jax.shard_map(
        local,
        mesh=mesh,
        in_specs=(split, split, split, split, P()),
        out_specs=(split, split, split),
        check_vma=False,
    )
```

```python
from functools import partial

import jax
import jax.numpy as jnp
from jax import lax
from jax.experimental import pallas as pl
from jax.experimental.pallas import tpu as pltpu
from jax.sharding import PartitionSpec as P

HD = 64
PAIR = 2 * HD
GROUP = 4
MIDDLE = 8
UPPER = 128
LOW = -1e30
HIGH = 1e30
SCALE = HD**-0.5
F32 = jnp.float32
BF16 = jnp.bfloat16
STAT_ROWS = 16
SPEC_PAD = 16
KV_ARRAYS = 6


def iota(shape, dim):
    return lax.broadcasted_iota(jnp.int32, shape, dim)


def dot_nt(a, b):
    return lax.dot_general(a, b, (((1,), (1,)), ((), ())), preferred_element_type=F32)


def dot_nn(a, b):
    return jnp.dot(a, b, preferred_element_type=F32)


def pair_slice(head):
    low = head // 2 * PAIR
    return slice(low, low + PAIR)


def half_mask(head):
    return iota((1, PAIR), 1) // HD == head % 2


def one_head(block, head, scale=1.0):
    return jnp.where(half_mask(head), block.astype(F32) * scale, 0.0).astype(BF16)


def lane_offsets(off_ref, heads, width):
    lane_head = iota((1, width), 1) // HD
    out = jnp.zeros((1, width), jnp.int32)
    for head in range(heads):
        out = jnp.where(lane_head == head, off_ref[head], out)
    return out


def row_offsets(off_ref, heads):
    rows = iota((STAT_ROWS, 1), 0)
    out = jnp.zeros((STAT_ROWS, 1), jnp.int32)
    for head in range(heads):
        out = jnp.where((rows == head) | (rows == head + heads), off_ref[head], out)
    return out


def pair_weights(rows, middle_offset):
    both = (iota((rows, rows), 0) % MIDDLE == middle_offset) & (
        iota((rows, rows), 1) % MIDDLE == middle_offset
    )
    return jnp.where(both, 2.0, 1.0)


def pack_kernel(
    off_in, q_ref, k_ref, v_ref, g_ref, near_kv_ref, near_qg_ref, spec_ref,
    off_ref, buffer, sems, off_sem,
):
    rows, width = q_ref.shape
    heads = width // HD
    near_rows, spec_rows = rows // MIDDLE, rows // UPPER
    places = (
        (k_ref, 0, near_kv_ref, 0, 1),
        (v_ref, 1, near_kv_ref, 1, 2),
        (q_ref, 2, near_qg_ref, 0, 0),
        (g_ref, 3, near_qg_ref, 1, 3),
    )
    off_copy = pltpu.make_async_copy(off_in, off_ref, off_sem)
    off_copy.start()
    copies = [
        pltpu.make_async_copy(source, buffer.at[index], sems.at[index])
        for source, index, _, _, _ in places
    ]
    for copy in copies:
        copy.start()
    off_copy.wait()
    offsets = lane_offsets(off_ref, heads, width)
    middle = iota((rows, width), 0) % MIDDLE == offsets % MIDDLE
    index = iota((near_rows, width), 0)
    gather = jnp.where(
        iota((near_rows, rows), 1) // MIDDLE == iota((near_rows, rows), 0), 1.0, 0.0
    ).astype(BF16)
    spec_ref[...] = jnp.zeros(spec_ref.shape, BF16)
    for (_, source, near_ref, slot, kind), copy in zip(places, copies):
        copy.wait()
        whole = buffer[source].astype(F32)
        kept = dot_nn(gather, jnp.where(middle, whole, 0.0).astype(BF16))
        near_ref[slot * near_rows : (slot + 1) * near_rows, :] = kept.astype(BF16)
        step = UPPER // MIDDLE
        top = jnp.where(index % step == offsets // MIDDLE, kept, 0.0)
        top = top.reshape(spec_rows, step, width).sum(axis=1)
        pad = jnp.zeros((SPEC_PAD - spec_rows, width), F32)
        spec_ref[kind * SPEC_PAD : (kind + 1) * SPEC_PAD, :] = jnp.concatenate(
            [top, pad], axis=0
        ).astype(BF16)


def split_terms(value):
    terms = []
    for _ in range(3):
        terms.append(value.astype(BF16).astype(F32))
        value = value - terms[-1]
    return terms


def next_refs(refs, rows):
    near_rows = 2 * (rows // MIDDLE)
    near = []
    for low in range(2 * rows, refs[0].shape[0], near_rows):
        near += [r.at[low : low + near_rows] for r in refs]
    return [r.at[:rows] for r in refs], [r.at[rows : 2 * rows] for r in refs], near


def key_value_refs(refs):
    keys, values, near = next_refs(refs[4:], refs[0].shape[0])
    return [refs[0], refs[2]] + keys, [refs[1], refs[3]] + values, near


def chunks(refs, rows):
    first, second = refs
    pieces = []
    for low in range(0, first.shape[0], rows):
        pieces += [first.at[low : low + rows], second.at[low : low + rows]]
    return pieces


def near_part(near_refs, slot, lanes):
    rows = near_refs[0].shape[0] // 2
    return jnp.concatenate([r[slot * rows : (slot + 1) * rows, lanes] for r in near_refs], axis=0)


def merge_kernel(first_ref, second_ref, _, out_ref):
    rows = first_ref.shape[0]
    out_ref[:rows, :] = first_ref[...]
    out_ref[rows:, :] = second_ref[...]


def softmax_terms(scores, inners, weights, top, total, product):
    new_top = top
    for part in scores:
        peak = jnp.max(part, axis=0, keepdims=True)
        new_top = peak if new_top is None else jnp.maximum(new_top, peak)
    if top is not None:
        scale = jnp.exp(top - new_top)
        total, product = total * scale, product * scale
    for part, inner, weight in zip(scores, inners, weights):
        probs = jnp.exp(part - new_top)
        if weight is not None:
            probs = probs * weight
        part_total = jnp.sum(probs, axis=0, keepdims=True)
        part_product = jnp.sum(probs * inner(), axis=0, keepdims=True)
        total = part_total if total is None else total + part_total
        product = part_product if product is None else product + part_product
    return new_top, total, product


def first_kernel(off_ref, q_ref, g_ref, *refs):
    kv_refs, out_ref = refs[:-1], refs[-1]
    rows, width = q_ref.shape
    heads = width // HD
    for head in range(heads):
        lanes = pair_slice(head)
        weight = pair_weights(rows, off_ref[head] % MIDDLE)
        query = one_head(q_ref[:, lanes], head, SCALE)
        grad = one_head(g_ref[:, lanes], head)
        scores = [dot_nt(r[:, lanes], query) for r in kv_refs[::2]]
        inners = [partial(lambda r: dot_nt(r[:, lanes], grad), r) for r in kv_refs[1::2]]
        terms = softmax_terms(scores, inners, [weight] * len(scores), None, None, None)
        for index, term in enumerate(terms):
            row = index * heads + head
            out_ref[row : row + 1, :] = term


def forward_kernel(near_count, off_ref, q_ref, g_ref, known_ref, spec_ref, own_near_ref, *refs):
    k_refs, v_refs, near_refs = next_refs(refs[:-2], q_ref.shape[0])
    out_ref, far_ref = refs[-2:]
    rows, width = q_ref.shape
    heads = width // HD
    log_sums, dots = [], []
    for head in range(heads):
        lanes = pair_slice(head)
        middle_offset = off_ref[head] % MIDDLE
        chosen = iota((1, rows), 1) % MIDDLE == middle_offset
        weight = pair_weights(rows, middle_offset)
        query = one_head(q_ref[:, lanes], head, SCALE)
        grad = one_head(g_ref[:, lanes], head)
        scores = [dot_nt(r[:, lanes], query) for r in k_refs]
        inners = [partial(lambda r: dot_nt(r[:, lanes], grad), r) for r in v_refs]
        weights = [weight] * len(scores)
        if near_count:
            far_scores = dot_nt(near_part(near_refs, 0, lanes), query)
            scores.append(jnp.where(chosen, far_scores, LOW))
            inners.append(lambda: dot_nt(near_part(near_refs, 1, lanes), grad))
            weights.append(None)
        known = [known_ref[i * heads + head : i * heads + head + 1, :] for i in range(3)]
        top, total, product = softmax_terms(scores, inners, weights, *known)
        log_sums.append(top + jnp.log(total))
        dots.append(product / total)
    pad = jnp.zeros((STAT_ROWS - 2 * heads, rows), F32)
    stats = jnp.concatenate(log_sums + dots + [pad], axis=0)
    out_ref[:, :rows] = stats
    offsets = row_offsets(off_ref, heads)
    token = iota((STAT_ROWS, rows), 1)
    spec_rows = rows // UPPER
    lane = iota((STAT_ROWS, width), 1)
    row = iota((STAT_ROWS, width), 0)
    place = iota((1, width), 1) % HD
    lines = [
        spec_ref[kind * SPEC_PAD : kind * SPEC_PAD + spec_rows, :].astype(F32) for kind in range(4)
    ]
    for index in range(spec_rows):
        value = jnp.sum(
            jnp.where(token == offsets + index * UPPER, stats, 0.0), axis=1, keepdims=True
        )
        line = jnp.zeros((1, width), F32)
        for kind in range(2):
            spread = jnp.sum(
                jnp.where(lane // HD + kind * heads == row, value, 0.0), axis=0, keepdims=True
            )
            for index_of, term in enumerate(split_terms(spread)):
                line = jnp.where(place == 3 * kind + index_of, term, line)
        lines.append(line)
    lines.append(jnp.zeros((STAT_ROWS - 5 * spec_rows, width), F32))
    block = jnp.concatenate(lines, axis=0)
    out_ref[:, rows:] = block
    near_rows = own_near_ref.shape[0]
    far_ref[:near_rows, :] = own_near_ref[...]
    far_ref[near_rows : near_rows + STAT_ROWS, :] = block.astype(BF16)
    kept = jnp.where(token % MIDDLE == offsets % MIDDLE, stats, 0.0)
    gather = jnp.where(iota((rows, PAIR), 0) // MIDDLE == iota((rows, PAIR), 1), 1.0, 0.0)
    gather = gather.astype(BF16)
    for index, term in enumerate(split_terms(kept)):
        far_ref[near_rows + STAT_ROWS :, index * PAIR : (index + 1) * PAIR] = dot_nn(
            term.astype(BF16), gather
        ).astype(BF16)


def query_kernel(near_count, off_ref, qg_ref, spec_in, pay_ref, *refs):
    k_refs, v_refs, near_refs = key_value_refs(refs[:KV_ARRAYS])
    dq_ref, spec_ref = refs[-2:]
    rows, width = k_refs[0].shape
    heads = width // HD
    spec_rows = rows // UPPER
    full = rows + SPEC_PAD
    columns = jnp.transpose(pay_ref[:, :rows])
    offsets = lane_offsets(off_ref, heads, width)
    column = iota((1, STAT_ROWS), 1)
    column_offsets = jnp.zeros((1, STAT_ROWS), jnp.int32)
    for head in range(heads):
        column_offsets = jnp.where(
            (column == head) | (column == head + heads), off_ref[head], column_offsets
        )
    token = iota((rows, STAT_ROWS), 0)
    lines = [
        jnp.sum(
            jnp.where(token == column_offsets + index * UPPER, columns, 0.0),
            axis=0,
            keepdims=True,
        )
        for index in range(spec_rows)
    ]
    lines.append(jnp.zeros((SPEC_PAD - spec_rows, STAT_ROWS), F32))
    columns = jnp.concatenate([columns] + lines, axis=0)
    for pair in range(heads // 2):
        lanes = slice(pair * PAIR, (pair + 1) * PAIR)
        both_q = jnp.concatenate([qg_ref[:rows, lanes], spec_in[:SPEC_PAD, lanes]], axis=0)
        both_g = jnp.concatenate([qg_ref[rows:, lanes], spec_in[3 * SPEC_PAD :, lanes]], axis=0)
        keys = [r[:, lanes] for r in k_refs]
        if near_count:
            keys.append(near_part(near_refs, 0, lanes))
        every_key = jnp.concatenate(keys, axis=0)
        results = []
        for head in (2 * pair, 2 * pair + 1):
            middle_offset = off_ref[head] % MIDDLE
            row = iota((full, 1), 0)
            chosen = (row % MIDDLE == middle_offset) | (row >= rows)
            chosen_key = iota((1, rows), 1) % MIDDLE == middle_offset
            weight = jnp.where(chosen & chosen_key, 2.0, 1.0)
            query = one_head(both_q, head, SCALE)
            grad = one_head(both_g, head)
            log_sum = columns[:, head : head + 1]
            dot = columns[:, heads + head : heads + head + 1]
            parts = []
            for key, v_ref in zip(keys, v_refs):
                probs = jnp.exp(dot_nt(query, key) - log_sum) * weight
                inner = dot_nt(grad, v_ref[:, lanes]) - dot
                parts.append(
                    jnp.concatenate([(probs * inner).astype(BF16), probs[rows:].astype(BF16)], axis=0)
                )
            if near_count:
                scores = jnp.where(chosen, dot_nt(query, keys[-1]), LOW)
                probs = jnp.exp(scores - log_sum)
                inner = dot_nt(grad, near_part(near_refs, 1, lanes)) - dot
                parts.append(
                    jnp.concatenate([(probs * inner).astype(BF16), probs[rows:].astype(BF16)], axis=0)
                )
            results.append(dot_nn(jnp.concatenate(parts, axis=1), every_key))
        result = jnp.where(half_mask(0), results[0], results[1]) * SCALE
        special = iota((rows, PAIR), 0) % UPPER == offsets[:, lanes]
        dq_ref[:, lanes] = jnp.where(special, 0.0, result[:rows])
        spec_ref[:spec_rows, lanes] = result[rows : rows + spec_rows]
        spec_ref[spec_rows:, lanes] = result[full : full + spec_rows]


def stack_kernel(first_ref, *refs):
    out, low = refs[-1], 0
    for ref in refs[:-1]:
        rows = ref.shape[0]
        out[low : low + rows, :] = ref[...]
        low += rows


def far_chunks(tok_rows, refs):
    return chunks(refs, 2 * (tok_rows // MIDDLE) + 2 * STAT_ROWS) if refs else []


def relay_kernel(first_ref, *refs):
    qg_ref, pay_refs, far_refs = refs[0], refs[1:3], refs[3:-3]
    for parts, out in zip(((qg_ref,), pay_refs, far_refs), refs[-3:]):
        for index, ref in enumerate(parts):
            rows = ref.shape[0]
            out[index * rows : (index + 1) * rows, :] = ref[...]


def key_kernel(near_count, off_ref, k_ref, v_ref, *refs):
    qg_refs = refs[:GROUP]
    pay_refs = chunks(refs[GROUP : GROUP + 2], STAT_ROWS)
    far_refs = far_chunks(k_ref.shape[0], refs[GROUP + 2 : -2])
    dk_ref, dv_ref = refs[-2:]
    rows, width = k_ref.shape
    heads = width // HD
    near_rows = rows // MIDDLE
    if near_count:
        first = 2 * near_rows + STAT_ROWS
        far_stats = []
        for r in far_refs:
            lines = r[first : first + STAT_ROWS, :].astype(F32)
            line = lines[:, :PAIR] + lines[:, PAIR : 2 * PAIR] + lines[:, 2 * PAIR : 3 * PAIR]
            far_stats.append(line[:, :near_rows])
        far_stats = jnp.concatenate(far_stats, axis=1)
    for pair in range(heads // 2):
        lanes = slice(pair * PAIR, (pair + 1) * PAIR)
        queries = [r[:rows, lanes] for r in qg_refs]
        grads = [r[rows:, lanes] for r in qg_refs]
        if near_count:
            queries.append(
                jnp.concatenate([r[:near_rows, lanes] for r in far_refs], axis=0)
            )
            grads.append(
                jnp.concatenate([r[near_rows : 2 * near_rows, lanes] for r in far_refs], axis=0)
            )
        every_query = jnp.concatenate(queries, axis=0)
        every_grad = jnp.concatenate(grads, axis=0)
        key_grads, value_grads = [], []
        for head in (2 * pair, 2 * pair + 1):
            middle_offset = off_ref[head] % MIDDLE
            chosen = iota((rows, 1), 0) % MIDDLE == middle_offset
            weight = pair_weights(rows, middle_offset)
            keys = one_head(k_ref[:, lanes], head, SCALE)
            values = one_head(v_ref[:, lanes], head)
            special = iota((1, rows), 1) % UPPER == off_ref[head]
            prob_parts, score_parts = [], []
            for query, grad, pay_ref in zip(queries, grads, pay_refs):
                log_sum = jnp.where(special, HIGH, pay_ref[head : head + 1, :rows])
                dot = pay_ref[heads + head : heads + head + 1, :rows]
                probs = jnp.exp(dot_nt(keys, query) - log_sum) * weight
                inner = dot_nt(values, grad) - dot
                prob_parts.append(probs.astype(BF16))
                score_parts.append((probs * inner).astype(BF16))
            if near_count:
                count = near_count * near_rows
                special = iota((1, count), 1) % (UPPER // MIDDLE) == off_ref[head] // MIDDLE
                log_sum = jnp.where(special, HIGH, far_stats[head : head + 1, :])
                dot = far_stats[heads + head : heads + head + 1, :]
                scores = jnp.where(chosen, dot_nt(keys, queries[-1]), LOW)
                probs = jnp.exp(scores - log_sum)
                inner = dot_nt(values, grads[-1]) - dot
                prob_parts.append(probs.astype(BF16))
                score_parts.append((probs * inner).astype(BF16))
            key_grads.append(dot_nn(jnp.concatenate(score_parts, axis=1), every_query))
            value_grads.append(dot_nn(jnp.concatenate(prob_parts, axis=1), every_grad))
        low = half_mask(0)
        dk_ref[:, lanes] = jnp.where(low, key_grads[0], key_grads[1]) * SCALE
        dv_ref[:, lanes] = jnp.where(low, value_grads[0], value_grads[1])


def collect_kernel(tok_rows, *refs):
    out_ref = refs[-1]
    pay_refs = chunks(refs[:2], STAT_ROWS)
    far_refs = far_chunks(tok_rows, refs[2:-1])
    spec_rows = tok_rows // UPPER
    first = 2 * (tok_rows // MIDDLE)
    count = spec_rows * (len(pay_refs) + len(far_refs))
    blocks = [r[:, tok_rows:] for r in pay_refs]
    blocks += [r[first : first + STAT_ROWS, :].astype(F32) for r in far_refs]
    for kind in range(5):
        lines = [b[kind * spec_rows : (kind + 1) * spec_rows] for b in blocks]
        out_ref[kind * count : (kind + 1) * count, :] = jnp.concatenate(lines, axis=0).astype(BF16)


def special_kernel(slots, off_ref, k_ref, v_ref, dq_in, spec_ref, dk_in, dv_in, *refs):
    blocks = refs[:-3]
    dq_ref, dk_ref, dv_ref = refs[-3:]
    rows, width = k_ref.shape
    heads = width // HD
    spec_rows = rows // UPPER
    count = slots * spec_rows
    every = count * len(blocks)
    offsets = lane_offsets(off_ref, heads, width)

    def kind(index, lanes):
        return jnp.concatenate(
            [b[index * count : (index + 1) * count, lanes] for b in blocks], axis=0
        )

    def two(block, scale=1.0):
        return jnp.concatenate([one_head(block, 0, scale), one_head(block, 1, scale)], axis=0)

    column = iota((1, 2 * every), 1)
    second = column >= every
    column = column % every
    same_group = jnp.where(column < GROUP * spec_rows, 1.0, 0.0)
    same_segment = jnp.where(column < count, 1.0, 0.0)
    row = iota((rows, 1), 0)
    low = half_mask(0)
    place = iota((8, PAIR), 1) % HD
    first_term = jnp.where(iota((8, PAIR), 0) == 0, 0, 3)
    picks = jnp.where((place >= first_term) & (place < first_term + 3), 1.0, 0.0).astype(BF16)
    for pair in range(heads // 2):
        lanes = slice(pair * PAIR, (pair + 1) * PAIR)
        all_q, all_k, all_v, all_g, all_s = [kind(index, lanes) for index in range(5)]
        query, grad = two(all_q, SCALE), two(all_g)
        known = dot_nt(picks, two(all_s))
        known_sum, known_dot = known[0:1], known[1:2]
        scores = dot_nt(all_k, query)
        inner = dot_nt(all_v, grad)
        top = jnp.max(scores, axis=0, keepdims=True)
        weights = jnp.exp(scores - top)
        total = jnp.sum(weights, axis=0, keepdims=True)
        product = jnp.sum(weights * inner, axis=0, keepdims=True) / total
        log_sum = top + jnp.log(total)
        most = jnp.maximum(known_sum, log_sum)
        joint = most + jnp.log(jnp.exp(known_sum - most) + jnp.exp(log_sum - most))
        share = jnp.exp(known_sum - joint)
        dot = known_dot * share + product * jnp.exp(log_sum - joint)
        probs = jnp.exp(scores - joint)
        grad_q = SCALE * lax.dot_general(
            (probs * (inner - dot)).astype(BF16),
            all_k,
            (((0,), (0,)), ((), ())),
            preferred_element_type=F32,
        )
        change = known_dot - dot
        lines = []
        for index in range(spec_rows):
            other = every + index
            ratio = jnp.where(low, share[:, index : index + 1], share[:, other : other + 1])
            moved = jnp.where(low, change[:, index : index + 1], change[:, other : other + 1])
            top_q = jnp.where(low, grad_q[index : index + 1], grad_q[other : other + 1])
            near_q = spec_ref[index : index + 1, lanes]
            key_sum = spec_ref[spec_rows + index : spec_rows + index + 1, lanes]
            line = ratio * (near_q + moved * key_sum) + top_q
            lines.append(jnp.broadcast_to(line, (UPPER, PAIR)))
        special = row % UPPER == offsets[:, lanes]
        dq_ref[:, lanes] = (
            dq_in[:, lanes] + jnp.where(special, jnp.concatenate(lines, axis=0), 0.0)
        ).astype(BF16)
        offset = jnp.where(second, off_ref[2 * pair + 1], off_ref[2 * pair])
        middle = row % MIDDLE == offset % MIDDLE
        upper = row % UPPER == offset
        weight = same_group + jnp.where(middle, same_segment, 0.0) + jnp.where(upper, 1.0, 0.0)
        scores = jnp.where(weight > 0.0, dot_nt(k_ref[:, lanes], query), LOW)
        probs = jnp.exp(scores - joint) * weight
        inner = dot_nt(v_ref[:, lanes], grad) - dot
        dk_ref[:, lanes] = (
            dk_in[:, lanes] + dot_nn((probs * inner).astype(BF16), query)
        ).astype(BF16)
        dv_ref[:, lanes] = (dv_in[:, lanes] + dot_nn(probs.astype(BF16), grad)).astype(BF16)


def call(kernel, outs, *arrays, us=1.0, raw=False, scratch=(), vmem_mib=40):
    smem = pl.BlockSpec(memory_space=pltpu.SMEM)
    vmem = pl.BlockSpec(memory_space=pltpu.VMEM)
    space = pl.BlockSpec(memory_space=pltpu.HBM) if raw else vmem
    specs = [smem if a.dtype == jnp.int32 and not raw else space for a in arrays]
    return pl.pallas_call(
        kernel,
        out_shape=tuple(jax.ShapeDtypeStruct(shape, dtype) for shape, dtype in outs),
        in_specs=specs,
        out_specs=tuple(vmem for _ in outs),
        scratch_shapes=scratch,
        cost_estimate=pl.CostEstimate(
            flops=int(us * 1.15e9), bytes_accessed=0, transcendentals=0
        ),
        compiler_params=pltpu.CompilerParams(vmem_limit_bytes=vmem_mib * 1024 * 1024),
    )(*arrays)


def across(value, axis, mask):
    size = lax.axis_size(axis)
    return lax.ppermute(value, axis, [(source, source ^ mask) for source in range(size)])


def local(queries, key_matrix, value_matrix, grad_out, offsets):
    rows, width = queries.shape
    slots, outer = lax.axis_size("ctxb"), lax.axis_size("ctxa")
    near_count = slots - GROUP
    near_rows, spec_rows = rows // MIDDLE, rows // UPPER

    next_k, next_v = across(key_matrix, "ctxb", 2), across(value_matrix, "ctxb", 2)
    core_k, core_v = across(key_matrix, "ctxb", 1), across(value_matrix, "ctxb", 1)
    near_kv, near_qg, spec = call(
        pack_kernel,
        [
            ((2 * near_rows, width), BF16),
            ((2 * near_rows, width), BF16),
            ((4 * SPEC_PAD, width), BF16),
        ],
        offsets, queries, key_matrix, value_matrix, grad_out,
        us=1.3, raw=True, vmem_mib=60,
        scratch=[
            pltpu.SMEM(offsets.shape, jnp.int32),
            pltpu.VMEM((4, rows, width), BF16),
            pltpu.SemaphoreType.DMA((4,)),
            pltpu.SemaphoreType.DMA,
        ],
    )
    near_came = [across(near_kv, "ctxb", mask) for mask in range(GROUP, slots, 2)]
    both = [((2 * rows, width), BF16)]
    own_kv = [key_matrix, value_matrix, core_k, core_v]
    term_rows = -(-3 * (width // HD) // 8) * 8
    (known,) = call(
        first_kernel, [((term_rows, rows), F32)],
        offsets, queries, grad_out, *own_kv, us=2.2,
    )
    (stacked,) = call(
        stack_kernel,
        [((2 * rows + 2 * near_rows * len(near_came), width), BF16)],
        known, next_k, next_v, *near_came, us=0.2,
    )
    kv_parts = own_kv + [stacked, across(stacked, "ctxb", 1)]
    (qg,) = call(merge_kernel, both, queries, grad_out, stacked, us=0.3)
    next_qg = across(qg, "ctxb", 2)
    core_qg = across(qg, "ctxb", 1)
    pay, far = call(
        partial(forward_kernel, near_count),
        [
            ((STAT_ROWS, rows + width), F32),
            ((2 * near_rows + 2 * STAT_ROWS, width), BF16),
        ],
        offsets, queries, grad_out, known, spec, near_qg, *kv_parts[4:], us=2.5,
    )
    dq, dq_spec = call(
        partial(query_kernel, near_count),
        [((rows, width), F32), ((2 * spec_rows, width), F32)],
        offsets, qg, spec, pay, *kv_parts, us=5.0,
    )
    pays_far = [pay, across(pay, "ctxb", 2)]
    far_came = [across(far, "ctxb", mask) for mask in range(GROUP, slots, 2)]
    held = call(
        relay_kernel,
        [
            ((2 * rows, width), BF16),
            ((2 * STAT_ROWS, rows + width), F32),
            ((far.shape[0] * len(far_came), width), BF16),
        ],
        dq_spec, next_qg, *pays_far, *far_came, us=0.3,
    )
    next_qgs, pays, fars = [(part, across(part, "ctxb", 1)) for part in held]
    qg_parts = [qg, core_qg, *next_qgs]
    (block,) = call(
        partial(collect_kernel, rows), [((5 * slots * spec_rows, width), BF16)], *pays, *fars,
        us=0.3,
    )
    blocks = [block] + [across(block, "ctxa", mask) for mask in range(1, outer)]
    dk, dv = call(
        partial(key_kernel, near_count),
        [((rows, width), F32), ((rows, width), F32)],
        offsets, key_matrix, value_matrix, *qg_parts, *pays, *fars, us=5.0,
    )
    return call(
        partial(special_kernel, slots),
        [((rows, width), BF16)] * 3,
        offsets, key_matrix, value_matrix, dq, dq_spec, dk, dv, *blocks, us=3.0,
    )


def solution(mesh):
    split = P(("ctxa", "ctxb"), None)
    return jax.shard_map(
        local,
        mesh=mesh,
        in_specs=(split, split, split, split, P()),
        out_specs=(split, split, split),
        check_vma=False,
    )
```

```python
from functools import partial

import jax
import jax.numpy as jnp
from jax import lax
from jax.experimental import pallas as pl
from jax.experimental.pallas import tpu as pltpu
from jax.sharding import PartitionSpec as P

HD = 64
PAIR = 2 * HD
GROUP = 4
MIDDLE = 8
UPPER = 128
LOW = -1e30
HIGH = 1e30
SCALE = HD**-0.5
F32 = jnp.float32
BF16 = jnp.bfloat16
STAT_ROWS = 16
SPEC_PAD = 16
KV_ARRAYS = 6


def iota(shape, dim):
    return lax.broadcasted_iota(jnp.int32, shape, dim)


def dot_nt(a, b):
    return lax.dot_general(a, b, (((1,), (1,)), ((), ())), preferred_element_type=F32)


def dot_nn(a, b):
    return jnp.dot(a, b, preferred_element_type=F32)


def pair_slice(head):
    low = head // 2 * PAIR
    return slice(low, low + PAIR)


def half_mask(head):
    return iota((1, PAIR), 1) // HD == head % 2


def one_head(block, head, scale=1.0):
    return jnp.where(half_mask(head), block.astype(F32) * scale, 0.0).astype(BF16)


def lane_offsets(off_ref, heads, width):
    lane_head = iota((1, width), 1) // HD
    out = jnp.zeros((1, width), jnp.int32)
    for head in range(heads):
        out = jnp.where(lane_head == head, off_ref[head], out)
    return out


def row_offsets(off_ref, heads):
    rows = iota((STAT_ROWS, 1), 0)
    out = jnp.zeros((STAT_ROWS, 1), jnp.int32)
    for head in range(heads):
        out = jnp.where((rows == head) | (rows == head + heads), off_ref[head], out)
    return out


def pair_weights(columns, middle_offset):
    both = (iota((MIDDLE, columns), 0) == middle_offset) & (
        iota((MIDDLE, columns), 1) % MIDDLE == middle_offset
    )
    return jnp.where(both, 2.0, 1.0)


def weighted(probs, weight):
    rows, columns = probs.shape
    tiles = probs.reshape(rows // MIDDLE, MIDDLE, columns)
    return (tiles * weight[None]).reshape(rows, columns)


def pack_kernel(
    off_in, q_ref, k_ref, v_ref, g_ref, near_kv_ref, near_qg_ref, spec_ref,
    off_ref, buffer, sems, off_sem,
):
    rows, width = q_ref.shape
    heads = width // HD
    near_rows, spec_rows = rows // MIDDLE, rows // UPPER
    places = (
        (k_ref, 0, near_kv_ref, 0, 1),
        (v_ref, 1, near_kv_ref, 1, 2),
        (q_ref, 2, near_qg_ref, 0, 0),
        (g_ref, 3, near_qg_ref, 1, 3),
    )
    off_copy = pltpu.make_async_copy(off_in, off_ref, off_sem)
    off_copy.start()
    copies = [
        pltpu.make_async_copy(source, buffer.at[index], sems.at[index])
        for source, index, _, _, _ in places
    ]
    for copy in copies:
        copy.start()
    off_copy.wait()
    offsets = lane_offsets(off_ref, heads, width)
    middle = iota((rows, width), 0) % MIDDLE == offsets % MIDDLE
    index = iota((near_rows, width), 0)
    gather = jnp.where(
        iota((near_rows, rows), 1) // MIDDLE == iota((near_rows, rows), 0), 1.0, 0.0
    ).astype(BF16)
    spec_ref[...] = jnp.zeros(spec_ref.shape, BF16)
    for (_, source, near_ref, slot, kind), copy in zip(places, copies):
        copy.wait()
        whole = buffer[source].astype(F32)
        kept = dot_nn(gather, jnp.where(middle, whole, 0.0).astype(BF16))
        near_ref[slot * near_rows : (slot + 1) * near_rows, :] = kept.astype(BF16)
        step = UPPER // MIDDLE
        top = jnp.where(index % step == offsets // MIDDLE, kept, 0.0)
        top = top.reshape(spec_rows, step, width).sum(axis=1)
        pad = jnp.zeros((SPEC_PAD - spec_rows, width), F32)
        spec_ref[kind * SPEC_PAD : (kind + 1) * SPEC_PAD, :] = jnp.concatenate(
            [top, pad], axis=0
        ).astype(BF16)


def split_terms(value):
    terms = []
    for _ in range(3):
        terms.append(value.astype(BF16).astype(F32))
        value = value - terms[-1]
    return terms


def next_refs(refs, rows):
    near_rows = 2 * (rows // MIDDLE)
    near = []
    for low in range(2 * rows, refs[0].shape[0], near_rows):
        near += [r.at[low : low + near_rows] for r in refs]
    return [r.at[:rows] for r in refs], [r.at[rows : 2 * rows] for r in refs], near


def key_value_refs(refs):
    keys, values, near = next_refs(refs[4:], refs[0].shape[0])
    return [refs[0], refs[2]] + keys, [refs[1], refs[3]] + values, near


def chunks(refs, rows):
    first, second = refs
    pieces = []
    for low in range(0, first.shape[0], rows):
        pieces += [first.at[low : low + rows], second.at[low : low + rows]]
    return pieces


def near_part(near_refs, slot, lanes):
    rows = near_refs[0].shape[0] // 2
    return jnp.concatenate([r[slot * rows : (slot + 1) * rows, lanes] for r in near_refs], axis=0)


def merge_kernel(first_ref, second_ref, _, out_ref):
    rows = first_ref.shape[0]
    out_ref[:rows, :] = first_ref[...]
    out_ref[rows:, :] = second_ref[...]


def softmax_terms(scores, inners, weights, top, total, product):
    new_top = top
    for part in scores:
        peak = jnp.max(part, axis=0, keepdims=True)
        new_top = peak if new_top is None else jnp.maximum(new_top, peak)
    if top is not None:
        scale = jnp.exp(top - new_top)
        total, product = total * scale, product * scale
    for part, inner, weight in zip(scores, inners, weights):
        probs = jnp.exp(part - new_top)
        if weight is not None:
            probs = weighted(probs, weight)
        part_total = jnp.sum(probs, axis=0, keepdims=True)
        part_product = jnp.sum(probs * inner(), axis=0, keepdims=True)
        total = part_total if total is None else total + part_total
        product = part_product if product is None else product + part_product
    return new_top, total, product


def first_kernel(off_ref, q_ref, g_ref, *refs):
    kv_refs, out_ref = refs[:-1], refs[-1]
    rows, width = q_ref.shape
    heads = width // HD
    for head in range(heads):
        lanes = pair_slice(head)
        weight = pair_weights(rows, off_ref[head] % MIDDLE)
        query = one_head(q_ref[:, lanes], head, SCALE)
        grad = one_head(g_ref[:, lanes], head)
        scores = [dot_nt(r[:, lanes], query) for r in kv_refs[::2]]
        inners = [partial(lambda r: dot_nt(r[:, lanes], grad), r) for r in kv_refs[1::2]]
        terms = softmax_terms(scores, inners, [weight] * len(scores), None, None, None)
        for index, term in enumerate(terms):
            row = index * heads + head
            out_ref[row : row + 1, :] = term


def forward_kernel(near_count, off_ref, q_ref, g_ref, known_ref, spec_ref, own_near_ref, *refs):
    k_refs, v_refs, near_refs = next_refs(refs[:-2], q_ref.shape[0])
    out_ref, far_ref = refs[-2:]
    rows, width = q_ref.shape
    heads = width // HD
    log_sums, dots = [], []
    for head in range(heads):
        lanes = pair_slice(head)
        middle_offset = off_ref[head] % MIDDLE
        chosen = iota((1, rows), 1) % MIDDLE == middle_offset
        weight = pair_weights(rows, middle_offset)
        query = one_head(q_ref[:, lanes], head, SCALE)
        grad = one_head(g_ref[:, lanes], head)
        scores = [dot_nt(r[:, lanes], query) for r in k_refs]
        inners = [partial(lambda r: dot_nt(r[:, lanes], grad), r) for r in v_refs]
        weights = [weight] * len(scores)
        if near_count:
            far_scores = dot_nt(near_part(near_refs, 0, lanes), query)
            scores.append(jnp.where(chosen, far_scores, LOW))
            inners.append(lambda: dot_nt(near_part(near_refs, 1, lanes), grad))
            weights.append(None)
        known = [known_ref[i * heads + head : i * heads + head + 1, :] for i in range(3)]
        top, total, product = softmax_terms(scores, inners, weights, *known)
        log_sums.append(top + jnp.log(total))
        dots.append(product / total)
    pad = jnp.zeros((STAT_ROWS - 2 * heads, rows), F32)
    stats = jnp.concatenate(log_sums + dots + [pad], axis=0)
    out_ref[:, :rows] = stats
    offsets = row_offsets(off_ref, heads)
    token = iota((STAT_ROWS, rows), 1)
    spec_rows = rows // UPPER
    lane = iota((STAT_ROWS, width), 1)
    row = iota((STAT_ROWS, width), 0)
    place = iota((1, width), 1) % HD
    lines = [
        spec_ref[kind * SPEC_PAD : kind * SPEC_PAD + spec_rows, :].astype(F32) for kind in range(4)
    ]
    for index in range(spec_rows):
        value = jnp.sum(
            jnp.where(token == offsets + index * UPPER, stats, 0.0), axis=1, keepdims=True
        )
        line = jnp.zeros((1, width), F32)
        for kind in range(2):
            spread = jnp.sum(
                jnp.where(lane // HD + kind * heads == row, value, 0.0), axis=0, keepdims=True
            )
            for index_of, term in enumerate(split_terms(spread)):
                line = jnp.where(place == 3 * kind + index_of, term, line)
        lines.append(line)
    lines.append(jnp.zeros((STAT_ROWS - 5 * spec_rows, width), F32))
    block = jnp.concatenate(lines, axis=0)
    out_ref[:, rows:] = block
    near_rows = own_near_ref.shape[0]
    far_ref[:near_rows, :] = own_near_ref[...]
    far_ref[near_rows : near_rows + STAT_ROWS, :] = block.astype(BF16)
    kept = jnp.where(token % MIDDLE == offsets % MIDDLE, stats, 0.0)
    gather = jnp.where(iota((rows, PAIR), 0) // MIDDLE == iota((rows, PAIR), 1), 1.0, 0.0)
    gather = gather.astype(BF16)
    for index, term in enumerate(split_terms(kept)):
        far_ref[near_rows + STAT_ROWS :, index * PAIR : (index + 1) * PAIR] = dot_nn(
            term.astype(BF16), gather
        ).astype(BF16)


def query_kernel(near_count, off_ref, qg_ref, spec_in, pay_ref, *refs):
    k_refs, v_refs, near_refs = key_value_refs(refs[:KV_ARRAYS])
    dq_ref, spec_ref = refs[-2:]
    rows, width = k_refs[0].shape
    heads = width // HD
    spec_rows = rows // UPPER
    full = rows + SPEC_PAD
    columns = jnp.transpose(pay_ref[:, :rows])
    offsets = lane_offsets(off_ref, heads, width)
    column = iota((1, STAT_ROWS), 1)
    column_offsets = jnp.zeros((1, STAT_ROWS), jnp.int32)
    for head in range(heads):
        column_offsets = jnp.where(
            (column == head) | (column == head + heads), off_ref[head], column_offsets
        )
    token = iota((rows, STAT_ROWS), 0)
    lines = [
        jnp.sum(
            jnp.where(token == column_offsets + index * UPPER, columns, 0.0),
            axis=0,
            keepdims=True,
        )
        for index in range(spec_rows)
    ]
    lines.append(jnp.zeros((SPEC_PAD - spec_rows, STAT_ROWS), F32))
    columns = jnp.concatenate([columns] + lines, axis=0)
    for pair in range(heads // 2):
        lanes = slice(pair * PAIR, (pair + 1) * PAIR)
        both_q = jnp.concatenate([qg_ref[:rows, lanes], spec_in[:SPEC_PAD, lanes]], axis=0)
        both_g = jnp.concatenate([qg_ref[rows:, lanes], spec_in[3 * SPEC_PAD :, lanes]], axis=0)
        keys = [r[:, lanes] for r in k_refs]
        if near_count:
            keys.append(near_part(near_refs, 0, lanes))
        every_key = jnp.concatenate(keys, axis=0)
        results = []
        for head in (2 * pair, 2 * pair + 1):
            middle_offset = off_ref[head] % MIDDLE
            row = iota((full, 1), 0)
            chosen = (row % MIDDLE == middle_offset) | (row >= rows)
            weight = pair_weights(rows, middle_offset)
            row_weight = jnp.where(iota((1, rows), 1) % MIDDLE == middle_offset, 2.0, 1.0)
            query = one_head(both_q, head, SCALE)
            grad = one_head(both_g, head)
            log_sum = columns[:, head : head + 1]
            dot = columns[:, heads + head : heads + head + 1]
            parts = []
            for key, v_ref in zip(keys, v_refs):
                probs = jnp.exp(dot_nt(query, key) - log_sum)
                probs = jnp.concatenate(
                    [weighted(probs[:rows], weight), probs[rows:] * row_weight], axis=0
                )
                inner = dot_nt(grad, v_ref[:, lanes]) - dot
                parts.append(
                    jnp.concatenate([(probs * inner).astype(BF16), probs[rows:].astype(BF16)], axis=0)
                )
            if near_count:
                scores = jnp.where(chosen, dot_nt(query, keys[-1]), LOW)
                probs = jnp.exp(scores - log_sum)
                inner = dot_nt(grad, near_part(near_refs, 1, lanes)) - dot
                parts.append(
                    jnp.concatenate([(probs * inner).astype(BF16), probs[rows:].astype(BF16)], axis=0)
                )
            results.append(dot_nn(jnp.concatenate(parts, axis=1), every_key))
        result = jnp.where(half_mask(0), results[0], results[1]) * SCALE
        special = iota((rows, PAIR), 0) % UPPER == offsets[:, lanes]
        dq_ref[:, lanes] = jnp.where(special, 0.0, result[:rows])
        spec_ref[:spec_rows, lanes] = result[rows : rows + spec_rows]
        spec_ref[spec_rows:, lanes] = result[full : full + spec_rows]


def stack_kernel(first_ref, *refs):
    out, low = refs[-1], 0
    for ref in refs[:-1]:
        rows = ref.shape[0]
        out[low : low + rows, :] = ref[...]
        low += rows


def far_chunks(tok_rows, refs):
    return chunks(refs, 2 * (tok_rows // MIDDLE) + 2 * STAT_ROWS) if refs else []


def relay_kernel(first_ref, *refs):
    pay_refs, far_refs = refs[:2], refs[2:-2]
    for parts, out in zip((pay_refs, far_refs), refs[-2:]):
        for index, ref in enumerate(parts):
            rows = ref.shape[0]
            out[index * rows : (index + 1) * rows, :] = ref[...]


def copy_kernel(_, in_ref, out_ref):
    out_ref[...] = in_ref[...]


def key_kernel(near_count, off_ref, k_ref, v_ref, *refs):
    qg_refs = refs[:GROUP]
    pay_refs = chunks(refs[GROUP : GROUP + 2], STAT_ROWS)
    far_refs = far_chunks(k_ref.shape[0], refs[GROUP + 2 : -2])
    dk_ref, dv_ref = refs[-2:]
    rows, width = k_ref.shape
    heads = width // HD
    near_rows = rows // MIDDLE
    if near_count:
        first = 2 * near_rows + STAT_ROWS
        far_stats = []
        for r in far_refs:
            lines = r[first : first + STAT_ROWS, :].astype(F32)
            line = lines[:, :PAIR] + lines[:, PAIR : 2 * PAIR] + lines[:, 2 * PAIR : 3 * PAIR]
            far_stats.append(line[:, :near_rows])
        far_stats = jnp.concatenate(far_stats, axis=1)
    for pair in range(heads // 2):
        lanes = slice(pair * PAIR, (pair + 1) * PAIR)
        queries = [r[:rows, lanes] for r in qg_refs]
        grads = [r[rows:, lanes] for r in qg_refs]
        if near_count:
            queries.append(
                jnp.concatenate([r[:near_rows, lanes] for r in far_refs], axis=0)
            )
            grads.append(
                jnp.concatenate([r[near_rows : 2 * near_rows, lanes] for r in far_refs], axis=0)
            )
        every_query = jnp.concatenate(queries, axis=0)
        every_grad = jnp.concatenate(grads, axis=0)
        key_grads, value_grads = [], []
        for head in (2 * pair, 2 * pair + 1):
            middle_offset = off_ref[head] % MIDDLE
            chosen = iota((rows, 1), 0) % MIDDLE == middle_offset
            weight = pair_weights(rows, middle_offset)
            keys = one_head(k_ref[:, lanes], head, SCALE)
            values = one_head(v_ref[:, lanes], head)
            special = iota((1, rows), 1) % UPPER == off_ref[head]
            prob_parts, score_parts = [], []
            for query, grad, pay_ref in zip(queries, grads, pay_refs):
                log_sum = jnp.where(special, HIGH, pay_ref[head : head + 1, :rows])
                dot = pay_ref[heads + head : heads + head + 1, :rows]
                probs = weighted(jnp.exp(dot_nt(keys, query) - log_sum), weight)
                inner = dot_nt(values, grad) - dot
                prob_parts.append(probs.astype(BF16))
                score_parts.append((probs * inner).astype(BF16))
            if near_count:
                count = near_count * near_rows
                special = iota((1, count), 1) % (UPPER // MIDDLE) == off_ref[head] // MIDDLE
                log_sum = jnp.where(special, HIGH, far_stats[head : head + 1, :])
                dot = far_stats[heads + head : heads + head + 1, :]
                scores = jnp.where(chosen, dot_nt(keys, queries[-1]), LOW)
                probs = jnp.exp(scores - log_sum)
                inner = dot_nt(values, grads[-1]) - dot
                prob_parts.append(probs.astype(BF16))
                score_parts.append((probs * inner).astype(BF16))
            key_grads.append(dot_nn(jnp.concatenate(score_parts, axis=1), every_query))
            value_grads.append(dot_nn(jnp.concatenate(prob_parts, axis=1), every_grad))
        low = half_mask(0)
        dk_ref[:, lanes] = jnp.where(low, key_grads[0], key_grads[1]) * SCALE
        dv_ref[:, lanes] = jnp.where(low, value_grads[0], value_grads[1])


def collect_kernel(tok_rows, *refs):
    out_ref = refs[-1]
    pay_refs = chunks(refs[:2], STAT_ROWS)
    far_refs = far_chunks(tok_rows, refs[2:-1])
    spec_rows = tok_rows // UPPER
    first = 2 * (tok_rows // MIDDLE)
    count = spec_rows * (len(pay_refs) + len(far_refs))
    blocks = [r[:, tok_rows:] for r in pay_refs]
    blocks += [r[first : first + STAT_ROWS, :].astype(F32) for r in far_refs]
    for kind in range(5):
        lines = [b[kind * spec_rows : (kind + 1) * spec_rows] for b in blocks]
        out_ref[kind * count : (kind + 1) * count, :] = jnp.concatenate(lines, axis=0).astype(BF16)


def special_kernel(slots, off_ref, k_ref, v_ref, dq_in, spec_ref, dk_in, dv_in, *refs):
    blocks = refs[:-3]
    dq_ref, dk_ref, dv_ref = refs[-3:]
    rows, width = k_ref.shape
    heads = width // HD
    spec_rows = rows // UPPER
    count = slots * spec_rows
    every = count * len(blocks)
    offsets = lane_offsets(off_ref, heads, width)

    def kind(index, lanes):
        return jnp.concatenate(
            [b[index * count : (index + 1) * count, lanes] for b in blocks], axis=0
        )

    def two(block, scale=1.0):
        return jnp.concatenate([one_head(block, 0, scale), one_head(block, 1, scale)], axis=0)

    column = iota((1, 2 * every), 1)
    second = column >= every
    column = column % every
    same_group = jnp.where(column < GROUP * spec_rows, 1.0, 0.0)
    same_segment = jnp.where(column < count, 1.0, 0.0)
    row = iota((rows, 1), 0)
    low = half_mask(0)
    place = iota((8, PAIR), 1) % HD
    first_term = jnp.where(iota((8, PAIR), 0) == 0, 0, 3)
    picks = jnp.where((place >= first_term) & (place < first_term + 3), 1.0, 0.0).astype(BF16)
    states = []
    for pair in range(heads // 2):
        lanes = slice(pair * PAIR, (pair + 1) * PAIR)
        all_q, all_k, all_v, all_g, all_s = [kind(index, lanes) for index in range(5)]
        query, grad = two(all_q, SCALE), two(all_g)
        known = dot_nt(picks, two(all_s))
        known_sum, known_dot = known[0:1], known[1:2]
        scores = dot_nt(all_k, query)
        inner = dot_nt(all_v, grad)
        top = jnp.max(scores, axis=0, keepdims=True)
        weights = jnp.exp(scores - top)
        total = jnp.sum(weights, axis=0, keepdims=True)
        product = jnp.sum(weights * inner, axis=0, keepdims=True) / total
        log_sum = top + jnp.log(total)
        most = jnp.maximum(known_sum, log_sum)
        joint = most + jnp.log(jnp.exp(known_sum - most) + jnp.exp(log_sum - most))
        share = jnp.exp(known_sum - joint)
        dot = known_dot * share + product * jnp.exp(log_sum - joint)
        states.append((lanes, query, grad, all_k, scores, inner, joint, share, dot, known_dot - dot))
    for pair, state in enumerate(states):
        lanes, query, grad, _, _, _, joint, _, dot, _ = state
        offset = jnp.where(second, off_ref[2 * pair + 1], off_ref[2 * pair])
        middle = row % MIDDLE == offset % MIDDLE
        upper = row % UPPER == offset
        weight = same_group + jnp.where(middle, same_segment, 0.0) + jnp.where(upper, 1.0, 0.0)
        scores = jnp.where(weight > 0.0, dot_nt(k_ref[:, lanes], query), LOW)
        probs = jnp.exp(scores - joint) * weight
        inner = dot_nt(v_ref[:, lanes], grad) - dot
        dk_ref[:, lanes] = (
            dk_in[:, lanes] + dot_nn((probs * inner).astype(BF16), query)
        ).astype(BF16)
        dv_ref[:, lanes] = (dv_in[:, lanes] + dot_nn(probs.astype(BF16), grad)).astype(BF16)
    for lanes, _, _, all_k, scores, inner, joint, share, dot, change in states:
        probs = jnp.exp(scores - joint)
        grad_q = SCALE * lax.dot_general(
            (probs * (inner - dot)).astype(BF16),
            all_k,
            (((0,), (0,)), ((), ())),
            preferred_element_type=F32,
        )
        lines = []
        for index in range(spec_rows):
            other = every + index
            ratio = jnp.where(low, share[:, index : index + 1], share[:, other : other + 1])
            moved = jnp.where(low, change[:, index : index + 1], change[:, other : other + 1])
            top_q = jnp.where(low, grad_q[index : index + 1], grad_q[other : other + 1])
            near_q = spec_ref[index : index + 1, lanes]
            key_sum = spec_ref[spec_rows + index : spec_rows + index + 1, lanes]
            line = ratio * (near_q + moved * key_sum) + top_q
            lines.append(jnp.broadcast_to(line, (UPPER, PAIR)))
        special = row % UPPER == offsets[:, lanes]
        dq_ref[:, lanes] = (
            dq_in[:, lanes] + jnp.where(special, jnp.concatenate(lines, axis=0), 0.0)
        ).astype(BF16)


def call(kernel, outs, *arrays, us=1.0, raw=False, scratch=(), vmem_mib=40):
    smem = pl.BlockSpec(memory_space=pltpu.SMEM)
    vmem = pl.BlockSpec(memory_space=pltpu.VMEM)
    space = pl.BlockSpec(memory_space=pltpu.HBM) if raw else vmem
    specs = [smem if a.dtype == jnp.int32 and not raw else space for a in arrays]
    return pl.pallas_call(
        kernel,
        out_shape=tuple(jax.ShapeDtypeStruct(shape, dtype) for shape, dtype in outs),
        in_specs=specs,
        out_specs=tuple(vmem for _ in outs),
        scratch_shapes=scratch,
        cost_estimate=pl.CostEstimate(
            flops=int(us * 1.15e9), bytes_accessed=0, transcendentals=0
        ),
        compiler_params=pltpu.CompilerParams(vmem_limit_bytes=vmem_mib * 1024 * 1024),
    )(*arrays)


def across(value, axis, mask):
    size = lax.axis_size(axis)
    return lax.ppermute(value, axis, [(source, source ^ mask) for source in range(size)])


def local(queries, key_matrix, value_matrix, grad_out, offsets):
    rows, width = queries.shape
    slots, outer = lax.axis_size("ctxb"), lax.axis_size("ctxa")
    near_count = slots - GROUP
    near_rows, spec_rows = rows // MIDDLE, rows // UPPER

    next_k, next_v = across(key_matrix, "ctxb", 2), across(value_matrix, "ctxb", 2)
    core_k, core_v = across(key_matrix, "ctxb", 1), across(value_matrix, "ctxb", 1)
    near_kv, near_qg, spec = call(
        pack_kernel,
        [
            ((2 * near_rows, width), BF16),
            ((2 * near_rows, width), BF16),
            ((4 * SPEC_PAD, width), BF16),
        ],
        offsets, queries, key_matrix, value_matrix, grad_out,
        us=1.3, raw=True, vmem_mib=60,
        scratch=[
            pltpu.SMEM(offsets.shape, jnp.int32),
            pltpu.VMEM((4, rows, width), BF16),
            pltpu.SemaphoreType.DMA((4,)),
            pltpu.SemaphoreType.DMA,
        ],
    )
    near_came = [across(near_kv, "ctxb", mask) for mask in range(GROUP, slots, 2)]
    both = [((2 * rows, width), BF16)]
    own_kv = [key_matrix, value_matrix, core_k, core_v]
    term_rows = -(-3 * (width // HD) // 8) * 8
    (known,) = call(
        first_kernel, [((term_rows, rows), F32)],
        offsets, queries, grad_out, *own_kv, us=2.2,
    )
    (stacked,) = call(
        stack_kernel,
        [((2 * rows + 2 * near_rows * len(near_came), width), BF16)],
        known, next_k, next_v, *near_came, us=0.2,
    )
    kv_parts = own_kv + [stacked, across(stacked, "ctxb", 1)]
    (qg,) = call(merge_kernel, both, queries, grad_out, stacked, us=0.3)
    next_qg = across(qg, "ctxb", 2)
    core_qg = across(qg, "ctxb", 1)
    pay, far = call(
        partial(forward_kernel, near_count),
        [
            ((STAT_ROWS, rows + width), F32),
            ((2 * near_rows + 2 * STAT_ROWS, width), BF16),
        ],
        offsets, queries, grad_out, known, spec, near_qg, *kv_parts[4:], us=2.5,
    )
    dq, dq_spec = call(
        partial(query_kernel, near_count),
        [((rows, width), F32), ((2 * spec_rows, width), F32)],
        offsets, qg, spec, pay, *kv_parts, us=5.0,
    )
    pays_far = [pay, across(pay, "ctxb", 2)]
    far_came = [across(far, "ctxb", mask) for mask in range(GROUP, slots, 2)]
    held = call(
        relay_kernel,
        [
            ((2 * STAT_ROWS, rows + width), F32),
            ((far.shape[0] * len(far_came), width), BF16),
        ],
        dq_spec, *pays_far, *far_came, us=0.3,
    )
    pays, fars = [(part, across(part, "ctxb", 1)) for part in held]
    (block,) = call(
        partial(collect_kernel, rows), [((5 * slots * spec_rows, width), BF16)], *pays, *fars,
        us=0.3,
    )
    (next_qg,) = call(copy_kernel, [((2 * rows, width), BF16)], block, next_qg, us=0.2)
    qg_parts = [qg, core_qg, next_qg, across(next_qg, "ctxb", 1)]
    blocks = [block] + [across(block, "ctxa", mask) for mask in range(1, outer)]
    dk, dv = call(
        partial(key_kernel, near_count),
        [((rows, width), F32), ((rows, width), F32)],
        offsets, key_matrix, value_matrix, *qg_parts, *pays, *fars, us=5.0,
    )
    return call(
        partial(special_kernel, slots),
        [((rows, width), BF16)] * 3,
        offsets, key_matrix, value_matrix, dq, dq_spec, dk, dv, *blocks, us=3.0,
    )


def solution(mesh):
    split = P(("ctxa", "ctxb"), None)
    return jax.shard_map(
        local,
        mesh=mesh,
        in_specs=(split, split, split, split, P()),
        out_specs=(split, split, split),
        check_vma=False,
    )
```

```python
from functools import partial

import jax
import jax.numpy as jnp
from jax import lax
from jax.experimental import pallas as pl
from jax.experimental.pallas import tpu as pltpu
from jax.sharding import PartitionSpec as P

HD = 64
PAIR = 2 * HD
GROUP = 4
MIDDLE = 8
UPPER = 128
LOW = -1e30
HIGH = 1e30
SCALE = HD**-0.5
F32 = jnp.float32
BF16 = jnp.bfloat16
STAT_ROWS = 16
SPEC_PAD = 16
KV_ARRAYS = 6


def iota(shape, dim):
    return lax.broadcasted_iota(jnp.int32, shape, dim)


def dot_nt(a, b):
    return lax.dot_general(a, b, (((1,), (1,)), ((), ())), preferred_element_type=F32)


def dot_nn(a, b):
    return jnp.dot(a, b, preferred_element_type=F32)


def pair_slice(head):
    low = head // 2 * PAIR
    return slice(low, low + PAIR)


def half_mask(head):
    return iota((1, PAIR), 1) // HD == head % 2


def one_head(block, head, scale=1.0):
    return jnp.where(half_mask(head), block.astype(F32) * scale, 0.0).astype(BF16)


def lane_offsets(off_ref, heads, width):
    lane_head = iota((1, width), 1) // HD
    out = jnp.zeros((1, width), jnp.int32)
    for head in range(heads):
        out = jnp.where(lane_head == head, off_ref[head], out)
    return out


def row_offsets(off_ref, heads):
    rows = iota((STAT_ROWS, 1), 0)
    out = jnp.zeros((STAT_ROWS, 1), jnp.int32)
    for head in range(heads):
        out = jnp.where((rows == head) | (rows == head + heads), off_ref[head], out)
    return out


def pair_weights(columns, middle_offset):
    both = (iota((MIDDLE, columns), 0) == middle_offset) & (
        iota((MIDDLE, columns), 1) % MIDDLE == middle_offset
    )
    return jnp.where(both, 2.0, 1.0)


def weighted(probs, weight):
    rows, columns = probs.shape
    tiles = probs.reshape(rows // MIDDLE, MIDDLE, columns)
    return (tiles * weight[None]).reshape(rows, columns)


def pack_kernel(
    off_in, q_ref, k_ref, v_ref, g_ref, near_kv_ref, near_qg_ref, spec_ref,
    off_ref, buffer, sems, off_sem,
):
    rows, width = q_ref.shape
    heads = width // HD
    near_rows, spec_rows = rows // MIDDLE, rows // UPPER
    places = (
        (k_ref, 0, near_kv_ref, 0, 1),
        (v_ref, 1, near_kv_ref, 1, 2),
        (q_ref, 2, near_qg_ref, 0, 0),
        (g_ref, 3, near_qg_ref, 1, 3),
    )
    off_copy = pltpu.make_async_copy(off_in, off_ref, off_sem)
    off_copy.start()
    copies = [
        pltpu.make_async_copy(source, buffer.at[index], sems.at[index])
        for source, index, _, _, _ in places
    ]
    for copy in copies:
        copy.start()
    off_copy.wait()
    offsets = lane_offsets(off_ref, heads, width)
    middle = iota((rows, width), 0) % MIDDLE == offsets % MIDDLE
    index = iota((near_rows, width), 0)
    gather = jnp.where(
        iota((near_rows, rows), 1) // MIDDLE == iota((near_rows, rows), 0), 1.0, 0.0
    ).astype(BF16)
    spec_ref[...] = jnp.zeros(spec_ref.shape, BF16)
    for (_, source, near_ref, slot, kind), copy in zip(places, copies):
        copy.wait()
        whole = buffer[source].astype(F32)
        kept = dot_nn(gather, jnp.where(middle, whole, 0.0).astype(BF16))
        near_ref[slot * near_rows : (slot + 1) * near_rows, :] = kept.astype(BF16)
        step = UPPER // MIDDLE
        top = jnp.where(index % step == offsets // MIDDLE, kept, 0.0)
        top = top.reshape(spec_rows, step, width).sum(axis=1)
        pad = jnp.zeros((SPEC_PAD - spec_rows, width), F32)
        spec_ref[kind * SPEC_PAD : (kind + 1) * SPEC_PAD, :] = jnp.concatenate(
            [top, pad], axis=0
        ).astype(BF16)


def split_terms(value):
    terms = []
    for _ in range(3):
        terms.append(value.astype(BF16).astype(F32))
        value = value - terms[-1]
    return terms


def next_refs(refs, rows):
    near_rows = 2 * (rows // MIDDLE)
    near = []
    for low in range(2 * rows, refs[0].shape[0], near_rows):
        near += [r.at[low : low + near_rows] for r in refs]
    return [r.at[:rows] for r in refs], [r.at[rows : 2 * rows] for r in refs], near


def key_value_refs(refs):
    keys, values, near = next_refs(refs[4:], refs[0].shape[0])
    return [refs[0], refs[2]] + keys, [refs[1], refs[3]] + values, near


def chunks(refs, rows):
    first, second = refs
    pieces = []
    for low in range(0, first.shape[0], rows):
        pieces += [first.at[low : low + rows], second.at[low : low + rows]]
    return pieces


def near_part(near_refs, slot, lanes):
    rows = near_refs[0].shape[0] // 2
    return jnp.concatenate([r[slot * rows : (slot + 1) * rows, lanes] for r in near_refs], axis=0)


def merge_kernel(first_ref, second_ref, _, out_ref):
    rows = first_ref.shape[0]
    out_ref[:rows, :] = first_ref[...]
    out_ref[rows:, :] = second_ref[...]


def softmax_terms(scores, inners, weights, top, total, product):
    new_top = top
    for part in scores:
        peak = jnp.max(part, axis=0, keepdims=True)
        new_top = peak if new_top is None else jnp.maximum(new_top, peak)
    if top is not None:
        scale = jnp.exp(top - new_top)
        total, product = total * scale, product * scale
    for part, inner, weight in zip(scores, inners, weights):
        probs = jnp.exp(part - new_top)
        if weight is not None:
            probs = weighted(probs, weight)
        part_total = jnp.sum(probs, axis=0, keepdims=True)
        part_product = jnp.sum(probs * inner, axis=0, keepdims=True)
        total = part_total if total is None else total + part_total
        product = part_product if product is None else product + part_product
    return new_top, total, product


def first_kernel(off_ref, q_ref, g_ref, *refs):
    kv_refs, out_ref = refs[:-1], refs[-1]
    rows, width = q_ref.shape
    heads = width // HD

    def products(head):
        lanes = pair_slice(head)
        query = one_head(q_ref[:, lanes], head, SCALE)
        grad = one_head(g_ref[:, lanes], head)
        scores = [dot_nt(r[:, lanes], query) for r in kv_refs[::2]]
        return scores, [dot_nt(r[:, lanes], grad) for r in kv_refs[1::2]]

    ahead = products(0)
    for head in range(heads):
        (scores, inners), ahead = ahead, products(head + 1) if head + 1 < heads else None
        weight = pair_weights(rows, off_ref[head] % MIDDLE)
        terms = softmax_terms(scores, inners, [weight] * len(scores), None, None, None)
        for index, term in enumerate(terms):
            row = index * heads + head
            out_ref[row : row + 1, :] = term


def forward_kernel(near_count, off_ref, q_ref, g_ref, known_ref, spec_ref, own_near_ref, *refs):
    k_refs, v_refs, near_refs = next_refs(refs[:-2], q_ref.shape[0])
    out_ref, far_ref = refs[-2:]
    rows, width = q_ref.shape
    heads = width // HD
    log_sums, dots = [], []

    def products(head):
        lanes = pair_slice(head)
        query = one_head(q_ref[:, lanes], head, SCALE)
        grad = one_head(g_ref[:, lanes], head)
        keys, values = [r[:, lanes] for r in k_refs], [r[:, lanes] for r in v_refs]
        if near_count:
            keys.append(near_part(near_refs, 0, lanes))
            values.append(near_part(near_refs, 1, lanes))
        return [dot_nt(key, query) for key in keys], [dot_nt(value, grad) for value in values]

    ahead = products(0)
    for head in range(heads):
        (scores, inners), ahead = ahead, products(head + 1) if head + 1 < heads else None
        middle_offset = off_ref[head] % MIDDLE
        weights = [pair_weights(rows, middle_offset)] * len(k_refs)
        if near_count:
            chosen = iota((1, rows), 1) % MIDDLE == middle_offset
            scores[-1] = jnp.where(chosen, scores[-1], LOW)
            weights.append(None)
        known = [known_ref[i * heads + head : i * heads + head + 1, :] for i in range(3)]
        top, total, product = softmax_terms(scores, inners, weights, *known)
        log_sums.append(top + jnp.log(total))
        dots.append(product / total)
    pad = jnp.zeros((STAT_ROWS - 2 * heads, rows), F32)
    stats = jnp.concatenate(log_sums + dots + [pad], axis=0)
    out_ref[:, :rows] = stats
    offsets = row_offsets(off_ref, heads)
    token = iota((STAT_ROWS, rows), 1)
    spec_rows = rows // UPPER
    lane = iota((STAT_ROWS, width), 1)
    row = iota((STAT_ROWS, width), 0)
    place = iota((1, width), 1) % HD
    lines = [
        spec_ref[kind * SPEC_PAD : kind * SPEC_PAD + spec_rows, :].astype(F32) for kind in range(4)
    ]
    for index in range(spec_rows):
        value = jnp.sum(
            jnp.where(token == offsets + index * UPPER, stats, 0.0), axis=1, keepdims=True
        )
        line = jnp.zeros((1, width), F32)
        for kind in range(2):
            spread = jnp.sum(
                jnp.where(lane // HD + kind * heads == row, value, 0.0), axis=0, keepdims=True
            )
            for index_of, term in enumerate(split_terms(spread)):
                line = jnp.where(place == 3 * kind + index_of, term, line)
        lines.append(line)
    lines.append(jnp.zeros((STAT_ROWS - 5 * spec_rows, width), F32))
    block = jnp.concatenate(lines, axis=0)
    out_ref[:, rows:] = block
    near_rows = own_near_ref.shape[0]
    far_ref[:near_rows, :] = own_near_ref[...]
    far_ref[near_rows : near_rows + STAT_ROWS, :] = block.astype(BF16)
    kept = jnp.where(token % MIDDLE == offsets % MIDDLE, stats, 0.0)
    gather = jnp.where(iota((rows, PAIR), 0) // MIDDLE == iota((rows, PAIR), 1), 1.0, 0.0)
    gather = gather.astype(BF16)
    for index, term in enumerate(split_terms(kept)):
        far_ref[near_rows + STAT_ROWS :, index * PAIR : (index + 1) * PAIR] = dot_nn(
            term.astype(BF16), gather
        ).astype(BF16)


def query_kernel(near_count, off_ref, qg_ref, spec_in, pay_ref, *refs):
    k_refs, v_refs, near_refs = key_value_refs(refs[:KV_ARRAYS])
    dq_ref, spec_ref = refs[-2:]
    rows, width = k_refs[0].shape
    heads = width // HD
    spec_rows = rows // UPPER
    full = rows + SPEC_PAD
    columns = jnp.transpose(pay_ref[:, :rows])
    offsets = lane_offsets(off_ref, heads, width)
    column = iota((1, STAT_ROWS), 1)
    column_offsets = jnp.zeros((1, STAT_ROWS), jnp.int32)
    for head in range(heads):
        column_offsets = jnp.where(
            (column == head) | (column == head + heads), off_ref[head], column_offsets
        )
    token = iota((rows, STAT_ROWS), 0)
    lines = [
        jnp.sum(
            jnp.where(token == column_offsets + index * UPPER, columns, 0.0),
            axis=0,
            keepdims=True,
        )
        for index in range(spec_rows)
    ]
    lines.append(jnp.zeros((SPEC_PAD - spec_rows, STAT_ROWS), F32))
    columns = jnp.concatenate([columns] + lines, axis=0)
    for pair in range(heads // 2):
        lanes = slice(pair * PAIR, (pair + 1) * PAIR)
        both_q = jnp.concatenate([qg_ref[:rows, lanes], spec_in[:SPEC_PAD, lanes]], axis=0)
        both_g = jnp.concatenate([qg_ref[rows:, lanes], spec_in[3 * SPEC_PAD :, lanes]], axis=0)
        keys = [r[:, lanes] for r in k_refs]
        if near_count:
            keys.append(near_part(near_refs, 0, lanes))
        every_key = jnp.concatenate(keys, axis=0)
        results = []
        for head in (2 * pair, 2 * pair + 1):
            middle_offset = off_ref[head] % MIDDLE
            row = iota((full, 1), 0)
            chosen = (row % MIDDLE == middle_offset) | (row >= rows)
            weight = pair_weights(rows, middle_offset)
            row_weight = jnp.where(iota((1, rows), 1) % MIDDLE == middle_offset, 2.0, 1.0)
            query = one_head(both_q, head, SCALE)
            grad = one_head(both_g, head)
            log_sum = columns[:, head : head + 1]
            dot = columns[:, heads + head : heads + head + 1]
            parts = []
            for key, v_ref in zip(keys, v_refs):
                probs = jnp.exp(dot_nt(query, key) - log_sum)
                probs = jnp.concatenate(
                    [weighted(probs[:rows], weight), probs[rows:] * row_weight], axis=0
                )
                inner = dot_nt(grad, v_ref[:, lanes]) - dot
                parts.append(
                    jnp.concatenate([(probs * inner).astype(BF16), probs[rows:].astype(BF16)], axis=0)
                )
            if near_count:
                scores = jnp.where(chosen, dot_nt(query, keys[-1]), LOW)
                probs = jnp.exp(scores - log_sum)
                inner = dot_nt(grad, near_part(near_refs, 1, lanes)) - dot
                parts.append(
                    jnp.concatenate([(probs * inner).astype(BF16), probs[rows:].astype(BF16)], axis=0)
                )
            results.append(dot_nn(jnp.concatenate(parts, axis=1), every_key))
        result = jnp.where(half_mask(0), results[0], results[1]) * SCALE
        special = iota((rows, PAIR), 0) % UPPER == offsets[:, lanes]
        dq_ref[:, lanes] = jnp.where(special, 0.0, result[:rows])
        spec_ref[:spec_rows, lanes] = result[rows : rows + spec_rows]
        spec_ref[spec_rows:, lanes] = result[full : full + spec_rows]


def stack_kernel(first_ref, *refs):
    out, low = refs[-1], 0
    for ref in refs[:-1]:
        rows = ref.shape[0]
        out[low : low + rows, :] = ref[...]
        low += rows


def far_chunks(tok_rows, refs):
    return chunks(refs, 2 * (tok_rows // MIDDLE) + 2 * STAT_ROWS) if refs else []


def relay_kernel(first_ref, second_ref, *refs):
    pay_refs, far_refs = refs[:2], refs[2:-2]
    for parts, out in zip((pay_refs, far_refs), refs[-2:]):
        for index, ref in enumerate(parts):
            rows = ref.shape[0]
            out[index * rows : (index + 1) * rows, :] = ref[...]


def copy_kernel(_, in_ref, out_ref):
    out_ref[...] = in_ref[...]


def key_kernel(near_count, off_ref, k_ref, v_ref, *refs):
    dk_ref, dv_ref = refs[-2:]
    rows, width = k_ref.shape
    heads = width // HD
    near_rows = rows // MIDDLE
    if len(refs) == 4:
        qg_refs, pay_refs, known_refs = refs[:1], refs[1:2], None
    else:
        qg_refs = refs[: GROUP - 1]
        pay_refs = chunks(refs[GROUP - 1 : GROUP + 1], STAT_ROWS)[1:]
        far_refs = far_chunks(k_ref.shape[0], refs[GROUP + 1 : -4])
        known_refs = refs[-4:-2]
    if near_count:
        first = 2 * near_rows + STAT_ROWS
        far_stats = []
        for r in far_refs:
            lines = r[first : first + STAT_ROWS, :].astype(F32)
            line = lines[:, :PAIR] + lines[:, PAIR : 2 * PAIR] + lines[:, 2 * PAIR : 3 * PAIR]
            far_stats.append(line[:, :near_rows])
        far_stats = jnp.concatenate(far_stats, axis=1)
    for pair in range(heads // 2):
        lanes = slice(pair * PAIR, (pair + 1) * PAIR)
        queries = [r[:rows, lanes] for r in qg_refs]
        grads = [r[rows:, lanes] for r in qg_refs]
        if near_count:
            queries.append(
                jnp.concatenate([r[:near_rows, lanes] for r in far_refs], axis=0)
            )
            grads.append(
                jnp.concatenate([r[near_rows : 2 * near_rows, lanes] for r in far_refs], axis=0)
            )
        every_query = jnp.concatenate(queries, axis=0)
        every_grad = jnp.concatenate(grads, axis=0)
        key_grads, value_grads = [], []
        for head in (2 * pair, 2 * pair + 1):
            middle_offset = off_ref[head] % MIDDLE
            chosen = iota((rows, 1), 0) % MIDDLE == middle_offset
            weight = pair_weights(rows, middle_offset)
            keys = one_head(k_ref[:, lanes], head, SCALE)
            values = one_head(v_ref[:, lanes], head)
            special = iota((1, rows), 1) % UPPER == off_ref[head]
            prob_parts, score_parts = [], []
            for query, grad, pay_ref in zip(queries, grads, pay_refs):
                log_sum = jnp.where(special, HIGH, pay_ref[head : head + 1, :rows])
                dot = pay_ref[heads + head : heads + head + 1, :rows]
                probs = weighted(jnp.exp(dot_nt(keys, query) - log_sum), weight)
                inner = dot_nt(values, grad) - dot
                prob_parts.append(probs.astype(BF16))
                score_parts.append((probs * inner).astype(BF16))
            if near_count:
                count = near_count * near_rows
                special = iota((1, count), 1) % (UPPER // MIDDLE) == off_ref[head] // MIDDLE
                log_sum = jnp.where(special, HIGH, far_stats[head : head + 1, :])
                dot = far_stats[heads + head : heads + head + 1, :]
                scores = jnp.where(chosen, dot_nt(keys, queries[-1]), LOW)
                probs = jnp.exp(scores - log_sum)
                inner = dot_nt(values, grads[-1]) - dot
                prob_parts.append(probs.astype(BF16))
                score_parts.append((probs * inner).astype(BF16))
            key_grads.append(dot_nn(jnp.concatenate(score_parts, axis=1), every_query))
            value_grads.append(dot_nn(jnp.concatenate(prob_parts, axis=1), every_grad))
        low = half_mask(0)
        grad_k = jnp.where(low, key_grads[0], key_grads[1]) * SCALE
        grad_v = jnp.where(low, value_grads[0], value_grads[1])
        if known_refs:
            grad_k = grad_k + known_refs[0][:, lanes]
            grad_v = grad_v + known_refs[1][:, lanes]
        dk_ref[:, lanes] = grad_k
        dv_ref[:, lanes] = grad_v


def collect_kernel(tok_rows, *refs):
    out_ref = refs[-1]
    pay_refs = chunks(refs[:2], STAT_ROWS)
    far_refs = far_chunks(tok_rows, refs[2:-1])
    spec_rows = tok_rows // UPPER
    first = 2 * (tok_rows // MIDDLE)
    count = spec_rows * (len(pay_refs) + len(far_refs))
    blocks = [r[:, tok_rows:] for r in pay_refs]
    blocks += [r[first : first + STAT_ROWS, :].astype(F32) for r in far_refs]
    for kind in range(5):
        lines = [b[kind * spec_rows : (kind + 1) * spec_rows] for b in blocks]
        out_ref[kind * count : (kind + 1) * count, :] = jnp.concatenate(lines, axis=0).astype(BF16)


def special_kernel(slots, off_ref, k_ref, v_ref, dq_in, spec_ref, dk_in, dv_in, *refs):
    blocks = refs[:-3]
    dq_ref, dk_ref, dv_ref = refs[-3:]
    rows, width = k_ref.shape
    heads = width // HD
    spec_rows = rows // UPPER
    count = slots * spec_rows
    every = count * len(blocks)
    offsets = lane_offsets(off_ref, heads, width)

    def kind(index, lanes):
        return jnp.concatenate(
            [b[index * count : (index + 1) * count, lanes] for b in blocks], axis=0
        )

    def two(block, scale=1.0):
        return jnp.concatenate([one_head(block, 0, scale), one_head(block, 1, scale)], axis=0)

    column = iota((1, 2 * every), 1)
    second = column >= every
    column = column % every
    same_group = jnp.where(column < GROUP * spec_rows, 1.0, 0.0)
    same_segment = jnp.where(column < count, 1.0, 0.0)
    row = iota((rows, 1), 0)
    low = half_mask(0)
    place = iota((8, PAIR), 1) % HD
    first_term = jnp.where(iota((8, PAIR), 0) == 0, 0, 3)
    picks = jnp.where((place >= first_term) & (place < first_term + 3), 1.0, 0.0).astype(BF16)
    states = []
    for pair in range(heads // 2):
        lanes = slice(pair * PAIR, (pair + 1) * PAIR)
        all_q, all_k, all_v, all_g, all_s = [kind(index, lanes) for index in range(5)]
        query, grad = two(all_q, SCALE), two(all_g)
        known = dot_nt(picks, two(all_s))
        known_sum, known_dot = known[0:1], known[1:2]
        scores = dot_nt(all_k, query)
        inner = dot_nt(all_v, grad)
        top = jnp.max(scores, axis=0, keepdims=True)
        weights = jnp.exp(scores - top)
        total = jnp.sum(weights, axis=0, keepdims=True)
        product = jnp.sum(weights * inner, axis=0, keepdims=True) / total
        log_sum = top + jnp.log(total)
        most = jnp.maximum(known_sum, log_sum)
        joint = most + jnp.log(jnp.exp(known_sum - most) + jnp.exp(log_sum - most))
        share = jnp.exp(known_sum - joint)
        dot = known_dot * share + product * jnp.exp(log_sum - joint)
        states.append((lanes, query, grad, all_k, scores, inner, joint, share, dot, known_dot - dot))
    for pair, state in enumerate(states):
        lanes, query, grad, _, _, _, joint, _, dot, _ = state
        offset = jnp.where(second, off_ref[2 * pair + 1], off_ref[2 * pair])
        middle = row % MIDDLE == offset % MIDDLE
        upper = row % UPPER == offset
        weight = same_group + jnp.where(middle, same_segment, 0.0) + jnp.where(upper, 1.0, 0.0)
        scores = jnp.where(weight > 0.0, dot_nt(k_ref[:, lanes], query), LOW)
        probs = jnp.exp(scores - joint) * weight
        inner = dot_nt(v_ref[:, lanes], grad) - dot
        dk_ref[:, lanes] = (
            dk_in[:, lanes] + dot_nn((probs * inner).astype(BF16), query)
        ).astype(BF16)
        dv_ref[:, lanes] = (dv_in[:, lanes] + dot_nn(probs.astype(BF16), grad)).astype(BF16)
    for lanes, _, _, all_k, scores, inner, joint, share, dot, change in states:
        probs = jnp.exp(scores - joint)
        grad_q = SCALE * lax.dot_general(
            (probs * (inner - dot)).astype(BF16),
            all_k,
            (((0,), (0,)), ((), ())),
            preferred_element_type=F32,
        )
        lines = []
        for index in range(spec_rows):
            other = every + index
            ratio = jnp.where(low, share[:, index : index + 1], share[:, other : other + 1])
            moved = jnp.where(low, change[:, index : index + 1], change[:, other : other + 1])
            top_q = jnp.where(low, grad_q[index : index + 1], grad_q[other : other + 1])
            near_q = spec_ref[index : index + 1, lanes]
            key_sum = spec_ref[spec_rows + index : spec_rows + index + 1, lanes]
            line = ratio * (near_q + moved * key_sum) + top_q
            lines.append(jnp.broadcast_to(line, (UPPER, PAIR)))
        special = row % UPPER == offsets[:, lanes]
        dq_ref[:, lanes] = (
            dq_in[:, lanes] + jnp.where(special, jnp.concatenate(lines, axis=0), 0.0)
        ).astype(BF16)


def call(kernel, outs, *arrays, us=1.0, raw=False, scratch=(), vmem_mib=40):
    smem = pl.BlockSpec(memory_space=pltpu.SMEM)
    vmem = pl.BlockSpec(memory_space=pltpu.VMEM)
    space = pl.BlockSpec(memory_space=pltpu.HBM) if raw else vmem
    specs = [smem if a.dtype == jnp.int32 and not raw else space for a in arrays]
    return pl.pallas_call(
        kernel,
        out_shape=tuple(jax.ShapeDtypeStruct(shape, dtype) for shape, dtype in outs),
        in_specs=specs,
        out_specs=tuple(vmem for _ in outs),
        scratch_shapes=scratch,
        cost_estimate=pl.CostEstimate(
            flops=int(us * 1.15e9), bytes_accessed=0, transcendentals=0
        ),
        compiler_params=pltpu.CompilerParams(vmem_limit_bytes=vmem_mib * 1024 * 1024),
    )(*arrays)


def across(value, axis, mask):
    size = lax.axis_size(axis)
    return lax.ppermute(value, axis, [(source, source ^ mask) for source in range(size)])


def local(queries, key_matrix, value_matrix, grad_out, offsets):
    rows, width = queries.shape
    slots, outer = lax.axis_size("ctxb"), lax.axis_size("ctxa")
    near_count = slots - GROUP
    near_rows, spec_rows = rows // MIDDLE, rows // UPPER

    next_k, next_v = across(key_matrix, "ctxb", 2), across(value_matrix, "ctxb", 2)
    core_k, core_v = across(key_matrix, "ctxb", 1), across(value_matrix, "ctxb", 1)
    near_kv, near_qg, spec = call(
        pack_kernel,
        [
            ((2 * near_rows, width), BF16),
            ((2 * near_rows, width), BF16),
            ((4 * SPEC_PAD, width), BF16),
        ],
        offsets, queries, key_matrix, value_matrix, grad_out,
        us=1.3, raw=True, vmem_mib=60,
        scratch=[
            pltpu.SMEM(offsets.shape, jnp.int32),
            pltpu.VMEM((4, rows, width), BF16),
            pltpu.SemaphoreType.DMA((4,)),
            pltpu.SemaphoreType.DMA,
        ],
    )
    near_came = [across(near_kv, "ctxb", mask) for mask in reversed(range(GROUP, slots, 2))]
    both = [((2 * rows, width), BF16)]
    own_kv = [key_matrix, value_matrix, core_k, core_v]
    term_rows = -(-3 * (width // HD) // 8) * 8
    (known,) = call(
        first_kernel, [((term_rows, rows), F32)],
        offsets, queries, grad_out, *own_kv, us=2.2,
    )
    (stacked,) = call(
        stack_kernel,
        [((2 * rows + 2 * near_rows * len(near_came), width), BF16)],
        known, next_k, next_v, *near_came, us=0.2,
    )
    kv_parts = own_kv + [stacked, across(stacked, "ctxb", 1)]
    (qg,) = call(merge_kernel, both, queries, grad_out, stacked, us=0.3)
    next_qg = across(qg, "ctxb", 2)
    core_qg = across(qg, "ctxb", 1)
    pay, far = call(
        partial(forward_kernel, near_count),
        [
            ((STAT_ROWS, rows + width), F32),
            ((2 * near_rows + 2 * STAT_ROWS, width), BF16),
        ],
        offsets, queries, grad_out, known, spec, near_qg, *kv_parts[4:], us=2.5,
    )
    dq, dq_spec = call(
        partial(query_kernel, near_count),
        [((rows, width), F32), ((2 * spec_rows, width), F32)],
        offsets, qg, spec, pay, *kv_parts, us=5.0,
    )
    pays_far = [pay, across(pay, "ctxb", 2)]
    far_came = [across(far, "ctxb", mask) for mask in reversed(range(GROUP, slots, 2))]
    grads = [((rows, width), F32)] * 2
    own_dk, own_dv = call(
        partial(key_kernel, 0), grads, offsets, key_matrix, value_matrix, qg, pay, us=1.3,
    )
    held = call(
        relay_kernel,
        [
            ((2 * STAT_ROWS, rows + width), F32),
            ((far.shape[0] * len(far_came), width), BF16),
        ],
        dq_spec, own_dk, *pays_far, *far_came, us=0.3,
    )
    pays, fars = [(part, across(part, "ctxb", 1)) for part in held]
    (block,) = call(
        partial(collect_kernel, rows), [((5 * slots * spec_rows, width), BF16)], *pays, *fars,
        us=0.3,
    )
    (next_qg,) = call(copy_kernel, [((2 * rows, width), BF16)], block, next_qg, us=0.2)
    qg_parts = [qg, core_qg, next_qg, across(next_qg, "ctxb", 1)]
    blocks = [block] + [across(block, "ctxa", mask) for mask in reversed(range(1, outer))]
    dk, dv = call(
        partial(key_kernel, near_count),
        grads,
        offsets, key_matrix, value_matrix, *qg_parts[1:], *pays, *fars, own_dk, own_dv, us=4.0,
    )
    return call(
        partial(special_kernel, slots),
        [((rows, width), BF16)] * 3,
        offsets, key_matrix, value_matrix, dq, dq_spec, dk, dv, *blocks, us=3.0,
    )


def solution(mesh):
    split = P(("ctxa", "ctxb"), None)
    return jax.shard_map(
        local,
        mesh=mesh,
        in_specs=(split, split, split, split, P()),
        out_specs=(split, split, split),
        check_vma=False,
    )
```

```python
from functools import partial

import jax
import jax.numpy as jnp
from jax import lax
from jax.experimental import pallas as pl
from jax.experimental.pallas import tpu as pltpu
from jax.sharding import PartitionSpec as P

HD = 64
PAIR = 2 * HD
GROUP = 4
MIDDLE = 8
UPPER = 128
LOW = -1e30
HIGH = 1e30
SCALE = HD**-0.5
F32 = jnp.float32
BF16 = jnp.bfloat16
STAT_ROWS = 16
SPEC_PAD = 16
KV_ARRAYS = 6


def iota(shape, dim):
    return lax.broadcasted_iota(jnp.int32, shape, dim)


def dot_nt(a, b):
    return lax.dot_general(a, b, (((1,), (1,)), ((), ())), preferred_element_type=F32)


def dot_nn(a, b):
    return jnp.dot(a, b, preferred_element_type=F32)


def pair_slice(head):
    low = head // 2 * PAIR
    return slice(low, low + PAIR)


def half_mask(head):
    return iota((1, PAIR), 1) // HD == head % 2


def one_head(block, head, scale=1.0):
    return jnp.where(half_mask(head), block.astype(F32) * scale, 0.0).astype(BF16)


def lane_offsets(off_ref, heads, width):
    lane_head = iota((1, width), 1) // HD
    out = jnp.zeros((1, width), jnp.int32)
    for head in range(heads):
        out = jnp.where(lane_head == head, off_ref[head], out)
    return out


def row_offsets(off_ref, heads):
    rows = iota((STAT_ROWS, 1), 0)
    out = jnp.zeros((STAT_ROWS, 1), jnp.int32)
    for head in range(heads):
        out = jnp.where((rows == head) | (rows == head + heads), off_ref[head], out)
    return out


def pair_weights(columns, middle_offset):
    both = (iota((MIDDLE, columns), 0) == middle_offset) & (
        iota((MIDDLE, columns), 1) % MIDDLE == middle_offset
    )
    return jnp.where(both, 2.0, 1.0)


def weighted(probs, weight):
    rows, columns = probs.shape
    tiles = probs.reshape(rows // MIDDLE, MIDDLE, columns)
    return (tiles * weight[None]).reshape(rows, columns)


def pack_kernel(
    off_in, q_ref, k_ref, v_ref, g_ref, near_kv_ref, near_qg_ref, spec_ref,
    off_ref, buffer, sems, off_sem,
):
    rows, width = q_ref.shape
    heads = width // HD
    near_rows, spec_rows = rows // MIDDLE, rows // UPPER
    places = (
        (k_ref, 0, near_kv_ref, 0, 1),
        (v_ref, 1, near_kv_ref, 1, 2),
        (q_ref, 2, near_qg_ref, 0, 0),
        (g_ref, 3, near_qg_ref, 1, 3),
    )
    off_copy = pltpu.make_async_copy(off_in, off_ref, off_sem)
    off_copy.start()
    copies = [
        pltpu.make_async_copy(source, buffer.at[index], sems.at[index])
        for source, index, _, _, _ in places
    ]
    for copy in copies:
        copy.start()
    off_copy.wait()
    offsets = lane_offsets(off_ref, heads, width)
    middle = iota((rows, width), 0) % MIDDLE == offsets % MIDDLE
    index = iota((near_rows, width), 0)
    gather = jnp.where(
        iota((near_rows, rows), 1) // MIDDLE == iota((near_rows, rows), 0), 1.0, 0.0
    ).astype(BF16)
    spec_ref[...] = jnp.zeros(spec_ref.shape, BF16)
    for (_, source, near_ref, slot, kind), copy in zip(places, copies):
        copy.wait()
        whole = buffer[source].astype(F32)
        kept = dot_nn(gather, jnp.where(middle, whole, 0.0).astype(BF16))
        near_ref[slot * near_rows : (slot + 1) * near_rows, :] = kept.astype(BF16)
        step = UPPER // MIDDLE
        top = jnp.where(index % step == offsets // MIDDLE, kept, 0.0)
        top = top.reshape(spec_rows, step, width).sum(axis=1)
        pad = jnp.zeros((SPEC_PAD - spec_rows, width), F32)
        spec_ref[kind * SPEC_PAD : (kind + 1) * SPEC_PAD, :] = jnp.concatenate(
            [top, pad], axis=0
        ).astype(BF16)


def split_terms(value):
    terms = []
    for _ in range(3):
        terms.append(value.astype(BF16).astype(F32))
        value = value - terms[-1]
    return terms


def next_refs(refs, rows):
    near_rows = 2 * (rows // MIDDLE)
    near = []
    for low in range(2 * rows, refs[0].shape[0], near_rows):
        near += [r.at[low : low + near_rows] for r in refs]
    return [r.at[:rows] for r in refs], [r.at[rows : 2 * rows] for r in refs], near


def key_value_refs(refs):
    keys, values, near = next_refs(refs[4:], refs[0].shape[0])
    return [refs[0], refs[2]] + keys, [refs[1], refs[3]] + values, near


def chunks(refs, rows):
    first, second = refs
    pieces = []
    for low in range(0, first.shape[0], rows):
        pieces += [first.at[low : low + rows], second.at[low : low + rows]]
    return pieces


def near_part(near_refs, slot, lanes):
    rows = near_refs[0].shape[0] // 2
    return jnp.concatenate([r[slot * rows : (slot + 1) * rows, lanes] for r in near_refs], axis=0)


def merge_kernel(first_ref, second_ref, _, out_ref):
    rows = first_ref.shape[0]
    out_ref[:rows, :] = first_ref[...]
    out_ref[rows:, :] = second_ref[...]


def softmax_terms(scores, inners, weights, top, total, product):
    new_top = top
    for part in scores:
        peak = jnp.max(part, axis=0, keepdims=True)
        new_top = peak if new_top is None else jnp.maximum(new_top, peak)
    if top is not None:
        scale = jnp.exp(top - new_top)
        total, product = total * scale, product * scale
    for part, inner, weight in zip(scores, inners, weights):
        probs = jnp.exp(part - new_top)
        if weight is not None:
            probs = weighted(probs, weight)
        part_total = jnp.sum(probs, axis=0, keepdims=True)
        part_product = jnp.sum(probs * inner, axis=0, keepdims=True)
        total = part_total if total is None else total + part_total
        product = part_product if product is None else product + part_product
    return new_top, total, product


def first_kernel(off_ref, q_ref, g_ref, *refs):
    kv_refs, out_ref = refs[:-1], refs[-1]
    rows, width = q_ref.shape
    heads = width // HD

    def products(head):
        lanes = pair_slice(head)
        query = one_head(q_ref[:, lanes], head, SCALE)
        grad = one_head(g_ref[:, lanes], head)
        scores = [dot_nt(r[:, lanes], query) for r in kv_refs[::2]]
        return scores, [dot_nt(r[:, lanes], grad) for r in kv_refs[1::2]]

    ahead = products(0)
    for head in range(heads):
        (scores, inners), ahead = ahead, products(head + 1) if head + 1 < heads else None
        weight = pair_weights(rows, off_ref[head] % MIDDLE)
        terms = softmax_terms(scores, inners, [weight] * len(scores), None, None, None)
        for index, term in enumerate(terms):
            row = index * heads + head
            out_ref[row : row + 1, :] = term


def forward_kernel(near_count, off_ref, q_ref, g_ref, known_ref, spec_ref, own_near_ref, *refs):
    k_refs, v_refs, near_refs = next_refs(refs[:-2], q_ref.shape[0])
    out_ref, far_ref = refs[-2:]
    rows, width = q_ref.shape
    heads = width // HD
    terms = []

    def products(head):
        lanes = pair_slice(head)
        query = one_head(q_ref[:, lanes], head, SCALE)
        grad = one_head(g_ref[:, lanes], head)
        keys, values = [r[:, lanes] for r in k_refs], [r[:, lanes] for r in v_refs]
        if near_count:
            keys.append(near_part(near_refs, 0, lanes))
            values.append(near_part(near_refs, 1, lanes))
        return [dot_nt(key, query) for key in keys], [dot_nt(value, grad) for value in values]

    ahead = products(0)
    for head in range(heads):
        (scores, inners), ahead = ahead, products(head + 1) if head + 1 < heads else None
        middle_offset = off_ref[head] % MIDDLE
        weights = [pair_weights(rows, middle_offset)] * len(k_refs)
        if near_count:
            chosen = iota((1, rows), 1) % MIDDLE == middle_offset
            scores[-1] = jnp.where(chosen, scores[-1], LOW)
            weights.append(None)
        known = [known_ref[i * heads + head : i * heads + head + 1, :] for i in range(3)]
        terms.append(softmax_terms(scores, inners, weights, *known))
    top, total, product = [jnp.concatenate(lines, axis=0) for lines in zip(*terms)]
    pad = jnp.zeros((STAT_ROWS - 2 * heads, rows), F32)
    stats = jnp.concatenate([top + jnp.log(total), product / total, pad], axis=0)
    out_ref[:, :rows] = stats
    offsets = row_offsets(off_ref, heads)
    token = iota((STAT_ROWS, rows), 1)
    spec_rows = rows // UPPER
    lane = iota((STAT_ROWS, width), 1)
    row = iota((STAT_ROWS, width), 0)
    place = iota((1, width), 1) % HD
    lines = [
        spec_ref[kind * SPEC_PAD : kind * SPEC_PAD + spec_rows, :].astype(F32) for kind in range(4)
    ]
    for index in range(spec_rows):
        value = jnp.sum(
            jnp.where(token == offsets + index * UPPER, stats, 0.0), axis=1, keepdims=True
        )
        line = jnp.zeros((1, width), F32)
        for kind in range(2):
            spread = jnp.sum(
                jnp.where(lane // HD + kind * heads == row, value, 0.0), axis=0, keepdims=True
            )
            for index_of, term in enumerate(split_terms(spread)):
                line = jnp.where(place == 3 * kind + index_of, term, line)
        lines.append(line)
    lines.append(jnp.zeros((STAT_ROWS - 5 * spec_rows, width), F32))
    block = jnp.concatenate(lines, axis=0)
    out_ref[:, rows:] = block
    near_rows = own_near_ref.shape[0]
    far_ref[:near_rows, :] = own_near_ref[...]
    far_ref[near_rows : near_rows + STAT_ROWS, :] = block.astype(BF16)
    kept = jnp.where(token % MIDDLE == offsets % MIDDLE, stats, 0.0)
    gather = jnp.where(iota((rows, PAIR), 0) // MIDDLE == iota((rows, PAIR), 1), 1.0, 0.0)
    gather = gather.astype(BF16)
    for index, term in enumerate(split_terms(kept)):
        far_ref[near_rows + STAT_ROWS :, index * PAIR : (index + 1) * PAIR] = dot_nn(
            term.astype(BF16), gather
        ).astype(BF16)


def query_kernel(near_count, off_ref, qg_ref, spec_in, pay_ref, *refs):
    k_refs, v_refs, near_refs = key_value_refs(refs[:KV_ARRAYS])
    dq_ref, spec_ref = refs[-2:]
    rows, width = k_refs[0].shape
    heads = width // HD
    spec_rows = rows // UPPER
    full = rows + SPEC_PAD
    columns = jnp.transpose(pay_ref[:, :rows])
    offsets = lane_offsets(off_ref, heads, width)
    column = iota((1, STAT_ROWS), 1)
    column_offsets = jnp.zeros((1, STAT_ROWS), jnp.int32)
    for head in range(heads):
        column_offsets = jnp.where(
            (column == head) | (column == head + heads), off_ref[head], column_offsets
        )
    token = iota((rows, STAT_ROWS), 0)
    lines = [
        jnp.sum(
            jnp.where(token == column_offsets + index * UPPER, columns, 0.0),
            axis=0,
            keepdims=True,
        )
        for index in range(spec_rows)
    ]
    lines.append(jnp.zeros((SPEC_PAD - spec_rows, STAT_ROWS), F32))
    columns = jnp.concatenate([columns] + lines, axis=0)
    for pair in range(heads // 2):
        lanes = slice(pair * PAIR, (pair + 1) * PAIR)
        both_q = jnp.concatenate([qg_ref[:rows, lanes], spec_in[:SPEC_PAD, lanes]], axis=0)
        both_g = jnp.concatenate([qg_ref[rows:, lanes], spec_in[3 * SPEC_PAD :, lanes]], axis=0)
        keys = [r[:, lanes] for r in k_refs]
        if near_count:
            keys.append(near_part(near_refs, 0, lanes))
        every_key = jnp.concatenate(keys, axis=0)
        results = []
        for head in (2 * pair, 2 * pair + 1):
            middle_offset = off_ref[head] % MIDDLE
            row = iota((full, 1), 0)
            chosen = (row % MIDDLE == middle_offset) | (row >= rows)
            weight = pair_weights(rows, middle_offset)
            row_weight = jnp.where(iota((1, rows), 1) % MIDDLE == middle_offset, 2.0, 1.0)
            query = one_head(both_q, head, SCALE)
            grad = one_head(both_g, head)
            log_sum = columns[:, head : head + 1]
            dot = columns[:, heads + head : heads + head + 1]
            parts = []
            for key, v_ref in zip(keys, v_refs):
                probs = jnp.exp(dot_nt(query, key) - log_sum)
                probs = jnp.concatenate(
                    [weighted(probs[:rows], weight), probs[rows:] * row_weight], axis=0
                )
                inner = dot_nt(grad, v_ref[:, lanes]) - dot
                parts.append(
                    jnp.concatenate([(probs * inner).astype(BF16), probs[rows:].astype(BF16)], axis=0)
                )
            if near_count:
                scores = jnp.where(chosen, dot_nt(query, keys[-1]), LOW)
                probs = jnp.exp(scores - log_sum)
                inner = dot_nt(grad, near_part(near_refs, 1, lanes)) - dot
                parts.append(
                    jnp.concatenate([(probs * inner).astype(BF16), probs[rows:].astype(BF16)], axis=0)
                )
            results.append(dot_nn(jnp.concatenate(parts, axis=1), every_key))
        result = jnp.where(half_mask(0), results[0], results[1]) * SCALE
        special = iota((rows, PAIR), 0) % UPPER == offsets[:, lanes]
        dq_ref[:, lanes] = jnp.where(special, 0.0, result[:rows])
        spec_ref[:spec_rows, lanes] = result[rows : rows + spec_rows]
        spec_ref[spec_rows:, lanes] = result[full : full + spec_rows]


def stack_kernel(first_ref, *refs):
    out, low = refs[-1], 0
    for ref in refs[:-1]:
        rows = ref.shape[0]
        out[low : low + rows, :] = ref[...]
        low += rows


def far_chunks(tok_rows, refs):
    return chunks(refs, 2 * (tok_rows // MIDDLE) + 2 * STAT_ROWS) if refs else []


def relay_kernel(first_ref, second_ref, *refs):
    pay_refs, far_refs = refs[:2], refs[2:-2]
    for parts, out in zip((pay_refs, far_refs), refs[-2:]):
        for index, ref in enumerate(parts):
            rows = ref.shape[0]
            out[index * rows : (index + 1) * rows, :] = ref[...]


def copy_kernel(_, in_ref, out_ref):
    out_ref[...] = in_ref[...]


def key_kernel(near_count, off_ref, k_ref, v_ref, *refs):
    dk_ref, dv_ref = refs[-2:]
    rows, width = k_ref.shape
    heads = width // HD
    near_rows = rows // MIDDLE
    if len(refs) == 4:
        qg_refs, pay_refs, known_refs = refs[:1], refs[1:2], None
    else:
        qg_refs = refs[: GROUP - 1]
        pay_refs = chunks(refs[GROUP - 1 : GROUP + 1], STAT_ROWS)[1:]
        far_refs = far_chunks(k_ref.shape[0], refs[GROUP + 1 : -4])
        known_refs = refs[-4:-2]
    if near_count:
        first = 2 * near_rows + STAT_ROWS
        far_stats = []
        for r in far_refs:
            lines = r[first : first + STAT_ROWS, :].astype(F32)
            line = lines[:, :PAIR] + lines[:, PAIR : 2 * PAIR] + lines[:, 2 * PAIR : 3 * PAIR]
            far_stats.append(line[:, :near_rows])
        far_stats = jnp.concatenate(far_stats, axis=1)
    for pair in range(heads // 2):
        lanes = slice(pair * PAIR, (pair + 1) * PAIR)
        queries = [r[:rows, lanes] for r in qg_refs]
        grads = [r[rows:, lanes] for r in qg_refs]
        if near_count:
            queries.append(
                jnp.concatenate([r[:near_rows, lanes] for r in far_refs], axis=0)
            )
            grads.append(
                jnp.concatenate([r[near_rows : 2 * near_rows, lanes] for r in far_refs], axis=0)
            )
        every_query = jnp.concatenate(queries, axis=0)
        every_grad = jnp.concatenate(grads, axis=0)
        key_grads, value_grads = [], []
        for head in (2 * pair, 2 * pair + 1):
            middle_offset = off_ref[head] % MIDDLE
            chosen = iota((rows, 1), 0) % MIDDLE == middle_offset
            weight = pair_weights(rows, middle_offset)
            keys = one_head(k_ref[:, lanes], head, SCALE)
            values = one_head(v_ref[:, lanes], head)
            special = iota((1, rows), 1) % UPPER == off_ref[head]
            prob_parts, score_parts = [], []
            for query, grad, pay_ref in zip(queries, grads, pay_refs):
                log_sum = jnp.where(special, HIGH, pay_ref[head : head + 1, :rows])
                dot = pay_ref[heads + head : heads + head + 1, :rows]
                probs = weighted(jnp.exp(dot_nt(keys, query) - log_sum), weight)
                inner = dot_nt(values, grad) - dot
                prob_parts.append(probs.astype(BF16))
                score_parts.append((probs * inner).astype(BF16))
            if near_count:
                count = near_count * near_rows
                special = iota((1, count), 1) % (UPPER // MIDDLE) == off_ref[head] // MIDDLE
                log_sum = jnp.where(special, HIGH, far_stats[head : head + 1, :])
                dot = far_stats[heads + head : heads + head + 1, :]
                scores = jnp.where(chosen, dot_nt(keys, queries[-1]), LOW)
                probs = jnp.exp(scores - log_sum)
                inner = dot_nt(values, grads[-1]) - dot
                prob_parts.append(probs.astype(BF16))
                score_parts.append((probs * inner).astype(BF16))
            key_grads.append(dot_nn(jnp.concatenate(score_parts, axis=1), every_query))
            value_grads.append(dot_nn(jnp.concatenate(prob_parts, axis=1), every_grad))
        low = half_mask(0)
        grad_k = jnp.where(low, key_grads[0], key_grads[1]) * SCALE
        grad_v = jnp.where(low, value_grads[0], value_grads[1])
        if known_refs:
            grad_k = grad_k + known_refs[0][:, lanes]
            grad_v = grad_v + known_refs[1][:, lanes]
        dk_ref[:, lanes] = grad_k
        dv_ref[:, lanes] = grad_v


def collect_kernel(tok_rows, *refs):
    out_ref = refs[-1]
    pay_refs = chunks(refs[:2], STAT_ROWS)
    far_refs = far_chunks(tok_rows, refs[2:-1])
    spec_rows = tok_rows // UPPER
    first = 2 * (tok_rows // MIDDLE)
    count = spec_rows * (len(pay_refs) + len(far_refs))
    blocks = [r[:, tok_rows:] for r in pay_refs]
    blocks += [r[first : first + STAT_ROWS, :].astype(F32) for r in far_refs]
    for kind in range(5):
        lines = [b[kind * spec_rows : (kind + 1) * spec_rows] for b in blocks]
        out_ref[kind * count : (kind + 1) * count, :] = jnp.concatenate(lines, axis=0).astype(BF16)


def special_kernel(slots, off_ref, k_ref, v_ref, dq_in, spec_ref, dk_in, dv_in, *refs):
    blocks = refs[:-3]
    dq_ref, dk_ref, dv_ref = refs[-3:]
    rows, width = k_ref.shape
    heads = width // HD
    spec_rows = rows // UPPER
    count = slots * spec_rows
    every = count * len(blocks)
    offsets = lane_offsets(off_ref, heads, width)

    def kind(index, lanes):
        return jnp.concatenate(
            [b[index * count : (index + 1) * count, lanes] for b in blocks], axis=0
        )

    def two(block, scale=1.0):
        return jnp.concatenate([one_head(block, 0, scale), one_head(block, 1, scale)], axis=0)

    column = iota((1, 2 * every), 1)
    second = column >= every
    column = column % every
    same_group = jnp.where(column < GROUP * spec_rows, 1.0, 0.0)
    same_segment = jnp.where(column < count, 1.0, 0.0)
    row = iota((rows, 1), 0)
    low = half_mask(0)
    place = iota((8, PAIR), 1) % HD
    first_term = jnp.where(iota((8, PAIR), 0) == 0, 0, 3)
    picks = jnp.where((place >= first_term) & (place < first_term + 3), 1.0, 0.0).astype(BF16)
    every_product = []
    for pair in range(heads // 2):
        lanes = slice(pair * PAIR, (pair + 1) * PAIR)
        all_q, all_k, all_v, all_g, all_s = [kind(index, lanes) for index in range(5)]
        query, grad = two(all_q, SCALE), two(all_g)
        known = dot_nt(picks, two(all_s))
        scores, inner = dot_nt(all_k, query), dot_nt(all_v, grad)
        own = dot_nt(k_ref[:, lanes], query), dot_nt(v_ref[:, lanes], grad)
        every_product.append((lanes, query, grad, all_k, known, scores, inner, own))
    states = []
    for lanes, query, grad, all_k, known, scores, inner, own in every_product:
        known_sum, known_dot = known[0:1], known[1:2]
        top = jnp.max(scores, axis=0, keepdims=True)
        weights = jnp.exp(scores - top)
        total = jnp.sum(weights, axis=0, keepdims=True)
        product = jnp.sum(weights * inner, axis=0, keepdims=True) / total
        log_sum = top + jnp.log(total)
        most = jnp.maximum(known_sum, log_sum)
        joint = most + jnp.log(jnp.exp(known_sum - most) + jnp.exp(log_sum - most))
        share = jnp.exp(known_sum - joint)
        dot = known_dot * share + product * jnp.exp(log_sum - joint)
        change = known_dot - dot
        states.append((lanes, query, grad, all_k, scores, inner, own, joint, share, dot, change))
    for pair, state in enumerate(states):
        lanes, query, grad, _, _, _, own, joint, _, dot, _ = state
        offset = jnp.where(second, off_ref[2 * pair + 1], off_ref[2 * pair])
        middle = row % MIDDLE == offset % MIDDLE
        upper = row % UPPER == offset
        weight = same_group + jnp.where(middle, same_segment, 0.0) + jnp.where(upper, 1.0, 0.0)
        scores = jnp.where(weight > 0.0, own[0], LOW)
        probs = jnp.exp(scores - joint) * weight
        inner = own[1] - dot
        dk_ref[:, lanes] = (
            dk_in[:, lanes] + dot_nn((probs * inner).astype(BF16), query)
        ).astype(BF16)
        dv_ref[:, lanes] = (dv_in[:, lanes] + dot_nn(probs.astype(BF16), grad)).astype(BF16)
    for lanes, _, _, all_k, scores, inner, _, joint, share, dot, change in states:
        probs = jnp.exp(scores - joint)
        grad_q = SCALE * lax.dot_general(
            (probs * (inner - dot)).astype(BF16),
            all_k,
            (((0,), (0,)), ((), ())),
            preferred_element_type=F32,
        )
        lines = []
        for index in range(spec_rows):
            other = every + index
            ratio = jnp.where(low, share[:, index : index + 1], share[:, other : other + 1])
            moved = jnp.where(low, change[:, index : index + 1], change[:, other : other + 1])
            top_q = jnp.where(low, grad_q[index : index + 1], grad_q[other : other + 1])
            near_q = spec_ref[index : index + 1, lanes]
            key_sum = spec_ref[spec_rows + index : spec_rows + index + 1, lanes]
            line = ratio * (near_q + moved * key_sum) + top_q
            lines.append(jnp.broadcast_to(line, (UPPER, PAIR)))
        special = row % UPPER == offsets[:, lanes]
        dq_ref[:, lanes] = (
            dq_in[:, lanes] + jnp.where(special, jnp.concatenate(lines, axis=0), 0.0)
        ).astype(BF16)


def call(kernel, outs, *arrays, us=1.0, raw=False, scratch=(), vmem_mib=40):
    smem = pl.BlockSpec(memory_space=pltpu.SMEM)
    vmem = pl.BlockSpec(memory_space=pltpu.VMEM)
    space = pl.BlockSpec(memory_space=pltpu.HBM) if raw else vmem
    specs = [smem if a.dtype == jnp.int32 and not raw else space for a in arrays]
    return pl.pallas_call(
        kernel,
        out_shape=tuple(jax.ShapeDtypeStruct(shape, dtype) for shape, dtype in outs),
        in_specs=specs,
        out_specs=tuple(vmem for _ in outs),
        scratch_shapes=scratch,
        cost_estimate=pl.CostEstimate(
            flops=int(us * 1.15e9), bytes_accessed=0, transcendentals=0
        ),
        compiler_params=pltpu.CompilerParams(vmem_limit_bytes=vmem_mib * 1024 * 1024),
    )(*arrays)


def across(value, axis, mask):
    size = lax.axis_size(axis)
    return lax.ppermute(value, axis, [(source, source ^ mask) for source in range(size)])


def local(queries, key_matrix, value_matrix, grad_out, offsets):
    rows, width = queries.shape
    slots, outer = lax.axis_size("ctxb"), lax.axis_size("ctxa")
    near_count = slots - GROUP
    near_rows, spec_rows = rows // MIDDLE, rows // UPPER

    next_k, next_v = across(key_matrix, "ctxb", 2), across(value_matrix, "ctxb", 2)
    core_k, core_v = across(key_matrix, "ctxb", 1), across(value_matrix, "ctxb", 1)
    near_kv, near_qg, spec = call(
        pack_kernel,
        [
            ((2 * near_rows, width), BF16),
            ((2 * near_rows, width), BF16),
            ((4 * SPEC_PAD, width), BF16),
        ],
        offsets, queries, key_matrix, value_matrix, grad_out,
        us=1.3, raw=True, vmem_mib=60,
        scratch=[
            pltpu.SMEM(offsets.shape, jnp.int32),
            pltpu.VMEM((4, rows, width), BF16),
            pltpu.SemaphoreType.DMA((4,)),
            pltpu.SemaphoreType.DMA,
        ],
    )
    near_came = [across(near_kv, "ctxb", mask) for mask in reversed(range(GROUP, slots, 2))]
    both = [((2 * rows, width), BF16)]
    own_kv = [key_matrix, value_matrix, core_k, core_v]
    term_rows = -(-3 * (width // HD) // 8) * 8
    (known,) = call(
        first_kernel, [((term_rows, rows), F32)],
        offsets, queries, grad_out, *own_kv, us=2.2,
    )
    (stacked,) = call(
        stack_kernel,
        [((2 * rows + 2 * near_rows * len(near_came), width), BF16)],
        known, next_k, next_v, *near_came, us=0.2,
    )
    kv_parts = own_kv + [stacked, across(stacked, "ctxb", 1)]
    (qg,) = call(merge_kernel, both, queries, grad_out, stacked, us=0.3)
    next_qg = across(qg, "ctxb", 2)
    core_qg = across(qg, "ctxb", 1)
    pay, far = call(
        partial(forward_kernel, near_count),
        [
            ((STAT_ROWS, rows + width), F32),
            ((2 * near_rows + 2 * STAT_ROWS, width), BF16),
        ],
        offsets, queries, grad_out, known, spec, near_qg, *kv_parts[4:], us=2.5,
    )
    dq, dq_spec = call(
        partial(query_kernel, near_count),
        [((rows, width), F32), ((2 * spec_rows, width), F32)],
        offsets, qg, spec, pay, *kv_parts, us=5.0,
    )
    pays_far = [pay, across(pay, "ctxb", 2)]
    far_came = [across(far, "ctxb", mask) for mask in reversed(range(GROUP, slots, 2))]
    grads = [((rows, width), F32)] * 2
    own_dk, own_dv = call(
        partial(key_kernel, 0), grads, offsets, key_matrix, value_matrix, qg, pay, us=1.3,
    )
    held = call(
        relay_kernel,
        [
            ((2 * STAT_ROWS, rows + width), F32),
            ((far.shape[0] * len(far_came), width), BF16),
        ],
        dq_spec, own_dk, *pays_far, *far_came, us=0.3,
    )
    pays, fars = [(part, across(part, "ctxb", 1)) for part in held]
    (block,) = call(
        partial(collect_kernel, rows), [((5 * slots * spec_rows, width), BF16)], *pays, *fars,
        us=0.3,
    )
    (next_qg,) = call(copy_kernel, [((2 * rows, width), BF16)], block, next_qg, us=0.2)
    qg_parts = [qg, core_qg, next_qg, across(next_qg, "ctxb", 1)]
    blocks = [block] + [across(block, "ctxa", mask) for mask in reversed(range(1, outer))]
    dk, dv = call(
        partial(key_kernel, near_count),
        grads,
        offsets, key_matrix, value_matrix, *qg_parts[1:], *pays, *fars, own_dk, own_dv, us=4.0,
    )
    return call(
        partial(special_kernel, slots),
        [((rows, width), BF16)] * 3,
        offsets, key_matrix, value_matrix, dq, dq_spec, dk, dv, *blocks, us=3.0,
    )


def solution(mesh):
    split = P(("ctxa", "ctxb"), None)
    return jax.shard_map(
        local,
        mesh=mesh,
        in_specs=(split, split, split, split, P()),
        out_specs=(split, split, split),
        check_vma=False,
    )
```

```python
from functools import partial

import jax
import jax.numpy as jnp
from jax import lax
from jax.experimental import pallas as pl
from jax.experimental.pallas import tpu as pltpu
from jax.sharding import PartitionSpec as P

HD = 64
PAIR = 2 * HD
GROUP = 4
MIDDLE = 8
UPPER = 128
LOW = -1e30
HIGH = 1e30
SCALE = HD**-0.5
F32 = jnp.float32
BF16 = jnp.bfloat16
STAT_ROWS = 16
SPEC_PAD = 16
KV_ARRAYS = 6


def iota(shape, dim):
    return lax.broadcasted_iota(jnp.int32, shape, dim)


def dot_nt(a, b):
    return lax.dot_general(a, b, (((1,), (1,)), ((), ())), preferred_element_type=F32)


def dot_nn(a, b):
    return jnp.dot(a, b, preferred_element_type=F32)


def pair_slice(head):
    low = head // 2 * PAIR
    return slice(low, low + PAIR)


def half_mask(head):
    return iota((1, PAIR), 1) // HD == head % 2


def one_head(block, head, scale=1.0):
    return jnp.where(half_mask(head), block.astype(F32) * scale, 0.0).astype(BF16)


def lane_offsets(off_ref, heads, width):
    lane_head = iota((1, width), 1) // HD
    out = jnp.zeros((1, width), jnp.int32)
    for head in range(heads):
        out = jnp.where(lane_head == head, off_ref[head], out)
    return out


def row_offsets(off_ref, heads):
    rows = iota((STAT_ROWS, 1), 0)
    out = jnp.zeros((STAT_ROWS, 1), jnp.int32)
    for head in range(heads):
        out = jnp.where((rows == head) | (rows == head + heads), off_ref[head], out)
    return out


def pair_weights(columns, middle_offset):
    both = (iota((MIDDLE, columns), 0) == middle_offset) & (
        iota((MIDDLE, columns), 1) % MIDDLE == middle_offset
    )
    return jnp.where(both, 2.0, 1.0)


def weighted(probs, weight):
    rows, columns = probs.shape
    tiles = probs.reshape(rows // MIDDLE, MIDDLE, columns)
    return (tiles * weight[None]).reshape(rows, columns)


def pack_kernel(
    off_in, q_ref, k_ref, v_ref, g_ref, near_kv_ref, near_qg_ref, spec_ref,
    off_ref, buffer, sems, off_sem,
):
    rows, width = q_ref.shape
    heads = width // HD
    near_rows, spec_rows = rows // MIDDLE, rows // UPPER
    places = (
        (k_ref, 0, near_kv_ref, 0, 1),
        (v_ref, 1, near_kv_ref, 1, 2),
        (q_ref, 2, near_qg_ref, 0, 0),
        (g_ref, 3, near_qg_ref, 1, 3),
    )
    off_copy = pltpu.make_async_copy(off_in, off_ref, off_sem)
    off_copy.start()
    copies = [
        pltpu.make_async_copy(source, buffer.at[index], sems.at[index])
        for source, index, _, _, _ in places
    ]
    for copy in copies:
        copy.start()
    off_copy.wait()
    offsets = lane_offsets(off_ref, heads, width)
    middle = iota((rows, width), 0) % MIDDLE == offsets % MIDDLE
    index = iota((near_rows, width), 0)
    gather = jnp.where(
        iota((near_rows, rows), 1) // MIDDLE == iota((near_rows, rows), 0), 1.0, 0.0
    ).astype(BF16)
    spec_ref[...] = jnp.zeros(spec_ref.shape, BF16)
    for (_, source, near_ref, slot, kind), copy in zip(places, copies):
        copy.wait()
        whole = buffer[source].astype(F32)
        kept = dot_nn(gather, jnp.where(middle, whole, 0.0).astype(BF16))
        near_ref[slot * near_rows : (slot + 1) * near_rows, :] = kept.astype(BF16)
        step = UPPER // MIDDLE
        top = jnp.where(index % step == offsets // MIDDLE, kept, 0.0)
        top = top.reshape(spec_rows, step, width).sum(axis=1)
        pad = jnp.zeros((SPEC_PAD - spec_rows, width), F32)
        spec_ref[kind * SPEC_PAD : (kind + 1) * SPEC_PAD, :] = jnp.concatenate(
            [top, pad], axis=0
        ).astype(BF16)


def split_terms(value):
    terms = []
    for _ in range(3):
        terms.append(value.astype(BF16).astype(F32))
        value = value - terms[-1]
    return terms


def next_refs(refs, rows):
    near_rows = 2 * (rows // MIDDLE)
    near = []
    for low in range(2 * rows, refs[0].shape[0], near_rows):
        near += [r.at[low : low + near_rows] for r in refs]
    return [r.at[:rows] for r in refs], [r.at[rows : 2 * rows] for r in refs], near


def key_value_refs(refs):
    keys, values, near = next_refs(refs[4:], refs[0].shape[0])
    return [refs[0], refs[2]] + keys, [refs[1], refs[3]] + values, near


def chunks(refs, rows):
    first, second = refs
    pieces = []
    for low in range(0, first.shape[0], rows):
        pieces += [first.at[low : low + rows], second.at[low : low + rows]]
    return pieces


def near_part(near_refs, slot, lanes):
    rows = near_refs[0].shape[0] // 2
    return jnp.concatenate([r[slot * rows : (slot + 1) * rows, lanes] for r in near_refs], axis=0)


def merge_kernel(first_ref, second_ref, _, out_ref):
    rows = first_ref.shape[0]
    out_ref[:rows, :] = first_ref[...]
    out_ref[rows:, :] = second_ref[...]


def softmax_terms(scores, inners, weights, top, total, product):
    new_top = top
    for part in scores:
        peak = jnp.max(part, axis=0, keepdims=True)
        new_top = peak if new_top is None else jnp.maximum(new_top, peak)
    if top is not None:
        scale = jnp.exp(top - new_top)
        total, product = total * scale, product * scale
    for part, inner, weight in zip(scores, inners, weights):
        probs = jnp.exp(part - new_top)
        if weight is not None:
            probs = weighted(probs, weight)
        part_total = jnp.sum(probs, axis=0, keepdims=True)
        part_product = jnp.sum(probs * inner, axis=0, keepdims=True)
        total = part_total if total is None else total + part_total
        product = part_product if product is None else product + part_product
    return new_top, total, product


def first_kernel(off_ref, q_ref, g_ref, *refs):
    kv_refs, out_ref = refs[:-1], refs[-1]
    rows, width = q_ref.shape
    heads = width // HD

    def products(head):
        lanes = pair_slice(head)
        query = one_head(q_ref[:, lanes], head, SCALE)
        grad = one_head(g_ref[:, lanes], head)
        scores = [dot_nt(r[:, lanes], query) for r in kv_refs[::2]]
        return scores, [dot_nt(r[:, lanes], grad) for r in kv_refs[1::2]]

    ahead = products(0)
    for head in range(heads):
        (scores, inners), ahead = ahead, products(head + 1) if head + 1 < heads else None
        weight = pair_weights(rows, off_ref[head] % MIDDLE)
        terms = softmax_terms(scores, inners, [weight] * len(scores), None, None, None)
        for index, term in enumerate(terms):
            row = index * heads + head
            out_ref[row : row + 1, :] = term


def forward_kernel(near_count, off_ref, q_ref, g_ref, known_ref, spec_ref, own_near_ref, *refs):
    k_refs, v_refs, near_refs = next_refs(refs[:-2], q_ref.shape[0])
    out_ref, far_ref = refs[-2:]
    rows, width = q_ref.shape
    heads = width // HD
    terms = []

    def products(head):
        lanes = pair_slice(head)
        query = one_head(q_ref[:, lanes], head, SCALE)
        grad = one_head(g_ref[:, lanes], head)
        keys, values = [r[:, lanes] for r in k_refs], [r[:, lanes] for r in v_refs]
        if near_count:
            keys.append(near_part(near_refs, 0, lanes))
            values.append(near_part(near_refs, 1, lanes))
        return [dot_nt(key, query) for key in keys], [dot_nt(value, grad) for value in values]

    ahead = products(0)
    for head in range(heads):
        (scores, inners), ahead = ahead, products(head + 1) if head + 1 < heads else None
        middle_offset = off_ref[head] % MIDDLE
        weights = [pair_weights(rows, middle_offset)] * len(k_refs)
        if near_count:
            chosen = iota((1, rows), 1) % MIDDLE == middle_offset
            scores[-1] = jnp.where(chosen, scores[-1], LOW)
            weights.append(None)
        known = [known_ref[i * heads + head : i * heads + head + 1, :] for i in range(3)]
        terms.append(softmax_terms(scores, inners, weights, *known))
    top, total, product = [jnp.concatenate(lines, axis=0) for lines in zip(*terms)]
    pad = jnp.zeros((STAT_ROWS - 2 * heads, rows), F32)
    stats = jnp.concatenate([top + jnp.log(total), product / total, pad], axis=0)
    out_ref[:, :rows] = stats
    offsets = row_offsets(off_ref, heads)
    token = iota((STAT_ROWS, rows), 1)
    spec_rows = rows // UPPER
    lane = iota((STAT_ROWS, width), 1)
    row = iota((STAT_ROWS, width), 0)
    place = iota((1, width), 1) % HD
    lines = [
        spec_ref[kind * SPEC_PAD : kind * SPEC_PAD + spec_rows, :].astype(F32) for kind in range(4)
    ]
    for index in range(spec_rows):
        value = jnp.sum(
            jnp.where(token == offsets + index * UPPER, stats, 0.0), axis=1, keepdims=True
        )
        line = jnp.zeros((1, width), F32)
        for kind in range(2):
            spread = jnp.sum(
                jnp.where(lane // HD + kind * heads == row, value, 0.0), axis=0, keepdims=True
            )
            for index_of, term in enumerate(split_terms(spread)):
                line = jnp.where(place == 3 * kind + index_of, term, line)
        lines.append(line)
    lines.append(jnp.zeros((STAT_ROWS - 5 * spec_rows, width), F32))
    block = jnp.concatenate(lines, axis=0)
    out_ref[:, rows:] = block
    near_rows = own_near_ref.shape[0]
    far_ref[:near_rows, :] = own_near_ref[...]
    far_ref[near_rows : near_rows + STAT_ROWS, :] = block.astype(BF16)
    kept = jnp.where(token % MIDDLE == offsets % MIDDLE, stats, 0.0)
    gather = jnp.where(iota((rows, PAIR), 0) // MIDDLE == iota((rows, PAIR), 1), 1.0, 0.0)
    gather = gather.astype(BF16)
    for index, term in enumerate(split_terms(kept)):
        far_ref[near_rows + STAT_ROWS :, index * PAIR : (index + 1) * PAIR] = dot_nn(
            term.astype(BF16), gather
        ).astype(BF16)


def query_kernel(near_count, off_ref, qg_ref, spec_in, pay_ref, *refs):
    k_refs, v_refs, near_refs = key_value_refs(refs[:KV_ARRAYS])
    dq_ref, spec_ref = refs[-2:]
    rows, width = k_refs[0].shape
    heads = width // HD
    spec_rows = rows // UPPER
    full = rows + SPEC_PAD
    columns = jnp.transpose(pay_ref[:, :rows])
    offsets = lane_offsets(off_ref, heads, width)
    column = iota((1, STAT_ROWS), 1)
    column_offsets = jnp.zeros((1, STAT_ROWS), jnp.int32)
    for head in range(heads):
        column_offsets = jnp.where(
            (column == head) | (column == head + heads), off_ref[head], column_offsets
        )
    token = iota((rows, STAT_ROWS), 0)
    lines = [
        jnp.sum(
            jnp.where(token == column_offsets + index * UPPER, columns, 0.0),
            axis=0,
            keepdims=True,
        )
        for index in range(spec_rows)
    ]
    lines.append(jnp.zeros((SPEC_PAD - spec_rows, STAT_ROWS), F32))
    columns = jnp.concatenate([columns] + lines, axis=0)
    for pair in range(heads // 2):
        lanes = slice(pair * PAIR, (pair + 1) * PAIR)
        both_q = jnp.concatenate([qg_ref[:rows, lanes], spec_in[:SPEC_PAD, lanes]], axis=0)
        both_g = jnp.concatenate([qg_ref[rows:, lanes], spec_in[3 * SPEC_PAD :, lanes]], axis=0)
        keys = [r[:, lanes] for r in k_refs]
        if near_count:
            keys.append(near_part(near_refs, 0, lanes))
        every_key = jnp.concatenate(keys, axis=0)
        results = []
        for head in (2 * pair, 2 * pair + 1):
            middle_offset = off_ref[head] % MIDDLE
            row = iota((full, 1), 0)
            chosen = (row % MIDDLE == middle_offset) | (row >= rows)
            weight = pair_weights(rows, middle_offset)
            row_weight = jnp.where(iota((1, rows), 1) % MIDDLE == middle_offset, 2.0, 1.0)
            query = one_head(both_q, head, SCALE)
            grad = one_head(both_g, head)
            log_sum = columns[:, head : head + 1]
            dot = columns[:, heads + head : heads + head + 1]
            parts = []
            for key, v_ref in zip(keys, v_refs):
                probs = jnp.exp(dot_nt(query, key) - log_sum)
                probs = jnp.concatenate(
                    [weighted(probs[:rows], weight), probs[rows:] * row_weight], axis=0
                )
                inner = dot_nt(grad, v_ref[:, lanes]) - dot
                parts.append(
                    jnp.concatenate([(probs * inner).astype(BF16), probs[rows:].astype(BF16)], axis=0)
                )
            if near_count:
                scores = jnp.where(chosen, dot_nt(query, keys[-1]), LOW)
                probs = jnp.exp(scores - log_sum)
                inner = dot_nt(grad, near_part(near_refs, 1, lanes)) - dot
                parts.append(
                    jnp.concatenate([(probs * inner).astype(BF16), probs[rows:].astype(BF16)], axis=0)
                )
            results.append(dot_nn(jnp.concatenate(parts, axis=1), every_key))
        result = jnp.where(half_mask(0), results[0], results[1]) * SCALE
        special = iota((rows, PAIR), 0) % UPPER == offsets[:, lanes]
        dq_ref[:, lanes] = jnp.where(special, 0.0, result[:rows])
        spec_ref[:spec_rows, lanes] = result[rows : rows + spec_rows]
        spec_ref[spec_rows:, lanes] = result[full : full + spec_rows]


def stack_kernel(first_ref, *refs):
    out, low = refs[-1], 0
    for ref in refs[:-1]:
        rows = ref.shape[0]
        out[low : low + rows, :] = ref[...]
        low += rows


def far_chunks(tok_rows, refs):
    return chunks(refs, 2 * (tok_rows // MIDDLE) + 2 * STAT_ROWS) if refs else []


def relay_kernel(first_ref, second_ref, *refs):
    pay_refs, far_refs = refs[:2], refs[2:-2]
    for parts, out in zip((pay_refs, far_refs), refs[-2:]):
        for index, ref in enumerate(parts):
            rows = ref.shape[0]
            out[index * rows : (index + 1) * rows, :] = ref[...]


def copy_kernel(_, in_ref, out_ref):
    out_ref[...] = in_ref[...]


def key_kernel(near_count, off_ref, k_ref, v_ref, *refs):
    dk_ref, dv_ref = refs[-2:]
    rows, width = k_ref.shape
    heads = width // HD
    near_rows = rows // MIDDLE
    if len(refs) == 4:
        qg_refs, pay_refs, known_refs = refs[:1], refs[1:2], None
    else:
        qg_refs = refs[: GROUP - 1]
        pay_refs = chunks(refs[GROUP - 1 : GROUP + 1], STAT_ROWS)[1:]
        far_refs = far_chunks(k_ref.shape[0], refs[GROUP + 1 : -4])
        known_refs = refs[-4:-2]
    if near_count:
        first = 2 * near_rows + STAT_ROWS
        far_stats = []
        for r in far_refs:
            lines = r[first : first + STAT_ROWS, :].astype(F32)
            line = lines[:, :PAIR] + lines[:, PAIR : 2 * PAIR] + lines[:, 2 * PAIR : 3 * PAIR]
            far_stats.append(line[:, :near_rows])
        far_stats = jnp.concatenate(far_stats, axis=1)
    for pair in range(heads // 2):
        lanes = slice(pair * PAIR, (pair + 1) * PAIR)
        queries = [r[:rows, lanes] for r in qg_refs]
        grads = [r[rows:, lanes] for r in qg_refs]
        if near_count:
            queries.append(
                jnp.concatenate([r[:near_rows, lanes] for r in far_refs], axis=0)
            )
            grads.append(
                jnp.concatenate([r[near_rows : 2 * near_rows, lanes] for r in far_refs], axis=0)
            )
        every_query = jnp.concatenate(queries, axis=0)
        every_grad = jnp.concatenate(grads, axis=0)
        key_grads, value_grads = [], []
        for head in (2 * pair, 2 * pair + 1):
            middle_offset = off_ref[head] % MIDDLE
            chosen = iota((rows, 1), 0) % MIDDLE == middle_offset
            weight = pair_weights(rows, middle_offset)
            keys = one_head(k_ref[:, lanes], head, SCALE)
            values = one_head(v_ref[:, lanes], head)
            special = iota((1, rows), 1) % UPPER == off_ref[head]
            prob_parts, score_parts = [], []
            for query, grad, pay_ref in zip(queries, grads, pay_refs):
                log_sum = jnp.where(special, HIGH, pay_ref[head : head + 1, :rows])
                dot = pay_ref[heads + head : heads + head + 1, :rows]
                probs = weighted(jnp.exp(dot_nt(keys, query) - log_sum), weight)
                inner = dot_nt(values, grad) - dot
                prob_parts.append(probs.astype(BF16))
                score_parts.append((probs * inner).astype(BF16))
            if near_count:
                count = near_count * near_rows
                special = iota((1, count), 1) % (UPPER // MIDDLE) == off_ref[head] // MIDDLE
                log_sum = jnp.where(special, HIGH, far_stats[head : head + 1, :])
                dot = far_stats[heads + head : heads + head + 1, :]
                scores = jnp.where(chosen, dot_nt(keys, queries[-1]), LOW)
                probs = jnp.exp(scores - log_sum)
                inner = dot_nt(values, grads[-1]) - dot
                prob_parts.append(probs.astype(BF16))
                score_parts.append((probs * inner).astype(BF16))
            key_grads.append(dot_nn(jnp.concatenate(score_parts, axis=1), every_query))
            value_grads.append(dot_nn(jnp.concatenate(prob_parts, axis=1), every_grad))
        low = half_mask(0)
        grad_k = jnp.where(low, key_grads[0], key_grads[1]) * SCALE
        grad_v = jnp.where(low, value_grads[0], value_grads[1])
        if known_refs:
            grad_k = grad_k + known_refs[0][:, lanes]
            grad_v = grad_v + known_refs[1][:, lanes]
        dk_ref[:, lanes] = grad_k
        dv_ref[:, lanes] = grad_v


def collect_kernel(tok_rows, *refs):
    out_ref = refs[-1]
    pay_refs = chunks(refs[:2], STAT_ROWS)
    far_refs = far_chunks(tok_rows, refs[2:-1])
    spec_rows = tok_rows // UPPER
    first = 2 * (tok_rows // MIDDLE)
    count = spec_rows * (len(pay_refs) + len(far_refs))
    blocks = [r[:, tok_rows:] for r in pay_refs]
    blocks += [r[first : first + STAT_ROWS, :].astype(F32) for r in far_refs]
    for kind in range(5):
        lines = [b[kind * spec_rows : (kind + 1) * spec_rows] for b in blocks]
        out_ref[kind * count : (kind + 1) * count, :] = jnp.concatenate(lines, axis=0).astype(BF16)


def special_kernel(slots, off_ref, k_ref, v_ref, dq_in, spec_ref, dk_in, dv_in, *refs):
    blocks = refs[:-3]
    dq_ref, dk_ref, dv_ref = refs[-3:]
    rows, width = k_ref.shape
    heads = width // HD
    spec_rows = rows // UPPER
    count = slots * spec_rows
    every = count * len(blocks)
    offsets = lane_offsets(off_ref, heads, width)

    def kind(index, lanes):
        return jnp.concatenate(
            [b[index * count : (index + 1) * count, lanes] for b in blocks], axis=0
        )

    def two(block, scale=1.0):
        return jnp.concatenate([one_head(block, 0, scale), one_head(block, 1, scale)], axis=0)

    column = iota((1, 2 * every), 1)
    second = column >= every
    column = column % every
    same_group = jnp.where(column < GROUP * spec_rows, 1.0, 0.0)
    same_segment = jnp.where(column < count, 1.0, 0.0)
    row = iota((rows, 1), 0)
    low = half_mask(0)
    place = iota((8, PAIR), 1) % HD
    first_term = jnp.where(iota((8, PAIR), 0) == 0, 0, 3)
    picks = jnp.where((place >= first_term) & (place < first_term + 3), 1.0, 0.0).astype(BF16)
    every_product = []
    for pair in range(heads // 2):
        lanes = slice(pair * PAIR, (pair + 1) * PAIR)
        all_q, all_k, all_v, all_g, all_s = [kind(index, lanes) for index in range(5)]
        query, grad = two(all_q, SCALE), two(all_g)
        known = dot_nt(picks, two(all_s))
        scores, inner = dot_nt(all_k, query), dot_nt(all_v, grad)
        own = dot_nt(k_ref[:, lanes], query), dot_nt(v_ref[:, lanes], grad)
        every_product.append((lanes, query, grad, all_k, known, scores, inner, own))
    states = []
    for lanes, query, grad, all_k, known, scores, inner, own in every_product:
        known_sum, known_dot = known[0:1], known[1:2]
        top = jnp.max(scores, axis=0, keepdims=True)
        weights = jnp.exp(scores - top)
        total = jnp.sum(weights, axis=0, keepdims=True)
        product = jnp.sum(weights * inner, axis=0, keepdims=True) / total
        log_sum = top + jnp.log(total)
        most = jnp.maximum(known_sum, log_sum)
        joint = most + jnp.log(jnp.exp(known_sum - most) + jnp.exp(log_sum - most))
        share = jnp.exp(known_sum - joint)
        dot = known_dot * share + product * jnp.exp(log_sum - joint)
        change = known_dot - dot
        states.append((lanes, query, grad, all_k, scores, inner, own, joint, share, dot, change))
    for pair, state in enumerate(states):
        lanes, query, grad, _, _, _, own, joint, _, dot, _ = state
        offset = jnp.where(second, off_ref[2 * pair + 1], off_ref[2 * pair])
        middle = row % MIDDLE == offset % MIDDLE
        upper = row % UPPER == offset
        weight = same_group + jnp.where(middle, same_segment, 0.0) + jnp.where(upper, 1.0, 0.0)
        scores = jnp.where(weight > 0.0, own[0], LOW)
        probs = jnp.exp(scores - joint) * weight
        inner = own[1] - dot
        dk_ref[:, lanes] = (
            dk_in[:, lanes] + dot_nn((probs * inner).astype(BF16), query)
        ).astype(BF16)
        dv_ref[:, lanes] = (dv_in[:, lanes] + dot_nn(probs.astype(BF16), grad)).astype(BF16)
    for lanes, _, _, all_k, scores, inner, _, joint, share, dot, change in states:
        probs = jnp.exp(scores - joint)
        grad_q = SCALE * lax.dot_general(
            (probs * (inner - dot)).astype(BF16),
            all_k,
            (((0,), (0,)), ((), ())),
            preferred_element_type=F32,
        )
        lines = []
        for index in range(spec_rows):
            other = every + index
            ratio = jnp.where(low, share[:, index : index + 1], share[:, other : other + 1])
            moved = jnp.where(low, change[:, index : index + 1], change[:, other : other + 1])
            top_q = jnp.where(low, grad_q[index : index + 1], grad_q[other : other + 1])
            near_q = spec_ref[index : index + 1, lanes]
            key_sum = spec_ref[spec_rows + index : spec_rows + index + 1, lanes]
            line = ratio * (near_q + moved * key_sum) + top_q
            lines.append(jnp.broadcast_to(line, (UPPER, PAIR)))
        special = row % UPPER == offsets[:, lanes]
        dq_ref[:, lanes] = (
            dq_in[:, lanes] + jnp.where(special, jnp.concatenate(lines, axis=0), 0.0)
        ).astype(BF16)


def call(kernel, outs, *arrays, us=1.0, raw=False, scratch=(), vmem_mib=40):
    smem = pl.BlockSpec(memory_space=pltpu.SMEM)
    vmem = pl.BlockSpec(memory_space=pltpu.VMEM)
    space = pl.BlockSpec(memory_space=pltpu.HBM) if raw else vmem
    specs = [smem if a.dtype == jnp.int32 and not raw else space for a in arrays]
    return pl.pallas_call(
        kernel,
        out_shape=tuple(jax.ShapeDtypeStruct(shape, dtype) for shape, dtype in outs),
        in_specs=specs,
        out_specs=tuple(vmem for _ in outs),
        scratch_shapes=scratch,
        cost_estimate=pl.CostEstimate(
            flops=int(us * 1.15e9), bytes_accessed=0, transcendentals=0
        ),
        compiler_params=pltpu.CompilerParams(vmem_limit_bytes=vmem_mib * 1024 * 1024),
    )(*arrays)


def across(value, axis, mask):
    size = lax.axis_size(axis)
    return lax.ppermute(value, axis, [(source, source ^ mask) for source in range(size)])


def local(queries, key_matrix, value_matrix, grad_out, offsets):
    rows, width = queries.shape
    slots, outer = lax.axis_size("ctxb"), lax.axis_size("ctxa")
    near_count = slots - GROUP
    near_rows, spec_rows = rows // MIDDLE, rows // UPPER

    next_k, next_v = across(key_matrix, "ctxb", 2), across(value_matrix, "ctxb", 2)
    core_k, core_v = across(key_matrix, "ctxb", 1), across(value_matrix, "ctxb", 1)
    near_kv, near_qg, spec = call(
        pack_kernel,
        [
            ((2 * near_rows, width), BF16),
            ((2 * near_rows, width), BF16),
            ((4 * SPEC_PAD, width), BF16),
        ],
        offsets, queries, key_matrix, value_matrix, grad_out,
        us=1.3, raw=True, vmem_mib=60,
        scratch=[
            pltpu.SMEM(offsets.shape, jnp.int32),
            pltpu.VMEM((4, rows, width), BF16),
            pltpu.SemaphoreType.DMA((4,)),
            pltpu.SemaphoreType.DMA,
        ],
    )
    near_came = [across(near_kv, "ctxb", mask) for mask in reversed(range(GROUP, slots, 2))]
    both = [((2 * rows, width), BF16)]
    own_kv = [key_matrix, value_matrix, core_k, core_v]
    term_rows = -(-3 * (width // HD) // 8) * 8
    (known,) = call(
        first_kernel, [((term_rows, rows), F32)],
        offsets, queries, grad_out, *own_kv, us=2.2,
    )
    (stacked,) = call(
        stack_kernel,
        [((2 * rows + 2 * near_rows * len(near_came), width), BF16)],
        known, next_k, next_v, *near_came, us=0.2,
    )
    kv_parts = own_kv + [stacked, across(stacked, "ctxb", 1)]
    (qg,) = call(merge_kernel, both, queries, grad_out, near_came[0], us=0.3)
    next_qg = across(qg, "ctxb", 2)
    core_qg = across(qg, "ctxb", 1)
    pay, far = call(
        partial(forward_kernel, near_count),
        [
            ((STAT_ROWS, rows + width), F32),
            ((2 * near_rows + 2 * STAT_ROWS, width), BF16),
        ],
        offsets, queries, grad_out, known, spec, near_qg, *kv_parts[4:], us=2.5,
    )
    dq, dq_spec = call(
        partial(query_kernel, near_count),
        [((rows, width), F32), ((2 * spec_rows, width), F32)],
        offsets, qg, spec, pay, *kv_parts, us=5.0,
    )
    pays_far = [pay, across(pay, "ctxb", 2)]
    far_came = [across(far, "ctxb", mask) for mask in reversed(range(GROUP, slots, 2))]
    grads = [((rows, width), F32)] * 2
    own_dk, own_dv = call(
        partial(key_kernel, 0), grads, offsets, key_matrix, value_matrix, qg, pay, us=1.3,
    )
    held = call(
        relay_kernel,
        [
            ((2 * STAT_ROWS, rows + width), F32),
            ((far.shape[0] * len(far_came), width), BF16),
        ],
        dq_spec, own_dk, *pays_far, *far_came, us=0.3,
    )
    pays, fars = [(part, across(part, "ctxb", 1)) for part in held]
    (block,) = call(
        partial(collect_kernel, rows), [((5 * slots * spec_rows, width), BF16)], *pays, *fars,
        us=0.3,
    )
    (next_qg,) = call(copy_kernel, [((2 * rows, width), BF16)], block, next_qg, us=0.2)
    qg_parts = [qg, core_qg, next_qg, across(next_qg, "ctxb", 1)]
    blocks = [block] + [across(block, "ctxa", mask) for mask in reversed(range(1, outer))]
    dk, dv = call(
        partial(key_kernel, near_count),
        grads,
        offsets, key_matrix, value_matrix, *qg_parts[1:], *pays, *fars, own_dk, own_dv, us=4.0,
    )
    return call(
        partial(special_kernel, slots),
        [((rows, width), BF16)] * 3,
        offsets, key_matrix, value_matrix, dq, dq_spec, dk, dv, *blocks, us=3.0,
    )


def solution(mesh):
    split = P(("ctxa", "ctxb"), None)
    return jax.shard_map(
        local,
        mesh=mesh,
        in_specs=(split, split, split, split, P()),
        out_specs=(split, split, split),
        check_vma=False,
    )
```

```python
from functools import partial

import jax
import jax.numpy as jnp
from jax import lax
from jax.experimental import pallas as pl
from jax.experimental.pallas import tpu as pltpu
from jax.sharding import PartitionSpec as P

HD = 64
PAIR = 2 * HD
GROUP = 4
MIDDLE = 8
UPPER = 128
LOW = -1e30
HIGH = 1e30
SCALE = HD**-0.5
F32 = jnp.float32
BF16 = jnp.bfloat16
STAT_ROWS = 16
SPEC_PAD = 16
KV_ARRAYS = 6


def iota(shape, dim):
    return lax.broadcasted_iota(jnp.int32, shape, dim)


def dot_nt(a, b):
    return lax.dot_general(a, b, (((1,), (1,)), ((), ())), preferred_element_type=F32)


def dot_nn(a, b):
    return jnp.dot(a, b, preferred_element_type=F32)


def pair_slice(head):
    low = head // 2 * PAIR
    return slice(low, low + PAIR)


def half_mask(head):
    return iota((1, PAIR), 1) // HD == head % 2


def one_head(block, head, scale=1.0):
    return jnp.where(half_mask(head), block.astype(F32) * scale, 0.0).astype(BF16)


def lane_offsets(off_ref, heads, width):
    lane_head = iota((1, width), 1) // HD
    out = jnp.zeros((1, width), jnp.int32)
    for head in range(heads):
        out = jnp.where(lane_head == head, off_ref[head], out)
    return out


def row_offsets(off_ref, heads):
    rows = iota((STAT_ROWS, 1), 0)
    out = jnp.zeros((STAT_ROWS, 1), jnp.int32)
    for head in range(heads):
        out = jnp.where((rows == head) | (rows == head + heads), off_ref[head], out)
    return out


def pair_weights(columns, middle_offset):
    both = (iota((MIDDLE, columns), 0) == middle_offset) & (
        iota((MIDDLE, columns), 1) % MIDDLE == middle_offset
    )
    return jnp.where(both, 2.0, 1.0)


def weighted(probs, weight):
    rows, columns = probs.shape
    tiles = probs.reshape(rows // MIDDLE, MIDDLE, columns)
    return (tiles * weight[None]).reshape(rows, columns)


def keep_rows(off_ref, read, near_ref, spec_ref):
    near_rows, width = near_ref.shape[0] // 2, near_ref.shape[1]
    rows, heads = near_rows * MIDDLE, width // HD
    spec_rows, step = rows // UPPER, UPPER // MIDDLE
    offsets = lane_offsets(off_ref, heads, width)
    middle = iota((rows, width), 0) % MIDDLE == offsets % MIDDLE
    index = iota((near_rows, width), 0)
    gather = jnp.where(
        iota((near_rows, rows), 1) // MIDDLE == iota((near_rows, rows), 0), 1.0, 0.0
    ).astype(BF16)
    for slot in range(2):
        whole = read(slot).astype(F32)
        kept = dot_nn(gather, jnp.where(middle, whole, 0.0).astype(BF16))
        near_ref[slot * near_rows : (slot + 1) * near_rows, :] = kept.astype(BF16)
        top = jnp.where(index % step == offsets // MIDDLE, kept, 0.0)
        top = top.reshape(spec_rows, step, width).sum(axis=1)
        pad = jnp.zeros((SPEC_PAD - spec_rows, width), F32)
        spec_ref[slot * SPEC_PAD : (slot + 1) * SPEC_PAD, :] = jnp.concatenate(
            [top, pad], axis=0
        ).astype(BF16)


def pack_kernel(off_in, k_ref, v_ref, near_ref, spec_ref, off_ref, buffer, sems, off_sem):
    copies = [
        pltpu.make_async_copy(source, buffer.at[index], sems.at[index])
        for index, source in enumerate((k_ref, v_ref))
    ]
    off_copy = pltpu.make_async_copy(off_in, off_ref, off_sem)
    off_copy.start()
    for copy in copies:
        copy.start()
    off_copy.wait()

    def read(slot):
        copies[slot].wait()
        return buffer[slot]

    keep_rows(off_ref, read, near_ref, spec_ref)


def choose_kernel(off_ref, q_ref, g_ref, near_ref, spec_ref):
    keep_rows(off_ref, lambda slot: (q_ref, g_ref)[slot][...], near_ref, spec_ref)


def split_terms(value):
    terms = []
    for _ in range(3):
        terms.append(value.astype(BF16).astype(F32))
        value = value - terms[-1]
    return terms


def next_refs(refs, rows):
    near_rows = 2 * (rows // MIDDLE)
    near = []
    for low in range(2 * rows, refs[0].shape[0], near_rows):
        near += [r.at[low : low + near_rows] for r in refs]
    return [r.at[:rows] for r in refs], [r.at[rows : 2 * rows] for r in refs], near


def key_value_refs(refs):
    keys, values, near = next_refs(refs[4:], refs[0].shape[0])
    return [refs[0], refs[2]] + keys, [refs[1], refs[3]] + values, near


def chunks(refs, rows):
    first, second = refs
    pieces = []
    for low in range(0, first.shape[0], rows):
        pieces += [first.at[low : low + rows], second.at[low : low + rows]]
    return pieces


def near_part(near_refs, slot, lanes):
    rows = near_refs[0].shape[0] // 2
    return jnp.concatenate([r[slot * rows : (slot + 1) * rows, lanes] for r in near_refs], axis=0)


def merge_kernel(first_ref, second_ref, _, out_ref):
    rows = first_ref.shape[0]
    out_ref[:rows, :] = first_ref[...]
    out_ref[rows:, :] = second_ref[...]


def softmax_terms(scores, inners, weights, top, total, product):
    new_top = top
    for part in scores:
        peak = jnp.max(part, axis=0, keepdims=True)
        new_top = peak if new_top is None else jnp.maximum(new_top, peak)
    if top is not None:
        scale = jnp.exp(top - new_top)
        total, product = total * scale, product * scale
    for part, inner, weight in zip(scores, inners, weights):
        probs = jnp.exp(part - new_top)
        if weight is not None:
            probs = weighted(probs, weight)
        part_total = jnp.sum(probs, axis=0, keepdims=True)
        part_product = jnp.sum(probs * inner, axis=0, keepdims=True)
        total = part_total if total is None else total + part_total
        product = part_product if product is None else product + part_product
    return new_top, total, product


def first_kernel(off_ref, q_ref, g_ref, *refs):
    kv_refs, out_ref = refs[:-1], refs[-1]
    rows, width = q_ref.shape
    heads = width // HD

    def products(head):
        lanes = pair_slice(head)
        query = one_head(q_ref[:, lanes], head, SCALE)
        grad = one_head(g_ref[:, lanes], head)
        scores = [dot_nt(r[:, lanes], query) for r in kv_refs[::2]]
        return scores, [dot_nt(r[:, lanes], grad) for r in kv_refs[1::2]]

    ahead = products(0)
    for head in range(heads):
        (scores, inners), ahead = ahead, products(head + 1) if head + 1 < heads else None
        weight = pair_weights(rows, off_ref[head] % MIDDLE)
        terms = softmax_terms(scores, inners, [weight] * len(scores), None, None, None)
        for index, term in enumerate(terms):
            row = index * heads + head
            out_ref[row : row + 1, :] = term


def forward_kernel(near_count, off_ref, q_ref, g_ref, known_ref, kv_ref, qg_ref, own_near_ref, *refs):
    k_refs, v_refs, near_refs = next_refs(refs[:-2], q_ref.shape[0])
    out_ref, far_ref = refs[-2:]
    rows, width = q_ref.shape
    heads = width // HD
    terms = []

    def products(head):
        lanes = pair_slice(head)
        query = one_head(q_ref[:, lanes], head, SCALE)
        grad = one_head(g_ref[:, lanes], head)
        keys, values = [r[:, lanes] for r in k_refs], [r[:, lanes] for r in v_refs]
        if near_count:
            keys.append(near_part(near_refs, 0, lanes))
            values.append(near_part(near_refs, 1, lanes))
        return [dot_nt(key, query) for key in keys], [dot_nt(value, grad) for value in values]

    ahead = products(0)
    for head in range(heads):
        (scores, inners), ahead = ahead, products(head + 1) if head + 1 < heads else None
        middle_offset = off_ref[head] % MIDDLE
        weights = [pair_weights(rows, middle_offset)] * len(k_refs)
        if near_count:
            chosen = iota((1, rows), 1) % MIDDLE == middle_offset
            scores[-1] = jnp.where(chosen, scores[-1], LOW)
            weights.append(None)
        known = [known_ref[i * heads + head : i * heads + head + 1, :] for i in range(3)]
        terms.append(softmax_terms(scores, inners, weights, *known))
    top, total, product = [jnp.concatenate(lines, axis=0) for lines in zip(*terms)]
    pad = jnp.zeros((STAT_ROWS - 2 * heads, rows), F32)
    stats = jnp.concatenate([top + jnp.log(total), product / total, pad], axis=0)
    out_ref[:, :rows] = stats
    offsets = row_offsets(off_ref, heads)
    token = iota((STAT_ROWS, rows), 1)
    spec_rows = rows // UPPER
    lane = iota((STAT_ROWS, width), 1)
    row = iota((STAT_ROWS, width), 0)
    place = iota((1, width), 1) % HD
    lines = [
        ref[slot * SPEC_PAD : slot * SPEC_PAD + spec_rows, :].astype(F32)
        for ref, slot in ((qg_ref, 0), (kv_ref, 0), (kv_ref, 1), (qg_ref, 1))
    ]
    for index in range(spec_rows):
        value = jnp.sum(
            jnp.where(token == offsets + index * UPPER, stats, 0.0), axis=1, keepdims=True
        )
        line = jnp.zeros((1, width), F32)
        for kind in range(2):
            spread = jnp.sum(
                jnp.where(lane // HD + kind * heads == row, value, 0.0), axis=0, keepdims=True
            )
            for index_of, term in enumerate(split_terms(spread)):
                line = jnp.where(place == 3 * kind + index_of, term, line)
        lines.append(line)
    lines.append(jnp.zeros((STAT_ROWS - 5 * spec_rows, width), F32))
    block = jnp.concatenate(lines, axis=0)
    out_ref[:, rows:] = block
    near_rows = own_near_ref.shape[0]
    far_ref[:near_rows, :] = own_near_ref[...]
    far_ref[near_rows : near_rows + STAT_ROWS, :] = block.astype(BF16)
    kept = jnp.where(token % MIDDLE == offsets % MIDDLE, stats, 0.0)
    gather = jnp.where(iota((rows, PAIR), 0) // MIDDLE == iota((rows, PAIR), 1), 1.0, 0.0)
    gather = gather.astype(BF16)
    for index, term in enumerate(split_terms(kept)):
        far_ref[near_rows + STAT_ROWS :, index * PAIR : (index + 1) * PAIR] = dot_nn(
            term.astype(BF16), gather
        ).astype(BF16)


def query_kernel(near_count, off_ref, qg_ref, spec_in, pay_ref, *refs):
    k_refs, v_refs, near_refs = key_value_refs(refs[:KV_ARRAYS])
    dq_ref, spec_ref = refs[-2:]
    rows, width = k_refs[0].shape
    heads = width // HD
    spec_rows = rows // UPPER
    full = rows + SPEC_PAD
    columns = jnp.transpose(pay_ref[:, :rows])
    offsets = lane_offsets(off_ref, heads, width)
    column = iota((1, STAT_ROWS), 1)
    column_offsets = jnp.zeros((1, STAT_ROWS), jnp.int32)
    for head in range(heads):
        column_offsets = jnp.where(
            (column == head) | (column == head + heads), off_ref[head], column_offsets
        )
    token = iota((rows, STAT_ROWS), 0)
    lines = [
        jnp.sum(
            jnp.where(token == column_offsets + index * UPPER, columns, 0.0),
            axis=0,
            keepdims=True,
        )
        for index in range(spec_rows)
    ]
    lines.append(jnp.zeros((SPEC_PAD - spec_rows, STAT_ROWS), F32))
    columns = jnp.concatenate([columns] + lines, axis=0)
    for pair in range(heads // 2):
        lanes = slice(pair * PAIR, (pair + 1) * PAIR)
        both_q = jnp.concatenate([qg_ref[:rows, lanes], spec_in[:SPEC_PAD, lanes]], axis=0)
        both_g = jnp.concatenate([qg_ref[rows:, lanes], spec_in[SPEC_PAD:, lanes]], axis=0)
        keys = [r[:, lanes] for r in k_refs]
        if near_count:
            keys.append(near_part(near_refs, 0, lanes))
        every_key = jnp.concatenate(keys, axis=0)
        results = []
        for head in (2 * pair, 2 * pair + 1):
            middle_offset = off_ref[head] % MIDDLE
            row = iota((full, 1), 0)
            chosen = (row % MIDDLE == middle_offset) | (row >= rows)
            weight = pair_weights(rows, middle_offset)
            row_weight = jnp.where(iota((1, rows), 1) % MIDDLE == middle_offset, 2.0, 1.0)
            query = one_head(both_q, head, SCALE)
            grad = one_head(both_g, head)
            log_sum = columns[:, head : head + 1]
            dot = columns[:, heads + head : heads + head + 1]
            parts = []
            for key, v_ref in zip(keys, v_refs):
                probs = jnp.exp(dot_nt(query, key) - log_sum)
                probs = jnp.concatenate(
                    [weighted(probs[:rows], weight), probs[rows:] * row_weight], axis=0
                )
                inner = dot_nt(grad, v_ref[:, lanes]) - dot
                parts.append(
                    jnp.concatenate([(probs * inner).astype(BF16), probs[rows:].astype(BF16)], axis=0)
                )
            if near_count:
                scores = jnp.where(chosen, dot_nt(query, keys[-1]), LOW)
                probs = jnp.exp(scores - log_sum)
                inner = dot_nt(grad, near_part(near_refs, 1, lanes)) - dot
                parts.append(
                    jnp.concatenate([(probs * inner).astype(BF16), probs[rows:].astype(BF16)], axis=0)
                )
            results.append(dot_nn(jnp.concatenate(parts, axis=1), every_key))
        result = jnp.where(half_mask(0), results[0], results[1]) * SCALE
        special = iota((rows, PAIR), 0) % UPPER == offsets[:, lanes]
        dq_ref[:, lanes] = jnp.where(special, 0.0, result[:rows])
        spec_ref[:spec_rows, lanes] = result[rows : rows + spec_rows]
        spec_ref[spec_rows:, lanes] = result[full : full + spec_rows]


def stack_kernel(first_ref, second_ref, *refs):
    out, low = refs[-1], 0
    for ref in refs[:-1]:
        rows = ref.shape[0]
        out[low : low + rows, :] = ref[...]
        low += rows


def far_chunks(tok_rows, refs):
    return chunks(refs, 2 * (tok_rows // MIDDLE) + 2 * STAT_ROWS) if refs else []


def relay_kernel(first_ref, second_ref, *refs):
    pay_refs, far_refs = refs[:2], refs[2:-2]
    for parts, out in zip((pay_refs, far_refs), refs[-2:]):
        for index, ref in enumerate(parts):
            rows = ref.shape[0]
            out[index * rows : (index + 1) * rows, :] = ref[...]


def copy_kernel(_, in_ref, out_ref):
    out_ref[...] = in_ref[...]


def key_kernel(near_count, off_ref, k_ref, v_ref, *refs):
    dk_ref, dv_ref = refs[-2:]
    rows, width = k_ref.shape
    heads = width // HD
    near_rows = rows // MIDDLE
    if len(refs) == 4:
        qg_refs, pay_refs, known_refs = refs[:1], refs[1:2], None
    else:
        qg_refs = refs[: GROUP - 1]
        pay_refs = chunks(refs[GROUP - 1 : GROUP + 1], STAT_ROWS)[1:]
        far_refs = far_chunks(k_ref.shape[0], refs[GROUP + 1 : -4])
        known_refs = refs[-4:-2]
    if near_count:
        first = 2 * near_rows + STAT_ROWS
        far_stats = []
        for r in far_refs:
            lines = r[first : first + STAT_ROWS, :].astype(F32)
            line = lines[:, :PAIR] + lines[:, PAIR : 2 * PAIR] + lines[:, 2 * PAIR : 3 * PAIR]
            far_stats.append(line[:, :near_rows])
        far_stats = jnp.concatenate(far_stats, axis=1)
    for pair in range(heads // 2):
        lanes = slice(pair * PAIR, (pair + 1) * PAIR)
        queries = [r[:rows, lanes] for r in qg_refs]
        grads = [r[rows:, lanes] for r in qg_refs]
        if near_count:
            queries.append(
                jnp.concatenate([r[:near_rows, lanes] for r in far_refs], axis=0)
            )
            grads.append(
                jnp.concatenate([r[near_rows : 2 * near_rows, lanes] for r in far_refs], axis=0)
            )
        every_query = jnp.concatenate(queries, axis=0)
        every_grad = jnp.concatenate(grads, axis=0)
        key_grads, value_grads = [], []
        for head in (2 * pair, 2 * pair + 1):
            middle_offset = off_ref[head] % MIDDLE
            chosen = iota((rows, 1), 0) % MIDDLE == middle_offset
            weight = pair_weights(rows, middle_offset)
            keys = one_head(k_ref[:, lanes], head, SCALE)
            values = one_head(v_ref[:, lanes], head)
            special = iota((1, rows), 1) % UPPER == off_ref[head]
            prob_parts, score_parts = [], []
            for query, grad, pay_ref in zip(queries, grads, pay_refs):
                log_sum = jnp.where(special, HIGH, pay_ref[head : head + 1, :rows])
                dot = pay_ref[heads + head : heads + head + 1, :rows]
                probs = weighted(jnp.exp(dot_nt(keys, query) - log_sum), weight)
                inner = dot_nt(values, grad) - dot
                prob_parts.append(probs.astype(BF16))
                score_parts.append((probs * inner).astype(BF16))
            if near_count:
                count = near_count * near_rows
                special = iota((1, count), 1) % (UPPER // MIDDLE) == off_ref[head] // MIDDLE
                log_sum = jnp.where(special, HIGH, far_stats[head : head + 1, :])
                dot = far_stats[heads + head : heads + head + 1, :]
                scores = jnp.where(chosen, dot_nt(keys, queries[-1]), LOW)
                probs = jnp.exp(scores - log_sum)
                inner = dot_nt(values, grads[-1]) - dot
                prob_parts.append(probs.astype(BF16))
                score_parts.append((probs * inner).astype(BF16))
            key_grads.append(dot_nn(jnp.concatenate(score_parts, axis=1), every_query))
            value_grads.append(dot_nn(jnp.concatenate(prob_parts, axis=1), every_grad))
        low = half_mask(0)
        grad_k = jnp.where(low, key_grads[0], key_grads[1]) * SCALE
        grad_v = jnp.where(low, value_grads[0], value_grads[1])
        if known_refs:
            grad_k = grad_k + known_refs[0][:, lanes]
            grad_v = grad_v + known_refs[1][:, lanes]
        dk_ref[:, lanes] = grad_k
        dv_ref[:, lanes] = grad_v


def collect_kernel(tok_rows, *refs):
    out_ref = refs[-1]
    pay_refs = chunks(refs[:2], STAT_ROWS)
    far_refs = far_chunks(tok_rows, refs[2:-1])
    spec_rows = tok_rows // UPPER
    first = 2 * (tok_rows // MIDDLE)
    count = spec_rows * (len(pay_refs) + len(far_refs))
    blocks = [r[:, tok_rows:] for r in pay_refs]
    blocks += [r[first : first + STAT_ROWS, :].astype(F32) for r in far_refs]
    for kind in range(5):
        lines = [b[kind * spec_rows : (kind + 1) * spec_rows] for b in blocks]
        out_ref[kind * count : (kind + 1) * count, :] = jnp.concatenate(lines, axis=0).astype(BF16)


def special_kernel(slots, off_ref, k_ref, v_ref, dq_in, spec_ref, dk_in, dv_in, *refs):
    blocks = refs[:-3]
    dq_ref, dk_ref, dv_ref = refs[-3:]
    rows, width = k_ref.shape
    heads = width // HD
    spec_rows = rows // UPPER
    count = slots * spec_rows
    every = count * len(blocks)
    offsets = lane_offsets(off_ref, heads, width)

    def kind(index, lanes):
        return jnp.concatenate(
            [b[index * count : (index + 1) * count, lanes] for b in blocks], axis=0
        )

    def two(block, scale=1.0):
        return jnp.concatenate([one_head(block, 0, scale), one_head(block, 1, scale)], axis=0)

    column = iota((1, 2 * every), 1)
    second = column >= every
    column = column % every
    same_group = jnp.where(column < GROUP * spec_rows, 1.0, 0.0)
    same_segment = jnp.where(column < count, 1.0, 0.0)
    row = iota((rows, 1), 0)
    low = half_mask(0)
    place = iota((8, PAIR), 1) % HD
    first_term = jnp.where(iota((8, PAIR), 0) == 0, 0, 3)
    picks = jnp.where((place >= first_term) & (place < first_term + 3), 1.0, 0.0).astype(BF16)
    every_product = []
    for pair in range(heads // 2):
        lanes = slice(pair * PAIR, (pair + 1) * PAIR)
        all_q, all_k, all_v, all_g, all_s = [kind(index, lanes) for index in range(5)]
        query, grad = two(all_q, SCALE), two(all_g)
        known = dot_nt(picks, two(all_s))
        scores, inner = dot_nt(all_k, query), dot_nt(all_v, grad)
        own = dot_nt(k_ref[:, lanes], query), dot_nt(v_ref[:, lanes], grad)
        every_product.append((lanes, query, grad, all_k, known, scores, inner, own))
    states = []
    for lanes, query, grad, all_k, known, scores, inner, own in every_product:
        known_sum, known_dot = known[0:1], known[1:2]
        top = jnp.max(scores, axis=0, keepdims=True)
        weights = jnp.exp(scores - top)
        total = jnp.sum(weights, axis=0, keepdims=True)
        product = jnp.sum(weights * inner, axis=0, keepdims=True) / total
        log_sum = top + jnp.log(total)
        most = jnp.maximum(known_sum, log_sum)
        joint = most + jnp.log(jnp.exp(known_sum - most) + jnp.exp(log_sum - most))
        share = jnp.exp(known_sum - joint)
        dot = known_dot * share + product * jnp.exp(log_sum - joint)
        change = known_dot - dot
        states.append((lanes, query, grad, all_k, scores, inner, own, joint, share, dot, change))
    for pair, state in enumerate(states):
        lanes, query, grad, _, _, _, own, joint, _, dot, _ = state
        offset = jnp.where(second, off_ref[2 * pair + 1], off_ref[2 * pair])
        middle = row % MIDDLE == offset % MIDDLE
        upper = row % UPPER == offset
        weight = same_group + jnp.where(middle, same_segment, 0.0) + jnp.where(upper, 1.0, 0.0)
        scores = jnp.where(weight > 0.0, own[0], LOW)
        probs = jnp.exp(scores - joint) * weight
        inner = own[1] - dot
        dk_ref[:, lanes] = (
            dk_in[:, lanes] + dot_nn((probs * inner).astype(BF16), query)
        ).astype(BF16)
        dv_ref[:, lanes] = (dv_in[:, lanes] + dot_nn(probs.astype(BF16), grad)).astype(BF16)
    for lanes, _, _, all_k, scores, inner, _, joint, share, dot, change in states:
        probs = jnp.exp(scores - joint)
        grad_q = SCALE * lax.dot_general(
            (probs * (inner - dot)).astype(BF16),
            all_k,
            (((0,), (0,)), ((), ())),
            preferred_element_type=F32,
        )
        lines = []
        for index in range(spec_rows):
            other = every + index
            ratio = jnp.where(low, share[:, index : index + 1], share[:, other : other + 1])
            moved = jnp.where(low, change[:, index : index + 1], change[:, other : other + 1])
            top_q = jnp.where(low, grad_q[index : index + 1], grad_q[other : other + 1])
            near_q = spec_ref[index : index + 1, lanes]
            key_sum = spec_ref[spec_rows + index : spec_rows + index + 1, lanes]
            line = ratio * (near_q + moved * key_sum) + top_q
            lines.append(jnp.broadcast_to(line, (UPPER, PAIR)))
        special = row % UPPER == offsets[:, lanes]
        dq_ref[:, lanes] = (
            dq_in[:, lanes] + jnp.where(special, jnp.concatenate(lines, axis=0), 0.0)
        ).astype(BF16)


def call(kernel, outs, *arrays, us=1.0, raw=False, scratch=(), vmem_mib=40):
    smem = pl.BlockSpec(memory_space=pltpu.SMEM)
    vmem = pl.BlockSpec(memory_space=pltpu.VMEM)
    space = pl.BlockSpec(memory_space=pltpu.HBM) if raw else vmem
    specs = [smem if a.dtype == jnp.int32 and not raw else space for a in arrays]
    return pl.pallas_call(
        kernel,
        out_shape=tuple(jax.ShapeDtypeStruct(shape, dtype) for shape, dtype in outs),
        in_specs=specs,
        out_specs=tuple(vmem for _ in outs),
        scratch_shapes=scratch,
        cost_estimate=pl.CostEstimate(
            flops=int(us * 1.15e9), bytes_accessed=0, transcendentals=0
        ),
        compiler_params=pltpu.CompilerParams(vmem_limit_bytes=vmem_mib * 1024 * 1024),
    )(*arrays)


def across(value, axis, mask):
    size = lax.axis_size(axis)
    return lax.ppermute(value, axis, [(source, source ^ mask) for source in range(size)])


def local(queries, key_matrix, value_matrix, grad_out, offsets):
    rows, width = queries.shape
    slots, outer = lax.axis_size("ctxb"), lax.axis_size("ctxa")
    near_count = slots - GROUP
    near_rows, spec_rows = rows // MIDDLE, rows // UPPER

    next_k, next_v = across(key_matrix, "ctxb", 2), across(value_matrix, "ctxb", 2)
    core_k, core_v = across(key_matrix, "ctxb", 1), across(value_matrix, "ctxb", 1)
    chosen = [((2 * near_rows, width), BF16), ((2 * SPEC_PAD, width), BF16)]
    near_kv, spec_kv = call(
        pack_kernel, chosen, offsets, key_matrix, value_matrix, us=1.3, raw=True, vmem_mib=60,
        scratch=[
            pltpu.SMEM(offsets.shape, jnp.int32),
            pltpu.VMEM((2, rows, width), BF16),
            pltpu.SemaphoreType.DMA((2,)),
            pltpu.SemaphoreType.DMA,
        ],
    )
    near_qg, spec_qg = call(choose_kernel, chosen, offsets, queries, grad_out, us=1.0)
    near_came = [across(near_kv, "ctxb", mask) for mask in reversed(range(GROUP, slots, 2))]
    both = [((2 * rows, width), BF16)]
    own_kv = [key_matrix, value_matrix, core_k, core_v]
    term_rows = -(-3 * (width // HD) // 8) * 8
    (known,) = call(
        first_kernel, [((term_rows, rows), F32)],
        offsets, queries, grad_out, *own_kv, us=2.2,
    )
    (stacked,) = call(
        stack_kernel,
        [((2 * rows + 2 * near_rows * len(near_came), width), BF16)],
        known, spec_qg, next_k, next_v, *near_came, us=0.2,
    )
    kv_parts = own_kv + [stacked, across(stacked, "ctxb", 1)]
    (qg,) = call(merge_kernel, both, queries, grad_out, stacked, us=0.3)
    next_qg = across(qg, "ctxb", 2)
    core_qg = across(qg, "ctxb", 1)
    pay, far = call(
        partial(forward_kernel, near_count),
        [
            ((STAT_ROWS, rows + width), F32),
            ((2 * near_rows + 2 * STAT_ROWS, width), BF16),
        ],
        offsets, queries, grad_out, known, spec_kv, spec_qg, near_qg, *kv_parts[4:], us=2.5,
    )
    dq, dq_spec = call(
        partial(query_kernel, near_count),
        [((rows, width), F32), ((2 * spec_rows, width), F32)],
        offsets, qg, spec_qg, pay, *kv_parts, us=5.0,
    )
    pays_far = [pay, across(pay, "ctxb", 2)]
    far_came = [across(far, "ctxb", mask) for mask in reversed(range(GROUP, slots, 2))]
    grads = [((rows, width), F32)] * 2
    own_dk, own_dv = call(
        partial(key_kernel, 0), grads, offsets, key_matrix, value_matrix, qg, pay, us=1.3,
    )
    held = call(
        relay_kernel,
        [
            ((2 * STAT_ROWS, rows + width), F32),
            ((far.shape[0] * len(far_came), width), BF16),
        ],
        dq_spec, own_dk, *pays_far, *far_came, us=0.3,
    )
    pays, fars = [(part, across(part, "ctxb", 1)) for part in held]
    (block,) = call(
        partial(collect_kernel, rows), [((5 * slots * spec_rows, width), BF16)], *pays, *fars,
        us=0.3,
    )
    (next_qg,) = call(copy_kernel, [((2 * rows, width), BF16)], block, next_qg, us=0.2)
    qg_parts = [qg, core_qg, next_qg, across(next_qg, "ctxb", 1)]
    blocks = [block] + [across(block, "ctxa", mask) for mask in reversed(range(1, outer))]
    dk, dv = call(
        partial(key_kernel, near_count),
        grads,
        offsets, key_matrix, value_matrix, *qg_parts[1:], *pays, *fars, own_dk, own_dv, us=4.0,
    )
    return call(
        partial(special_kernel, slots),
        [((rows, width), BF16)] * 3,
        offsets, key_matrix, value_matrix, dq, dq_spec, dk, dv, *blocks, us=3.0,
    )


def solution(mesh):
    split = P(("ctxa", "ctxb"), None)
    return jax.shard_map(
        local,
        mesh=mesh,
        in_specs=(split, split, split, split, P()),
        out_specs=(split, split, split),
        check_vma=False,
    )
```
